32 devices in a mesh: dp: 16 (over z, x, core), tensor: 2 (over y).
Axes of the slice: x: 2, y: 2, z: 4, core: 2. Of those that a mesh axis runs over, the one named last changes fastest.
Arguments:
- content_in: bfloat16 [32, 512, 768], P('dp'), may hold values from -6 to 6
- query_in: bfloat16 [32, 512, 768], P('dp'), may hold values from -6 to 6
- lengths: int32 [32], P('dp'), may hold values from 1 to 512, 9830 in all
- factor_order: int32 [32, 512], P('dp'), may hold values from 0 to 511, each once within a row
- buckets: int32 [32, 512, 512], P('dp'), may hold values from 0 to 31
- w_qkv: bfloat16 [3, 768, 768], P(None, 'dp', 'tensor'), may hold values from -0.21875 to 0.21875
- b_qv: bfloat16 [2, 768], P(None, 'tensor'), may hold values from -3 to 3
- w_out: bfloat16 [768, 768], P('tensor', 'dp'), may hold values from -1.75 to 1.75
- w_in: bfloat16 [768, 3072], P('dp', 'tensor'), may hold values from -0.21875 to 0.21875
- b_in: bfloat16 [3072], P('tensor'), may hold values from -3 to 3
- w_down: bfloat16 [3072, 768], P('tensor', 'dp'), may hold values from -0.109375 to 0.109375
- b_outs: bfloat16 [2, 768], replicated, may hold values from -2 to 2
- norm_gain: bfloat16 [2, 768], replicated, may hold values from 0.5 to 1.5
- norm_bias: bfloat16 [2, 768], replicated, may hold values from -2 to 2
- rel_table: bfloat16 [32, 12], P(None, 'tensor'), may hold values from -4 to 4
- cot_content: bfloat16 [32, 512, 768], P('dp'), may hold values from -6 to 6
- cot_query: bfloat16 [32, 512, 768], P('dp'), may hold values from -6 to 6
Outputs:
- out_content: bfloat16 [32, 512, 768], P('dp')
- out_query: bfloat16 [32, 512, 768], P('dp')
- grad_content: bfloat16 [32, 512, 768], P('dp', None, 'tensor')
- grad_query: bfloat16 [32, 512, 768], P('dp', None, 'tensor')
- grad_w_qkv: float32 [3, 768, 768], P(None, 'dp', 'tensor')
- grad_b_qv: float32 [2, 768], P(None, 'tensor')
- grad_w_out: float32 [768, 768], P('tensor', 'dp')
- grad_w_in: float32 [768, 3072], P('dp', 'tensor')
- grad_b_in: float32 [3072], P('tensor')
- grad_w_down: float32 [3072, 768], P('tensor', 'dp')
- grad_b_outs: float32 [2, 768], replicated
- grad_norm_gain: float32 [2, 768], replicated
- grad_norm_bias: float32 [2, 768], replicated
- grad_rel_table: float32 [32, 12], P(None, 'tensor')
The draws below stay inside these ranges and needn't reach their ends.
Inputs may be any that keep to these rules, and one draw needn't show every extreme that they name: `lengths`: positions at or past a sequence's length are padding; some sequence uses all 512 slots. `factor_order`: each row is a permutation of the positions 0 to 511.
All inputs are finite; a program needn't handle non-finite values. No bound on the sum of `lengths` on one device may be relied on, other than what follows from the above.
Results may differ from the reference program's by a relative error of at most 0.019.
Values may be sent and summed in bfloat16 or wider, within the bound.
No kernel may reach another device: no remote copies, remote signals or barrier semaphores. Data moves between devices by JAX's collectives and lax.ppermute only.
A program may use at most 256 MiB of HBM per device.

```python
import math
import jax
import jax.numpy as jnp
import numpy as np
from jax import lax

D = 768
H = 12
HD = 64
FF = 3072
NB = 32
L = 512
MB = 2
ROWS = 1
SEQS = 32


def place_ends(entries, own_key, smallest, high):
    index_at = [jax.random.randint(jax.random.fold_in(own_key, axis), (), 0, length) for axis, length in enumerate(entries.shape)]
    widest = entries.shape.index(max(entries.shape))
    neighbour = index_at[:widest] + [(index_at[widest] + 1) % entries.shape[widest]] + index_at[widest + 1:]
    return entries.at[tuple(index_at)].set(smallest).at[tuple(neighbour)].set(high)


def strengthened(values, stream_key, source, target, parts, factor):
    owner, partner = [(jnp.arange(values.shape[axis_at]) // (values.shape[axis_at] // parts)).reshape([-1 if axis == axis_at else 1 for axis in range(values.ndim)]) for axis_at in (source, target)]
    chosen = jax.random.permutation(stream_key, parts)[partner]
    strong = (owner == chosen) | (owner == (partner + parts // 2) % parts)
    return jnp.where(strong, factor * values, values)


def block_scale(own_key, shape, cuts, least, high):
    def one(position, blocks):
        draws = jax.random.uniform(jax.random.fold_in(jax.random.fold_in(own_key, 6), position), (blocks,), jnp.float32, least / len(cuts), high / len(cuts))
        return jnp.repeat(jnp.exp(draws), shape[position] // blocks).reshape((-1,) + (1,) * (len(shape) - position - 1))

    level = one(*cuts[0])
    for cut in cuts[1:]:
        level = level * one(*cut)
    return level


def split_up(count, total, bound, lean):
    loads = [(1 << 20) // math.isqrt(rank ** lean) + 1 for rank in range(2, count + 1)]
    rest, holding = total - bound - (count - 1), [1] * (count - 1)
    while rest > 0:
        free = [i for i in range(count - 1) if holding[i] < bound]
        whole, left = sum([loads[i] for i in free]), rest
        for i in free:
            more = min(bound - holding[i], max(1, left * loads[i] // whole), rest)
            holding[i] = holding[i] + more
            rest = rest - more
    return np.array([bound] + holding)


def uneven_parts(own_key, count, total, reach, skew):
    if count == 2:
        one = jax.random.randint(own_key, (), max(1, total - reach), min(reach, total - 1) + 1)
        return jnp.stack([one, total - one])
    tallies = jnp.asarray(split_up(count, total, reach, skew), jnp.int32)
    couples = (count - 1) // 2
    source_of, taker = tallies[1:1 + 2 * couples:2], tallies[2:2 + 2 * couples:2]
    slack = jnp.minimum(source_of - 1, reach - taker)
    shifted = jax.random.randint(jax.random.fold_in(own_key, 1), (couples,), 0, 1 << 20) % (slack + 1)
    tallies = tallies.at[1:1 + 2 * couples:2].set(source_of - shifted).at[2:2 + 2 * couples:2].set(taker + shifted)
    return tallies[jax.random.permutation(jax.random.fold_in(own_key, 2), count)]


def scatter_about(rng, shape, deviation, bound, cuts=(), held_as=jnp.bfloat16):
    loudness = block_scale(rng, shape, cuts, -0.22, 0.18) if cuts else 1.0
    values = jax.random.normal(rng, shape, jnp.float32) * deviation * loudness
    return jnp.minimum(jnp.maximum(values, -bound), bound).astype(held_as)


def bell_draw_with(stream_key, dims, deviation, bound, cuts, heavy, kind=jnp.bfloat16):
    drawn = deviation * jax.random.normal(stream_key, dims, jnp.float32)
    if cuts:
        drawn = drawn * block_scale(stream_key, dims, cuts, -0.22, 0.18)
    return jnp.clip(strengthened(drawn, jax.random.fold_in(stream_key, 3), *heavy), -bound, bound).astype(kind)


def setup_inputs(seed: int = 0) -> dict:
    key_of = jax.random.split(jax.random.key(seed), 18)
    content_in = bell_draw_with(key_of[0], (SEQS, L, D), 1.0, 6.0, ((0, 16),), (0, 2, 16, 2.0))
    query_in = scatter_about(key_of[1], (SEQS, L, D), 1.0, 6.0, ((0, 16),))
    lengths = uneven_parts(key_of[2], SEQS, SEQS * L * 3 // 5, L, 0).astype(jnp.int32)
    factor_order = jax.vmap(lambda own: jax.random.permutation(own, L))(jax.random.split(key_of[3], SEQS)).reshape((SEQS, L)).astype(jnp.int32)
    buckets = place_ends(jax.random.randint(key_of[4], (SEQS, L, L), 0, NB), jax.random.fold_in(key_of[4], 1), 0, NB - 1).astype(jnp.int32)
    w_qkv = scatter_about(key_of[5], (3, D, D), D ** -0.5, 0.21875, ((1, 16), (2, 2)))
    b_qv = scatter_about(key_of[6], (2, D), 0.5, 3.0, ((1, 2),))
    w_out = scatter_about(key_of[7], (D, D), (D // 64) ** -0.5, 1.75, ((0, 2), (1, 16)))
    w_in = scatter_about(key_of[8], (D, FF), D ** -0.5, 0.21875, ((0, 16), (1, 2)))
    b_in = scatter_about(key_of[9], (FF,), 0.5, 3.0, ((0, 2),))
    w_down = scatter_about(key_of[10], (FF, D), FF ** -0.5, 0.109375, ((0, 2), (1, 16)))
    b_outs = scatter_about(key_of[11], (2, D), 0.3, 2.0)
    norm_gain = jnp.clip(1.0 + 0.1 * jax.random.normal(key_of[12], (2, D), jnp.float32), 0.5, 1.5).astype(jnp.bfloat16)
    norm_bias = scatter_about(key_of[13], (2, D), 0.3, 2.0)
    rel_table = scatter_about(key_of[14], (NB, H), 1.0, 4.0, ((1, 2),))
    cot_content = bell_draw_with(key_of[15], (SEQS, L, D), 1.0, 6.0, ((0, 16),), (0, 2, 16, 2.0))
    cot_query = bell_draw_with(key_of[16], (SEQS, L, D), 1.0, 6.0, ((0, 16),), (0, 2, 16, 2.0))
    return {"content_in": content_in, "query_in": query_in, "lengths": lengths, "factor_order": factor_order, "buckets": buckets, "w_qkv": w_qkv, "b_qv": b_qv, "w_out": w_out, "w_in": w_in, "b_in": b_in, "w_down": w_down, "b_outs": b_outs, "norm_gain": norm_gain, "norm_bias": norm_bias, "rel_table": rel_table, "cot_content": cot_content, "cot_query": cot_query}


@jax.custom_vjp
def low(v):
    return lax.optimization_barrier(v.astype(jnp.bfloat16)).astype(jnp.float32)

@jax.custom_vjp
def low_back(v):
    return v

def low_keep(v):
    return (low(v), None)

def low_pass(kept, grad):
    return (grad,)

def back_keep(v):
    return (v, None)

def back_low(kept, grad):
    return (low(grad),)
low.defvjp(low_keep, low_pass)
low_back.defvjp(back_keep, back_low)
EPSILON = 1e-05
PRECISE = lax.Precision.HIGHEST

def layer_norm(residual, gain_row, shift_row):
    average = lax.optimization_barrier(jnp.mean(residual, axis=-1, keepdims=True))
    centred = residual - average
    variance = lax.optimization_barrier(jnp.mean(centred * centred, axis=-1, keepdims=True))
    return centred * lax.rsqrt(variance + EPSILON) * gain_row + shift_row

def gelu_exact(values):
    return 0.5 * values * (1.0 + lax.erf(values * 0.7071067811865476))

def forward(content_in, query_in, w_qkv, b_qv, w_out, w_in, b_in, w_down, b_outs, norm_gain, norm_bias, rel_table, lengths, factor_order, buckets):
    seq_count = content_in.shape[0]
    seq_len = content_in.shape[1]
    positions = jnp.arange(seq_len, dtype=jnp.int32)
    key_valid = positions[None, None, :] < lengths[:, None, None]
    rank_query = factor_order[:, :, None]
    rank_key = factor_order[:, None, :]
    itself = (positions[:, None] == positions[None, :])[None]
    content_mask = key_valid & (rank_key <= rank_query) | itself
    query_mask = key_valid & (rank_key < rank_query) | (positions[None, None, :] == 0)
    pair_bias = jnp.transpose(rel_table[buckets], (0, 3, 1, 2))
    head_shape = (seq_count, seq_len, H, HD)

    def project(inputs, matrix):
        return jnp.einsum('gld,de->gle', inputs, matrix, precision=PRECISE)
    key_heads = low(low_back(project(content_in, w_qkv[1]))).reshape(head_shape)
    value_heads = low(low_back(project(content_in, w_qkv[2])) + b_qv[1]).reshape(head_shape)

    def one_stream(inputs, visible):
        query_heads = low(low_back(project(inputs, w_qkv[0])) + b_qv[0]).reshape(head_shape)
        raw_scores = low_back(jnp.einsum('gihd,gjhd->ghij', query_heads, key_heads, precision=PRECISE) * 0.125)
        scores = jnp.where(visible[:, None], raw_scores + pair_bias, -1e+30)
        row_max = lax.optimization_barrier(jnp.max(scores, axis=-1, keepdims=True))
        exp_scores = jnp.exp(scores - row_max)
        attn_low = low(exp_scores / lax.optimization_barrier(jnp.sum(exp_scores, axis=-1, keepdims=True)))
        context = jnp.einsum('ghij,gjhd->gihd', attn_low, value_heads, precision=PRECISE)
        context = low_back(low(context)).reshape(seq_count, seq_len, D)
        residual_one = inputs + low_back(project(context, w_out)) + b_outs[0]
        normed = layer_norm(residual_one, norm_gain[0], norm_bias[0])
        hidden = low_back(project(low(normed), w_in)) + b_in
        active = low(gelu_exact(hidden))
        residual_two = normed + low_back(project(active, w_down)) + b_outs[1]
        return layer_norm(residual_two, norm_gain[1], norm_bias[1])
    return (one_stream(content_in, content_mask), one_stream(query_in, query_mask))

def reference(content_in, query_in, lengths, factor_order, buckets, w_qkv, b_qv, w_out, w_in, b_in, w_down, b_outs, norm_gain, norm_bias, rel_table, cot_content, cot_query):
    per_group = MB * ROWS
    group_count = content_in.shape[0] // per_group
    params = tuple((p.astype(jnp.float32) for p in (w_qkv, b_qv, w_out, w_in, b_in, w_down, b_outs, norm_gain, norm_bias, rel_table)))

    def by_group(array):
        return array.reshape((group_count, per_group) + array.shape[1:])
    grouped = tuple((by_group(a) for a in (content_in, query_in, lengths, factor_order, buckets, cot_content, cot_query)))

    def one_group(running, member):
        content_rows, query_rows, length_rows, order_rows, bucket_rows, cot_rows, cot_query_rows = member

        def apply_layer(content_float, query_float, weights):
            return forward(content_float, query_float, *weights, length_rows, order_rows, bucket_rows)
        results, pullback = jax.vjp(apply_layer, content_rows.astype(jnp.float32), query_rows.astype(jnp.float32), params)
        content_grad, query_grad, weight_grads = pullback((cot_rows.astype(jnp.float32), cot_query_rows.astype(jnp.float32)))
        running = tuple((a + b for a, b in zip(running, weight_grads)))
        return (running, (results[0].astype(jnp.bfloat16), results[1].astype(jnp.bfloat16), content_grad.astype(jnp.bfloat16), query_grad.astype(jnp.bfloat16)))
    start_sums = tuple((jnp.zeros_like(p) for p in params))
    grads, pieces = lax.scan(one_group, start_sums, grouped)
    whole = tuple((p.reshape((group_count * per_group,) + p.shape[2:]) for p in pieces))
    return (whole[0], whole[1], whole[2], whole[3], grads[0], grads[1], grads[2], grads[3], grads[4], grads[5], grads[6], grads[7], grads[8], grads[9])
```

```python
import functools

import jax
import jax.numpy as jnp
from jax import lax
from jax.experimental import pallas as pl
from jax.experimental.pallas import tpu as pltpu
from jax.sharding import Mesh, PartitionSpec as P

EPSILON = 1e-05

NEG = -1e30
BF = jnp.bfloat16
F32 = jnp.float32


def dot(a, b, dims):
    return lax.dot_general(a, b, (dims, ((), ())), preferred_element_type=F32)


NN = ((1,), (0,))
NT = ((1,), (1,))
TN = ((0,), (0,))


def bias_kernel(len_ref, buckets_ref, rank_row_ref, rank_col_ref, table_ref, out_ref):
    rows, cols = buckets_ref.shape
    heads = table_ref.shape[0]
    start = pl.program_id(0) * rows
    key = start + lax.broadcasted_iota(jnp.int32, (rows, cols), 0)
    query = lax.broadcasted_iota(jnp.int32, (rows, cols), 1)
    valid = key < len_ref[0]
    rank_key = rank_col_ref[...]
    rank_query = rank_row_ref[...]
    content = (valid & (rank_key <= rank_query)) | (key == query)
    stream = (valid & (rank_key < rank_query)) | (key == 0)
    index = buckets_ref[...]
    for head in range(heads):
        row = jnp.broadcast_to(table_ref[head : head + 1, :], (rows, 128))
        bias = jnp.concatenate(
            [
                jnp.take_along_axis(
                    row, index[:, c : c + 128], axis=1, mode="promise_in_bounds"
                )
                for c in range(0, cols, 128)
            ],
            axis=1,
        )
        out_ref[head, :, :cols] = jnp.where(content, bias, NEG).astype(BF)
        out_ref[head, :, cols:] = jnp.where(stream, bias, NEG).astype(BF)


def masked_bias(length, buckets_t, rank, table):
    seq = buckets_t.shape[0]
    heads = table.shape[0]
    step = 128
    return pl.pallas_call(
        bias_kernel,
        grid=(seq // step,),
        in_specs=[
            pl.BlockSpec(memory_space=pltpu.SMEM),
            pl.BlockSpec((step, seq), lambda g: (g, 0)),
            pl.BlockSpec((1, seq), lambda g: (0, 0)),
            pl.BlockSpec((step, 1), lambda g: (g, 0)),
            pl.BlockSpec((heads, 128), lambda g: (0, 0)),
        ],
        out_specs=pl.BlockSpec((heads, step, 2 * seq), lambda g: (0, g, 0)),
        out_shape=jax.ShapeDtypeStruct((heads, seq, 2 * seq), BF),
    )(length, buckets_t, rank.reshape(1, seq), rank.reshape(seq, 1), table)


def forward_kernel(q_ref, k_ref, v_ref, bias_ref, probs_ref, ctx_ref, inv_ref, *, tile):
    keys = (k_ref[...].astype(F32) * 0.125).astype(BF)
    values = v_ref[...]
    for t in range(q_ref.shape[1] // tile):
        at = pl.ds(t * tile, tile)
        scores = dot(keys, q_ref[:, at], TN) + bias_ref[0, :, at].astype(F32)
        high = jnp.max(scores, axis=0, keepdims=True)
        weight = jnp.exp(scores - high)
        inverse = 1.0 / jnp.sum(weight, axis=0, keepdims=True)
        low = weight.astype(BF)
        probs_ref[0, :, at] = low
        ctx_ref[:, at] = (dot(values, low, NN) * inverse).astype(BF)
        inv_ref[0, :, at] = inverse


def attention(q_t, k_t, v_t, bias, heads, tile=256):
    width, both = q_t.shape
    seq = k_t.shape[1]
    size = width // heads
    return pl.pallas_call(
        functools.partial(forward_kernel, tile=tile),
        grid=(heads,),
        in_specs=[
            pl.BlockSpec((size, both), lambda h: (h, 0)),
            pl.BlockSpec((size, seq), lambda h: (h, 0)),
            pl.BlockSpec((size, seq), lambda h: (h, 0)),
            pl.BlockSpec((1, seq, both), lambda h: (h, 0, 0)),
        ],
        out_specs=[
            pl.BlockSpec((1, seq, both), lambda h: (h, 0, 0)),
            pl.BlockSpec((size, both), lambda h: (h, 0)),
            pl.BlockSpec((1, 1, both), lambda h: (h, 0, 0)),
        ],
        out_shape=[
            jax.ShapeDtypeStruct((heads, seq, both), BF),
            jax.ShapeDtypeStruct((width, both), BF),
            jax.ShapeDtypeStruct((heads, 1, both), F32),
        ],
    )(q_t, k_t, v_t, bias)


def backward_kernel(
    q_ref, k_ref, v_ref, p_ref, inv_ref, ctx_ref, dctx_ref, buckets_ref,
    dq_ref, dk_ref, dv_ref, table_ref, held, total, *, tile, buckets,
):
    head = pl.program_id(0)
    heads = pl.num_programs(0)
    seq = k_ref.shape[1]
    group = 16
    queries = q_ref[...]
    keys = k_ref[...]
    values = v_ref[...]
    grad = dctx_ref[...].astype(F32) * inv_ref[0]
    inner = jnp.sum(grad * ctx_ref[...].astype(F32), axis=0, keepdims=True)
    grad = grad.astype(BF)
    dk = jnp.zeros(keys.shape, F32)
    dv = jnp.zeros(keys.shape, F32)
    for t in range(seq // tile):
        both = None
        for stream in range(2):
            lo = stream * seq + t * tile
            at = slice(lo, lo + tile)
            weight = p_ref[0, :, at]
            part = dot(values, grad[:, at], TN) - inner[:, at]
            ds = weight.astype(F32) * part
            low = ds.astype(BF)
            dv += dot(grad[:, at], weight, NT)
            dk += dot(queries[:, at], low, NT)
            dq_ref[:, at] = (dot(keys, low, NN) * 0.125).astype(BF)
            both = ds if both is None else both + ds
        both = both.astype(BF).reshape(seq // group, group, tile)
        held[:, pl.ds(pl.multiple_of(head * group, group), group), t * tile : (t + 1) * tile] = both
    dk_ref[...] = (dk * 0.125).astype(BF)
    dv_ref[...] = dv.astype(BF)

    @pl.when(head == heads - 1)
    def _():
        total[...] = jnp.zeros_like(total)

        @pl.loop(0, seq // group)
        def _(g):
            index = buckets_ref[pl.ds(pl.multiple_of(g * group, group), group), :]
            hot = jnp.concatenate(
                [jnp.where(index == n, 1.0, 0.0).astype(BF) for n in range(buckets)], axis=0
            )
            total[...] += dot(hot, held[g], NT)

        whole = total[...]
        row = lax.broadcasted_iota(jnp.int32, whole.shape, 0) % group
        col = lax.broadcasted_iota(jnp.int32, whole.shape, 1) % group
        kept = jnp.where(row == col, whole, 0.0)
        table_ref[...] = jnp.sum(kept.reshape(buckets, group, whole.shape[1]), axis=1)


def attention_back(q_t, k_t, v_t, probs, inverse, ctx_t, dctx_t, buckets_t, heads, buckets, tile=256):
    width, both = q_t.shape
    seq = k_t.shape[1]
    size = width // heads
    wide = pl.BlockSpec((size, both), lambda h: (h, 0))
    thin = pl.BlockSpec((size, seq), lambda h: (h, 0))
    return pl.pallas_call(
        functools.partial(backward_kernel, tile=tile, buckets=buckets),
        grid=(heads,),
        in_specs=[
            wide,
            thin,
            thin,
            pl.BlockSpec((1, seq, both), lambda h: (h, 0, 0)),
            pl.BlockSpec((1, 1, both), lambda h: (h, 0, 0)),
            wide,
            wide,
            pl.BlockSpec((seq, seq), lambda h: (0, 0)),
        ],
        out_specs=[wide, thin, thin, pl.BlockSpec((buckets, heads * 16), lambda h: (0, 0))],
        out_shape=[
            jax.ShapeDtypeStruct((width, both), BF),
            jax.ShapeDtypeStruct((width, seq), BF),
            jax.ShapeDtypeStruct((width, seq), BF),
            jax.ShapeDtypeStruct((buckets, heads * 16), F32),
        ],
        scratch_shapes=[
            pltpu.VMEM((seq // 16, heads * 16, seq), BF),
            pltpu.VMEM((buckets * 16, heads * 16), F32),
        ],
        compiler_params=pltpu.CompilerParams(vmem_limit_bytes=56 * 1024 * 1024),
    )(q_t, k_t, v_t, probs, inverse, ctx_t, dctx_t, buckets_t)


def shifted(value, axis, step):
    size = lax.axis_size(axis)
    return lax.ppermute(value, axis, [(i, (i + step) % size) for i in range(size)])


def gather_axis(value, axis, where):
    size = lax.axis_size(axis)
    me = lax.axis_index(axis)
    pieces = [value] + [shifted(value, axis, k) for k in range(1, size)]
    slots = []
    for j in range(size):
        which = lax.rem(me - j + size, size)
        chosen = pieces[0]
        for k in range(1, size):
            chosen = jnp.where(which == k, pieces[k], chosen)
        slots.append(chosen)
    return jnp.stack(slots, axis=where)


def gather_rows(shard, order):
    names = ["y", "z", "x", "core"]
    value, have = shard, []
    for axis in order:
        where = sum(names.index(a) < names.index(axis) for a in have)
        value = gather_axis(value, axis, where)
        have.append(axis)
    return value


def scatter_axis(value, axis, where, low=True):
    size = lax.axis_size(axis)
    me = lax.axis_index(axis)
    total = lax.dynamic_index_in_dim(value, me, where, keepdims=False).astype(F32)
    for k in range(1, size):
        out = lax.dynamic_index_in_dim(value, lax.rem(me + k, size), where, keepdims=False)
        total = total + shifted(out.astype(BF), axis, k).astype(F32)
    return total.astype(BF) if low else total


def scatter_rows(value, order):
    have = ["y", "z", "x", "core"]
    for axis in order:
        where = have.index(axis)
        have.remove(axis)
        value = scatter_axis(value, axis, where, low=bool(have))
    return value


def sum_all(value):
    for axis in ("core", "x", "y", "z"):
        size = lax.axis_size(axis)
        value = value + sum(shifted(value, axis, k) for k in range(1, size))
    return value


def normalise(value):
    centred = value - jnp.mean(value, axis=-1, keepdims=True)
    inverse = lax.rsqrt(jnp.mean(centred * centred, axis=-1, keepdims=True) + EPSILON)
    return centred * inverse, inverse


def normalise_back(grad, unit, inverse):
    mean = jnp.mean(grad, axis=-1, keepdims=True)
    along = jnp.mean(grad * unit, axis=-1, keepdims=True)
    return (grad - mean - unit * along) * inverse


def ein(spec, a, b):
    return jnp.einsum(spec, a, b, preferred_element_type=F32)


def shards(
    content_in,
    query_in,
    lengths,
    factor_order,
    buckets,
    w_qkv,
    b_qv,
    w_out,
    w_in,
    b_in,
    w_down,
    b_outs,
    norm_gain,
    norm_bias,
    rel_table,
    cot_content,
    cot_query,
):
    me = lax.axis_index("y")
    halves = lax.axis_size("y")
    each = content_in.shape[0] // halves
    assert each == 1
    seq = content_in.shape[1]
    width = content_in.shape[2]
    bucket_count, heads_here = rel_table.shape
    heads = heads_here * halves
    part = w_qkv.shape[2]
    ffn = w_in.shape[1]
    rows = w_in.shape[0]

    def mine(array):
        return lax.dynamic_index_in_dim(array, me, 0, keepdims=False)

    qkv_shard = jnp.transpose(w_qkv, (1, 0, 2)).reshape(rows, 3 * part)
    cut = 5 * part // 3
    first = gather_rows(qkv_shard[:, :cut], ("z", "x", "y", "core"))
    second = gather_rows(qkv_shard[:, cut:], ("z", "y", "x", "core"))
    full_qkv = jnp.concatenate([first, second], axis=-1).reshape(halves, width, 3 * part)
    rest_shard = jnp.concatenate([w_in, w_down.T, w_out.T], axis=1)
    rest = lax.all_gather(rest_shard, ("y", "z", "x", "core"), axis=0).reshape(
        halves, width, 2 * ffn + part
    )
    w_q, w_k, w_v = (full_qkv[:, :, i * part : (i + 1) * part] for i in range(3))
    full_in, full_down, full_out = rest[:, :, :ffn], rest[:, :, ffn : 2 * ffn], rest[:, :, 2 * ffn :]

    vectors = jnp.concatenate([b_qv, b_in.reshape(ffn // part, part)], axis=0)
    vectors = jnp.concatenate(
        [vectors, jnp.pad(rel_table, ((0, 0), (0, part - heads_here)))], axis=0
    )
    vectors = gather_axis(vectors, "y", 0).astype(F32)
    q_bias = vectors[:, 0].reshape(width, 1)
    v_bias = vectors[:, 1].reshape(width, 1)
    hidden_bias = vectors[:, 2 : 2 + ffn // part].reshape(halves, 1, ffn)
    table = vectors[:, 2 + ffn // part :, :heads_here]
    table = jnp.transpose(table, (0, 2, 1)).reshape(heads, bucket_count)
    table = jnp.pad(table, ((0, 0), (0, 128 - bucket_count)))

    gains = norm_gain.astype(F32)
    shifts = norm_bias.astype(F32)
    out_bias = b_outs.astype(F32)

    content = mine(content_in)
    stacked = jnp.concatenate([content, mine(query_in)], axis=0)
    buckets_t = mine(buckets).T
    rank = mine(factor_order)
    length = lax.dynamic_slice_in_dim(lengths, me, 1, 0)
    bias = masked_bias(length, buckets_t, rank, table)

    q_t = (ein("yde,nd->yen", w_q, stacked).reshape(width, 2 * seq) + q_bias).astype(BF)
    k_t = ein("yde,nd->yen", w_k, content).reshape(width, seq).astype(BF)
    v_t = (ein("yde,nd->yen", w_v, content).reshape(width, seq) + v_bias).astype(BF)
    probs, ctx_t, inverse = attention(q_t, k_t, v_t, bias, heads)
    ctx_parts = ctx_t.reshape(halves, part, 2 * seq)

    resid_one = stacked.astype(F32) + ein("yen,yoe->no", ctx_parts, full_out) + out_bias[0]
    unit_one, inv_one = normalise(resid_one)
    normed = unit_one * gains[0] + shifts[0]
    normed_low = normed.astype(BF)
    hidden = ein("nd,ydf->ynf", normed_low, full_in) + hidden_bias
    cdf = 0.5 * (1.0 + lax.erf(hidden * 0.7071067811865476))
    active = (hidden * cdf).astype(BF)
    slope = (cdf + hidden * (jnp.exp(hidden * hidden * -0.5) * 0.3989422804014327)).astype(BF)
    resid_two = normed + ein("ynf,yof->no", active, full_down) + out_bias[1]
    unit_two, inv_two = normalise(resid_two)
    output = (unit_two * gains[1] + shifts[1]).astype(BF)
    outs = lax.all_gather(output, "y", axis=0).reshape(halves, 2, seq, width)

    cot = jnp.concatenate([mine(cot_content), mine(cot_query)], axis=0).astype(F32)
    d_two = normalise_back(cot * gains[1], unit_two, inv_two)
    d_two_low = d_two.astype(BF)
    d_active = ein("no,yof->ynf", d_two_low, full_down)
    d_hidden = d_active * slope.astype(F32)
    d_hidden_low = d_hidden.astype(BF)
    down_grad = ein("no,ynf->yof", d_two_low, active).astype(BF)
    in_grad = ein("nd,ynf->ydf", normed_low, d_hidden_low).astype(BF)
    d_normed = d_two + ein("ynf,ydf->nd", d_hidden_low, full_in)
    d_one = normalise_back(d_normed * gains[0], unit_one, inv_one)
    d_one_low = d_one.astype(BF)
    out_grad = ein("no,yen->yoe", d_one_low, ctx_parts).astype(BF)
    dctx_t = ein("yoe,no->yen", full_out, d_one_low).reshape(width, 2 * seq).astype(BF)

    blocks = (halves, lax.axis_size("z"), lax.axis_size("x"), 2, rows)
    down_share = scatter_rows(down_grad.reshape(blocks + (ffn,)), ("core", "x", "y", "z"))
    in_out = jnp.concatenate([in_grad, out_grad], axis=-1)
    in_out_share = scatter_rows(in_out.reshape(blocks + (ffn + part,)), ("core", "y", "x", "z"))

    early = jnp.concatenate(
        [
            jnp.sum(d_hidden, axis=1).reshape(-1),
            jnp.sum(d_one, axis=0),
            jnp.sum(d_two, axis=0),
            jnp.sum(d_normed * unit_one, axis=0),
            jnp.sum(cot * unit_two, axis=0),
            jnp.sum(d_normed, axis=0),
            jnp.sum(cot, axis=0),
        ]
    )
    early = sum_all(early.reshape(-1, 128)).reshape(-1)

    dq_t, dk_t, dv_t, table_grad = attention_back(
        q_t, k_t, v_t, probs, inverse, ctx_t, dctx_t, buckets_t, heads, bucket_count
    )
    dq_parts = dq_t.reshape(halves, part, 2 * seq)
    dk_parts = dk_t.reshape(halves, part, seq)
    dv_parts = dv_t.reshape(halves, part, seq)
    qkv_grad = jnp.concatenate(
        [
            ein("nd,yen->yde", stacked, dq_parts),
            ein("nd,yen->yde", content, dk_parts),
            ein("nd,yen->yde", content, dv_parts),
        ],
        axis=-1,
    ).astype(BF)
    qkv_grad = qkv_grad.reshape(blocks + (3 * part,))
    first_share = scatter_rows(qkv_grad[..., :cut], ("core", "x", "y", "z"))
    second_share = scatter_rows(qkv_grad[..., cut:], ("core", "y", "x", "z"))
    qkv_share = jnp.concatenate([first_share, second_share], axis=-1)

    grad_in = ein("yen,yde->nd", dq_parts, w_q)
    extra = ein("yen,yde->nd", dk_parts, w_k) + ein("yen,yde->nd", dv_parts, w_v)
    grad_in = d_one + grad_in
    grad_in = jnp.concatenate([grad_in[:seq] + extra, grad_in[seq:]], axis=0).astype(BF)
    grad_ins = lax.all_to_all(
        grad_in.reshape(1, 2, seq, width), "y", split_axis=3, concat_axis=0, tiled=True
    )

    table_grad = jnp.sum(table_grad.reshape(bucket_count, heads, 16), axis=2).T
    late = jnp.concatenate(
        [
            jnp.sum(dq_t.astype(F32), axis=1),
            jnp.sum(dv_t.astype(F32), axis=1),
            table_grad.reshape(-1),
        ]
    )
    late = sum_all(late.reshape(-1, 128)).reshape(-1)

    grad_b_qv = mine(jnp.transpose(late[: 2 * width].reshape(2, halves, part), (1, 0, 2)))
    grad_table = mine(late[2 * width :].reshape(halves, heads_here, bucket_count)).T
    grad_b_in = mine(early[: halves * ffn].reshape(halves, ffn))
    pairs = early[halves * ffn :].reshape(3, 2, width)
    return (
        outs[:, 0],
        outs[:, 1],
        grad_ins[:, 0],
        grad_ins[:, 1],
        jnp.transpose(qkv_share.reshape(rows, 3, part), (1, 0, 2)),
        grad_b_qv,
        in_out_share[:, ffn:].T,
        in_out_share[:, :ffn],
        grad_b_in,
        down_share.T,
        pairs[0],
        pairs[1],
        pairs[2],
        grad_table,
    )


def solution(mesh):
    count = mesh.shape["dp"] // 2
    depth = 4 if count % 4 == 0 else 1
    while count // depth > depth:
        depth *= 2
    grid = mesh.devices.reshape(depth, count // depth, 2, mesh.shape["tensor"])
    fine = Mesh(grid, ("z", "x", "core", "y"))
    dp = ("z", "x", "core")
    return jax.shard_map(
        shards,
        mesh=fine,
        in_specs=(
            P(dp, None, None),
            P(dp, None, None),
            P(dp),
            P(dp, None),
            P(dp, None, None),
            P(None, dp, "y"),
            P(None, "y"),
            P("y", dp),
            P(dp, "y"),
            P("y"),
            P("y", dp),
            P(),
            P(),
            P(),
            P(None, "y"),
            P(dp, None, None),
            P(dp, None, None),
        ),
        out_specs=(
            P(dp, None, None),
            P(dp, None, None),
            P(dp, None, "y"),
            P(dp, None, "y"),
            P(None, dp, "y"),
            P(None, "y"),
            P("y", dp),
            P(dp, "y"),
            P("y"),
            P("y", dp),
            P(),
            P(),
            P(),
            P(None, "y"),
        ),
        check_vma=False,
    )
```

```python
import functools

import jax
import jax.numpy as jnp
from jax import lax
from jax.experimental import pallas as pl
from jax.experimental.pallas import tpu as pltpu
from jax.sharding import Mesh, PartitionSpec as P

EPSILON = 1e-05


def cost(us):
    return pl.CostEstimate(flops=int(us * 1e7), bytes_accessed=int(us * 1e4), transcendentals=0)

NEG = -1e30
BF = jnp.bfloat16
F32 = jnp.float32


def dot(a, b, dims):
    return lax.dot_general(a, b, (dims, ((), ())), preferred_element_type=F32)


NN = ((1,), (0,))
NT = ((1,), (1,))
TN = ((0,), (0,))


def bias_kernel(len_ref, buckets_ref, rank_row_ref, rank_col_ref, table_ref, out_ref):
    rows, cols = buckets_ref.shape
    heads = table_ref.shape[0]
    start = pl.program_id(0) * rows
    key = start + lax.broadcasted_iota(jnp.int32, (rows, cols), 0)
    query = lax.broadcasted_iota(jnp.int32, (rows, cols), 1)
    valid = key < len_ref[0]
    rank_key = rank_col_ref[...]
    rank_query = rank_row_ref[...]
    content = (valid & (rank_key <= rank_query)) | (key == query)
    stream = (valid & (rank_key < rank_query)) | (key == 0)
    index = buckets_ref[...]
    for head in range(heads):
        row = jnp.broadcast_to(table_ref[head : head + 1, :], (rows, 128))
        bias = jnp.concatenate(
            [
                jnp.take_along_axis(
                    row, index[:, c : c + 128], axis=1, mode="promise_in_bounds"
                )
                for c in range(0, cols, 128)
            ],
            axis=1,
        )
        out_ref[head, :, :cols] = jnp.where(content, bias, NEG).astype(BF)
        out_ref[head, :, cols:] = jnp.where(stream, bias, NEG).astype(BF)


def masked_bias(length, buckets_t, rank, table, after=()):
    seq = buckets_t.shape[0]
    heads = table.shape[0]
    step = 128
    return call(
        bias_kernel,
        after,
        [length, buckets_t, rank.reshape(1, seq), rank.reshape(seq, 1), table],
        grid=(seq // step,),
        in_specs=[
            pl.BlockSpec(memory_space=pltpu.SMEM),
            pl.BlockSpec((step, seq), lambda g: (g, 0)),
            pl.BlockSpec((1, seq), lambda g: (0, 0)),
            pl.BlockSpec((step, 1), lambda g: (g, 0)),
            pl.BlockSpec((heads, 128), lambda g: (0, 0)),
        ],
        out_specs=pl.BlockSpec((heads, step, 2 * seq), lambda g: (0, g, 0)),
        out_shape=jax.ShapeDtypeStruct((heads, seq, 2 * seq), BF),
        cost_estimate=cost(9),
    )


def forward_kernel(q_ref, k_ref, v_ref, bias_ref, probs_ref, ctx_ref, inv_ref, *, tile):
    keys = (k_ref[...].astype(F32) * 0.125).astype(BF)
    values = v_ref[...]
    for t in range(q_ref.shape[1] // tile):
        at = pl.ds(t * tile, tile)
        scores = dot(keys, q_ref[:, at], TN) + bias_ref[0, :, at].astype(F32)
        high = jnp.max(scores, axis=0, keepdims=True)
        weight = jnp.exp(scores - high)
        inverse = 1.0 / jnp.sum(weight, axis=0, keepdims=True)
        low = weight.astype(BF)
        probs_ref[0, :, at] = low
        ctx_ref[:, at] = (dot(values, low, NN) * inverse).astype(BF)
        inv_ref[0, :, at] = inverse


def attention(q_t, k_t, v_t, bias, heads, tile=256, after=()):
    width, both = q_t.shape
    seq = k_t.shape[1]
    size = width // heads
    return call(
        functools.partial(forward_kernel, tile=tile),
        after,
        [q_t, k_t, v_t, bias],
        grid=(heads,),
        in_specs=[
            pl.BlockSpec((size, both), lambda h: (h, 0)),
            pl.BlockSpec((size, seq), lambda h: (h, 0)),
            pl.BlockSpec((size, seq), lambda h: (h, 0)),
            pl.BlockSpec((1, seq, both), lambda h: (h, 0, 0)),
        ],
        out_specs=[
            pl.BlockSpec((1, seq, both), lambda h: (h, 0, 0)),
            pl.BlockSpec((size, both), lambda h: (h, 0)),
            pl.BlockSpec((1, 1, both), lambda h: (h, 0, 0)),
        ],
        out_shape=[
            jax.ShapeDtypeStruct((heads, seq, both), BF),
            jax.ShapeDtypeStruct((width, both), BF),
            jax.ShapeDtypeStruct((heads, 1, both), F32),
        ],
        cost_estimate=cost(24),
    )


def backward_kernel(
    q_ref, k_ref, v_ref, p_ref, inv_ref, ctx_ref, dctx_ref, *refs, tile
):
    dq_ref, dk_ref, dv_ref, held_ref = refs[-4:]
    seq = k_ref.shape[1]
    group = held_ref.shape[1]
    queries = q_ref[...]
    keys = k_ref[...]
    values = v_ref[...]
    grad = dctx_ref[...].astype(F32) * inv_ref[0]
    inner = jnp.sum(grad * ctx_ref[...].astype(F32), axis=0, keepdims=True)
    grad = grad.astype(BF)
    dk = jnp.zeros(keys.shape, F32)
    dv = jnp.zeros(keys.shape, F32)
    for t in range(seq // tile):
        both = None
        for stream in range(2):
            lo = stream * seq + t * tile
            at = slice(lo, lo + tile)
            weight = p_ref[0, :, at]
            part = dot(values, grad[:, at], TN) - inner[:, at]
            ds = weight.astype(F32) * part
            low = ds.astype(BF)
            dv += dot(grad[:, at], weight, NT)
            dk += dot(queries[:, at], low, NT)
            dq_ref[:, at] = (dot(keys, low, NN) * 0.125).astype(BF)
            both = ds if both is None else both + ds
        held_ref[:, :, t * tile : (t + 1) * tile] = both.astype(BF).reshape(seq // group, group, tile)
    dk_ref[...] = (dk * 0.125).astype(BF)
    dv_ref[...] = dv.astype(BF)


def attention_back(q_t, k_t, v_t, probs, inverse, ctx_t, dctx_t, before, heads, begin, count, group=16, tile=256, after=()):
    width, both = q_t.shape
    seq = k_t.shape[1]
    size = width // heads
    wide = pl.BlockSpec((size, both), lambda h: (h + begin, 0))
    thin = pl.BlockSpec((size, seq), lambda h: (h + begin, 0))
    operands = [q_t, k_t, v_t, probs, inverse, ctx_t, dctx_t, *before]
    return call(
        functools.partial(backward_kernel, tile=tile),
        after,
        operands,
        grid=(count,),
        in_specs=[
            wide,
            thin,
            thin,
            pl.BlockSpec((1, seq, both), lambda h: (h + begin, 0, 0)),
            pl.BlockSpec((1, 1, both), lambda h: (h + begin, 0, 0)),
            wide,
            wide,
        ]
        + [pl.BlockSpec(memory_space=pl.ANY)] * len(before),
        out_specs=[
            wide,
            thin,
            thin,
            pl.BlockSpec((seq // group, group, seq), lambda h: (0, h + begin, 0)),
        ],
        out_shape=[
            jax.ShapeDtypeStruct((width, both), BF),
            jax.ShapeDtypeStruct((width, seq), BF),
            jax.ShapeDtypeStruct((width, seq), BF),
            jax.ShapeDtypeStruct((seq // group, heads * group, seq), BF),
        ],
        input_output_aliases={7 + i: i for i in range(len(before))},
        compiler_params=pltpu.CompilerParams(vmem_limit_bytes=56 * 1024 * 1024),
        cost_estimate=cost(2.2 * count),
    )


def table_kernel(buckets_ref, *refs, buckets, group):
    held_ref, out_ref, total = refs
    step, steps = pl.program_id(0), pl.num_programs(0)
    parts = buckets_ref.shape[0] // group
    index = buckets_ref[...].astype(F32).astype(BF)
    hot = jnp.concatenate(
        [
            jnp.concatenate(
                [
                    jnp.where(index[p * group : (p + 1) * group] == jnp.asarray(n, BF), 1.0, 0.0).astype(BF)
                    for n in range(buckets)
                ],
                axis=0,
            )
            for p in range(parts)
        ],
        axis=1,
    )
    held = jnp.concatenate([held_ref[p] for p in range(parts)], axis=1)
    value = dot(hot, held, NT)

    @pl.when(step == 0)
    def _():
        total[...] = value

    @pl.when(step > 0)
    def _():
        total[...] += value

    @pl.when(step == steps - 1)
    def _():
        value = total[...]
        row = lax.broadcasted_iota(jnp.int32, value.shape, 0) % group
        col = lax.broadcasted_iota(jnp.int32, value.shape, 1) % group
        kept = jnp.where(row == col, value, 0.0)
        out_ref[...] = jnp.sum(kept.reshape(buckets, group, value.shape[1]), axis=1)


def table_back(buckets_t, held, buckets, group=16, parts=4, after=()):
    seq = buckets_t.shape[0]
    cols = held.shape[1]
    return call(
        functools.partial(table_kernel, buckets=buckets, group=group),
        after,
        [buckets_t, held],
        grid=(seq // (group * parts),),
        in_specs=[
            pl.BlockSpec((group * parts, seq), lambda g: (g, 0)),
            pl.BlockSpec((parts, cols, seq), lambda g: (g, 0, 0)),
        ],
        out_specs=whole((buckets, cols)),
        out_shape=jax.ShapeDtypeStruct((buckets, cols), F32),
        scratch_shapes=[pltpu.VMEM((buckets * group, cols), F32)],
        compiler_params=pltpu.CompilerParams(vmem_limit_bytes=40 * 1024 * 1024),
        cost_estimate=cost(6),
    )


def call(kernel, after, operands, *, in_specs, **settings):
    count = len(operands)

    def body(*refs):
        kernel(*refs[:count], *refs[count + len(after) :])

    anywhere = [pl.BlockSpec(memory_space=pl.ANY)] * len(after)
    return pl.pallas_call(body, in_specs=in_specs + anywhere, **settings)(*operands, *after)


def whole(shape):
    return pl.BlockSpec(shape, lambda *_: (0,) * len(shape))


def once(shape, at):
    return pl.BlockSpec(shape, lambda *_: at, pipeline_mode=pl.Buffered(1))


def unit(value):
    centred = value - jnp.mean(value, axis=-1, keepdims=True)
    inverse = lax.rsqrt(jnp.mean(centred * centred, axis=-1, keepdims=True) + EPSILON)
    return centred * inverse, inverse


def unit_back(grad, along, inverse):
    mean = jnp.mean(grad, axis=-1, keepdims=True)
    slope = jnp.mean(grad * along, axis=-1, keepdims=True)
    return (grad - mean - along * slope) * inverse


def column_sum(value):
    rows = value.shape[0]
    return jnp.sum(value.reshape(rows // 8, 8, value.shape[1]), axis=0)


def up_kernel(
    ctx_ref, x_ref, cot_ref, wo_ref, wi_ref, wd_ref, bi_ref, rows_ref,
    out_ref, lowt_ref, act_ref, slope_ref, unit_ref, inv_ref, dres_ref, dlow_ref, dlowt_ref, sums_ref,
    *, chunk, part_rows,
):
    halves, width, part = wo_ref.shape
    ffn = wi_ref.shape[2]
    row = lambda i: rows_ref[i : i + 1, :]
    parts = [slice(r, r + part_rows) for r in range(0, x_ref.shape[0], part_rows)]
    resids, lows = [], []
    for at in parts:
        resid = x_ref[at, :].astype(F32) + row(0)
        for y in range(halves):
            resid += dot(ctx_ref[y * part : (y + 1) * part, at].T, wo_ref[y], NT)
        along, inverse = unit(resid)
        unit_ref[at, :] = along
        inv_ref[at, :] = inverse
        normed = along * row(2) + row(4)
        low = normed.astype(BF)
        lowt_ref[:, at] = low.T
        resids.append(normed + row(1))
        lows.append(low)
    for y in range(halves):
        for n, at in enumerate(parts):
            for c in range(0, ffn, chunk):
                cols = slice(c, c + chunk)
                hidden = dot(lows[n], wi_ref[y, :, cols], NN) + bi_ref[y, :, cols]
                cdf = 0.5 * lax.erf(hidden * 0.7071067811865476) + 0.5
                density = jnp.exp(hidden * hidden * -0.5) * 0.3989422804014327
                act_ref[y, at, cols] = (hidden * cdf).astype(BF)
                slope_ref[y, at, cols] = (cdf + hidden * density).astype(BF)
            resids[n] += dot(act_ref[y, at, :], wd_ref[y], NT)
    sums = [0.0, 0.0, 0.0]
    for n, at in enumerate(parts):
        along, inverse = unit(resids[n])
        out_ref[at, :] = (along * row(3) + row(5)).astype(BF)
        cot = cot_ref[at, :].astype(F32)
        dres = unit_back(cot * row(3), along, inverse)
        dres_ref[at, :] = dres
        dlow = dres.astype(BF)
        dlow_ref[at, :] = dlow
        dlowt_ref[:, at] = dlow.T
        for i, value in enumerate((dres, cot * along, cot)):
            sums[i] += column_sum(value)
    for i in range(3):
        sums_ref[0, i] = sums[i]


def up(ctx_t, stacked, cot, rest, hidden_bias, rows, part, tile=256, chunk=512, part_rows=256, after=()):
    tokens, width = stacked.shape
    halves = rest.shape[0]
    ffn = (rest.shape[2] - part) // 2
    tall = pl.BlockSpec((width, tile), lambda t: (0, t))
    flat = pl.BlockSpec((tile, width), lambda t: (t, 0))
    wide = pl.BlockSpec((halves, tile, ffn), lambda t: (0, t, 0))
    sds = jax.ShapeDtypeStruct
    return call(
        functools.partial(up_kernel, chunk=chunk, part_rows=part_rows),
        after,
        [ctx_t, stacked, cot, rest, rest, rest, hidden_bias, rows],
        grid=(tokens // tile,),
        in_specs=[
            tall,
            flat,
            flat,
            once((halves, width, part), (0, 0, 2 * ffn // part)),
            once((halves, width, ffn), (0, 0, 0)),
            once((halves, width, ffn), (0, 0, 1)),
            whole((halves, 1, ffn)),
            whole(rows.shape),
        ],
        out_specs=[
            flat, tall, wide, wide, flat, pl.BlockSpec((tile, 1), lambda t: (t, 0)), flat, flat, tall,
            pl.BlockSpec((1, 3, 8, width), lambda t: (t, 0, 0, 0)),
        ],
        out_shape=[
            sds((tokens, width), BF),
            sds((width, tokens), BF),
            sds((halves, tokens, ffn), BF),
            sds((halves, tokens, ffn), BF),
            sds((tokens, width), F32),
            sds((tokens, 1), F32),
            sds((tokens, width), F32),
            sds((tokens, width), BF),
            sds((width, tokens), BF),
            sds((tokens // tile, 3, 8, width), F32),
        ],
        compiler_params=pltpu.CompilerParams(vmem_limit_bytes=58 * 1024 * 1024),
        cost_estimate=cost(20),
    )


def down_kernel(
    dlow_ref, dres_ref, slope_ref, unit_ref, inv_ref, wo_ref, wi_ref, wd_ref, rows_ref,
    dhid_ref, done_ref, dot_ref, dctx_ref, sums_ref, hsum_ref, *, chunk, part_rows,
):
    halves, width, part = wo_ref.shape
    ffn = wi_ref.shape[2]
    parts = [slice(r, r + part_rows) for r in range(0, dlow_ref.shape[0], part_rows)]
    dnorms = [dres_ref[at, :] for at in parts]
    for y in range(halves):
        for n, at in enumerate(parts):
            for c in range(0, ffn, chunk):
                cols = slice(c, c + chunk)
                dhid = dot(dlow_ref[at, :], wd_ref[y, :, cols], NN) * slope_ref[y, at, cols].astype(F32)
                hsum_ref[0, n, y, :, cols] = column_sum(dhid)
                dhid_ref[y, at, cols] = dhid.astype(BF)
            dnorms[n] += dot(dhid_ref[y, at, :], wi_ref[y], NT)
    sums = [0.0, 0.0, 0.0]
    for n, at in enumerate(parts):
        dnorm = dnorms[n]
        along = unit_ref[at, :]
        done = unit_back(dnorm * rows_ref[2:3, :], along, inv_ref[at, :])
        done_ref[at, :] = done
        low = done.astype(BF)
        dot_ref[:, at] = low.T
        for y in range(halves):
            dctx_ref[y * part : (y + 1) * part, at] = dot(low, wo_ref[y], NN).astype(BF).T
        for i, value in enumerate((done, dnorm * along, dnorm)):
            sums[i] += column_sum(value)
    for i in range(3):
        sums_ref[0, i] = sums[i]


def down(dlow, dres, slope, along, inverse, rest, rows, part, tile=256, chunk=512, part_rows=256, after=()):
    tokens, width = dlow.shape
    halves = rest.shape[0]
    ffn = (rest.shape[2] - part) // 2
    tall = pl.BlockSpec((width, tile), lambda t: (0, t))
    flat = pl.BlockSpec((tile, width), lambda t: (t, 0))
    wide = pl.BlockSpec((halves, tile, ffn), lambda t: (0, t, 0))
    sds = jax.ShapeDtypeStruct
    return call(
        functools.partial(down_kernel, chunk=chunk, part_rows=part_rows),
        after,
        [dlow, dres, slope, along, inverse, rest, rest, rest, rows],
        grid=(tokens // tile,),
        in_specs=[
            flat,
            flat,
            wide,
            flat,
            pl.BlockSpec((tile, 1), lambda t: (t, 0)),
            once((halves, width, part), (0, 0, 2 * ffn // part)),
            once((halves, width, ffn), (0, 0, 0)),
            once((halves, width, ffn), (0, 0, 1)),
            whole(rows.shape),
        ],
        out_specs=[
            wide, flat, tall, tall,
            pl.BlockSpec((1, 3, 8, width), lambda t: (t, 0, 0, 0)),
            pl.BlockSpec((1, tile // part_rows, halves, 8, ffn), lambda t: (t, 0, 0, 0, 0)),
        ],
        out_shape=[
            sds((halves, tokens, ffn), BF),
            sds((tokens, width), F32),
            sds((width, tokens), BF),
            sds((width, tokens), BF),
            sds((tokens // tile, 3, 8, width), F32),
            sds((tokens // tile, tile // part_rows, halves, 8, ffn), F32),
        ],
        compiler_params=pltpu.CompilerParams(vmem_limit_bytes=58 * 1024 * 1024),
        cost_estimate=cost(18),
    )


def put_rows(core, value, keep_ref, send_ref, at):
    chips, rows = keep_ref.shape[1], keep_ref.shape[2]
    value = value.reshape(chips, 2, rows, value.shape[1])

    @pl.when(core == 0)
    def _():
        keep_ref[at] = value[:, 0]
        send_ref[at] = value[:, 1]

    @pl.when(core != 0)
    def _():
        keep_ref[at] = value[:, 1]
        send_ref[at] = value[:, 0]


def outer_kernel(core_ref, left_ref, right_ref, keep_ref, send_ref):
    value = dot(left_ref[...], right_ref[0], NN).astype(BF)
    put_rows(core_ref[0], value, keep_ref, send_ref, 0)


def outer(core, left_t, right, rows, tile=768, after=()):
    width, tokens = left_t.shape
    halves, _, cols = right.shape
    block = pl.BlockSpec((1, width // (2 * rows), rows, tile), lambda y, c: (y, 0, 0, c))
    shape = jax.ShapeDtypeStruct((halves, width // (2 * rows), rows, cols), BF)
    return call(
        outer_kernel,
        after,
        [core, left_t, right],
        grid=(halves, cols // tile),
        in_specs=[
            pl.BlockSpec(memory_space=pltpu.SMEM),
            whole(left_t.shape),
            pl.BlockSpec((1, tokens, tile), lambda y, c: (y, 0, c)),
        ],
        out_specs=[block, block],
        out_shape=[shape, shape],
        cost_estimate=cost(5),
    )


def outer_in_kernel(core_ref, low_ref, dhid_ref, dot_ref, ctx_ref, keep_ref, send_ref, *, chunk):
    ffn = dhid_ref.shape[2]
    values = [dot(low_ref[...], dhid_ref[0, :, c : c + chunk], NN).astype(BF) for c in range(0, ffn, chunk)]
    values.append(dot(dot_ref[...], ctx_ref[...], NT).astype(BF))
    put_rows(core_ref[0], jnp.concatenate(values, axis=1), keep_ref, send_ref, 0)


def outer_in(core, low_t, dhid, do_t, ctx_t, rows, chunk=768, after=()):
    width, tokens = low_t.shape
    halves, _, ffn = dhid.shape
    part = ctx_t.shape[0] // halves
    block = pl.BlockSpec((1, width // (2 * rows), rows, ffn + part), lambda y: (y, 0, 0, 0))
    shape = jax.ShapeDtypeStruct((halves, width // (2 * rows), rows, ffn + part), BF)
    return call(
        functools.partial(outer_in_kernel, chunk=chunk),
        after,
        [core, low_t, dhid, do_t, ctx_t],
        grid=(halves,),
        in_specs=[
            pl.BlockSpec(memory_space=pltpu.SMEM),
            whole(low_t.shape),
            pl.BlockSpec((1, tokens, ffn), lambda y: (y, 0, 0)),
            whole(do_t.shape),
            pl.BlockSpec((part, tokens), lambda y: (y, 0)),
        ],
        out_specs=[block, block],
        out_shape=[shape, shape],
        compiler_params=pltpu.CompilerParams(vmem_limit_bytes=48 * 1024 * 1024),
        cost_estimate=cost(6),
    )


def project_kernel(core_ref, own_a, own_b, other_a, other_b, x_ref, bias_ref, q_ref, k_ref, v_ref, w_ref):
    core = core_ref[0]
    cut = own_a.shape[3]
    width = x_ref.shape[1]
    part, seq = k_ref.shape
    w_ref[0, :, core, :, :cut] = own_a[0]
    w_ref[0, :, core, :, cut:] = own_b[0]
    w_ref[0, :, 1 - core, :, :cut] = other_a[0]
    w_ref[0, :, 1 - core, :, cut:] = other_b[0]
    weights = w_ref[0].reshape(width, 3 * part)
    q = dot(x_ref[...], weights[:, :part], NN) + bias_ref[0, 0:1, :]
    q_ref[...] = q.astype(BF).T
    kv = dot(x_ref[:seq, :], weights[:, part:], NN)
    k_ref[...] = kv[:, :part].astype(BF).T
    v_ref[...] = (kv[:, part:] + bias_ref[0, 1:2, :]).astype(BF).T


def project(core, pieces, stacked, bias, part, after=()):
    tokens, width = stacked.shape
    halves, chips, rows, cut = pieces[0].shape
    cols = 3 * part
    seq = tokens // 2
    sds = jax.ShapeDtypeStruct
    one = pl.BlockSpec((1, chips, rows, cut), lambda y: (y, 0, 0, 0))
    two = pl.BlockSpec((1, chips, rows, cols - cut), lambda y: (y, 0, 0, 0))
    return call(
        project_kernel,
        after,
        [core, *pieces, stacked, bias],
        grid=(halves,),
        in_specs=[
            pl.BlockSpec(memory_space=pltpu.SMEM), one, two, one, two,
            whole(stacked.shape),
            pl.BlockSpec((1, 2, part), lambda y: (y, 0, 0)),
        ],
        out_specs=[
            pl.BlockSpec((part, tokens), lambda y: (y, 0)),
            pl.BlockSpec((part, seq), lambda y: (y, 0)),
            pl.BlockSpec((part, seq), lambda y: (y, 0)),
            pl.BlockSpec((1, chips, 2, rows, cols), lambda y: (y, 0, 0, 0, 0)),
        ],
        out_shape=[
            sds((width, tokens), BF),
            sds((width, seq), BF),
            sds((width, seq), BF),
            sds((halves, chips, 2, rows, cols), BF),
        ],
        compiler_params=pltpu.CompilerParams(vmem_limit_bytes=40 * 1024 * 1024),
        cost_estimate=cost(6),
    )


def project_back_kernel(core_ref, x_ref, dq_ref, dk_ref, dv_ref, ka_ref, sa_ref, kb_ref, sb_ref, xt_ref):
    core = core_ref[0]
    part = dq_ref.shape[0]
    cut = ka_ref.shape[3]

    @pl.when(pl.program_id(0) == 0)
    def _():
        xt_ref[...] = x_ref[...].T

    values = []
    for ref in (dq_ref, dk_ref, dv_ref):
        tokens = ref.shape[1]
        values.append(dot(xt_ref[:, :tokens], ref[...], NT).astype(BF))
    value = jnp.concatenate(values, axis=1)
    put_rows(core, value[:, :cut], ka_ref, sa_ref, 0)
    put_rows(core, value[:, cut:], kb_ref, sb_ref, 0)


def project_back(core, stacked, dq_t, dk_t, dv_t, halves, rows, cut, after=()):
    tokens, width = stacked.shape
    chips = width // (2 * rows)
    part = width // halves
    one = pl.BlockSpec((1, chips, rows, cut), lambda y: (y, 0, 0, 0))
    two = pl.BlockSpec((1, chips, rows, 3 * part - cut), lambda y: (y, 0, 0, 0))
    first = jax.ShapeDtypeStruct((halves, chips, rows, cut), BF)
    second = jax.ShapeDtypeStruct((halves, chips, rows, 3 * part - cut), BF)
    return call(
        project_back_kernel,
        after,
        [core, stacked, dq_t, dk_t, dv_t],
        grid=(halves,),
        in_specs=[pl.BlockSpec(memory_space=pltpu.SMEM), whole(stacked.shape)]
        + [pl.BlockSpec((part, g.shape[1]), lambda y: (y, 0)) for g in (dq_t, dk_t, dv_t)],
        out_specs=[one, one, two, two],
        out_shape=[first, first, second, second],
        scratch_shapes=[pltpu.VMEM((width, tokens), BF)],
        compiler_params=pltpu.CompilerParams(vmem_limit_bytes=40 * 1024 * 1024),
        cost_estimate=cost(5),
    )


def inputs_kernel(half_ref, w_ref, done_ref, dq_ref, dk_ref, dv_ref, keep_ref, send_ref, sum_ref):
    step, steps = pl.program_id(0), pl.num_programs(0)
    halves, width, cols = w_ref.shape
    part = cols // 3
    total = done_ref[...]
    for y in range(halves):
        total += dot(dq_ref[y * part : (y + 1) * part, :].T, w_ref[y, :, :part], NT)
    sum_ref[...] = total

    @pl.when(step < steps // 2)
    def _():
        extra = 0.0
        for y in range(halves):
            at = slice(y * part, (y + 1) * part)
            extra += dot(dk_ref[at, :].T, w_ref[y, :, part : 2 * part], NT)
            extra += dot(dv_ref[at, :].T, w_ref[y, :, 2 * part :], NT)
        sum_ref[...] += extra

    half = width // 2

    @pl.when(half_ref[0] == 0)
    def _():
        keep_ref[...] = sum_ref[:, :half].astype(BF)
        send_ref[...] = sum_ref[:, half:].astype(BF)

    @pl.when(half_ref[0] != 0)
    def _():
        keep_ref[...] = sum_ref[:, half:].astype(BF)
        send_ref[...] = sum_ref[:, :half].astype(BF)


def inputs_back(half, weights, done, dq_t, dk_t, dv_t, tile=256, after=()):
    tokens, width = done.shape
    last = tokens // (2 * tile) - 1
    thin = pl.BlockSpec((width, tile), lambda t: (0, jnp.minimum(t, last)))
    out = pl.BlockSpec((tile, width // 2), lambda t: (t, 0))
    return call(
        inputs_kernel,
        after,
        [half, weights, done, dq_t, dk_t, dv_t],
        grid=(tokens // tile,),
        in_specs=[
            pl.BlockSpec(memory_space=pltpu.SMEM),
            once(weights.shape, (0, 0, 0)),
            pl.BlockSpec((tile, width), lambda t: (t, 0)),
            pl.BlockSpec((width, tile), lambda t: (0, t)),
            thin,
            thin,
        ],
        out_specs=[out, out],
        out_shape=[jax.ShapeDtypeStruct((tokens, width // 2), BF)] * 2,
        scratch_shapes=[pltpu.VMEM((tile, width), F32)],
        compiler_params=pltpu.CompilerParams(vmem_limit_bytes=40 * 1024 * 1024),
        cost_estimate=cost(5),
    )


def shifted(value, axis, step):
    size = lax.axis_size(axis)
    return lax.ppermute(value, axis, [(i, (i + step) % size) for i in range(size)])


def gather_axis(value, axis, where):
    size = lax.axis_size(axis)
    me = lax.axis_index(axis)
    pieces = [value] + [shifted(value, axis, k) for k in range(1, size)]
    slots = []
    for j in range(size):
        which = lax.rem(me - j + size, size)
        chosen = pieces[0]
        for k in range(1, size):
            chosen = jnp.where(which == k, pieces[k], chosen)
        slots.append(chosen)
    return jnp.stack(slots, axis=where)


def gather_rows(shard, order):
    names = ["y", "z", "x", "core"]
    value, have = shard, []
    for axis in order:
        where = sum(names.index(a) < names.index(axis) for a in have)
        value = gather_axis(value, axis, where)
        have.append(axis)
    return value


def start(value, axis, where):
    size = lax.axis_size(axis)
    me = lax.axis_index(axis)
    parts = [lax.dynamic_index_in_dim(value, me, where, keepdims=False)]
    for k in range(1, size):
        out = lax.dynamic_index_in_dim(value, lax.rem(me + k, size), where, keepdims=False)
        parts.append(shifted(out, axis, k))
    return parts


def finish(parts, low=True):
    total = sum(part.astype(F32) for part in parts)
    return total.astype(BF) if low else total


def start_core(keep, send):
    return [keep, shifted(send, "core", 1)]


def finish_core(parts):
    value = finish(parts)
    halves, _, rows, cols = value.shape
    return value.reshape(halves, lax.axis_size("z"), lax.axis_size("x"), rows, cols)


def tie(*groups):
    return lax.optimization_barrier(groups)


def sum_pairs(value, axes):
    for axis in axes:
        size = lax.axis_size(axis)
        step = 1
        while step < size:
            value = value + lax.ppermute(value, axis, [(i, i ^ step) for i in range(size)])
            step *= 2
    return value


def shards(
    content_in,
    query_in,
    lengths,
    factor_order,
    buckets,
    w_qkv,
    b_qv,
    w_out,
    w_in,
    b_in,
    w_down,
    b_outs,
    norm_gain,
    norm_bias,
    rel_table,
    cot_content,
    cot_query,
):
    me = lax.axis_index("y")
    halves = lax.axis_size("y")
    each = content_in.shape[0] // halves
    assert each == 1
    seq = content_in.shape[1]
    width = content_in.shape[2]
    bucket_count, heads_here = rel_table.shape
    heads = heads_here * halves
    part = w_qkv.shape[2]
    ffn = w_in.shape[1]
    rows = w_in.shape[0]

    def mine(array):
        return lax.dynamic_index_in_dim(array, me, 0, keepdims=False)

    rest_shard = jnp.concatenate([w_in, w_down.T, w_out.T], axis=1)
    rest = lax.all_gather(rest_shard, ("y", "z", "x", "core"), axis=0).reshape(
        halves, width, 2 * ffn + part
    )

    vectors = jnp.concatenate([b_qv, b_in.reshape(ffn // part, part)], axis=0)
    vectors = jnp.concatenate(
        [vectors, jnp.pad(rel_table, ((0, 0), (0, part - heads_here)))], axis=0
    )
    vectors = gather_axis(vectors, "y", 0).astype(F32)
    qv_bias = vectors[:, :2]
    hidden_bias = vectors[:, 2 : 2 + ffn // part].reshape(halves, 1, ffn)
    table = vectors[:, 2 + ffn // part :, :heads_here]
    table = jnp.transpose(table, (0, 2, 1)).reshape(heads, bucket_count)
    table = jnp.pad(table, ((0, 0), (0, 128 - bucket_count)))
    vector_rows = jnp.concatenate([b_outs, norm_gain, norm_bias], axis=0).astype(F32)
    vector_rows = jnp.pad(vector_rows, ((0, 2), (0, 0)))

    core = lax.axis_index("core").astype(jnp.int32).reshape(1)
    content = mine(content_in)
    stacked = jnp.concatenate([content, mine(query_in)], axis=0)
    buckets_t = mine(buckets).T
    rank = mine(factor_order)
    length = lax.dynamic_slice_in_dim(lengths, me, 1, 0)
    bias = masked_bias(length, buckets_t, rank, table)

    qkv_shard = jnp.transpose(w_qkv, (1, 0, 2)).reshape(rows, 3 * part)
    cut = 5 * part // 3
    along_z = gather_axis(qkv_shard, "z", 0)
    one = gather_axis(along_z[:, :, :cut], "x", 1)
    two = gather_axis(along_z[:, :, cut:], "y", 0)
    one, two, bias = lax.optimization_barrier((one, two, bias))
    one = gather_axis(one, "y", 0)
    two = gather_axis(two, "x", 2)
    chips = width // (2 * rows)
    one = one.reshape(halves, chips, rows, cut)
    two = two.reshape(halves, chips, rows, 3 * part - cut)
    pieces = (one, two, shifted(one, "core", 1), shifted(two, "core", 1))

    q_t, k_t, v_t, full_qkv = project(core, pieces, stacked, qv_bias, part)
    probs, ctx_t, inverse = attention(q_t, k_t, v_t, bias, heads)

    cot = jnp.concatenate([mine(cot_content), mine(cot_query)], axis=0)
    output, low_t, active, slope, unit_one, inv_one, d_two, d_two_low, d_two_low_t, sums_two = up(
        ctx_t, stacked, cot, rest, hidden_bias, vector_rows, part
    )
    outs = lax.all_gather(output, "y", axis=0).reshape(halves, 2, seq, width)
    pending = start_core(*outer(core, d_two_low_t, active, rows))
    share = finish_core(pending)
    pending = start(share, "x", 2)
    after_up = down(
        d_two_low, d_two, slope, unit_one, inv_one, rest, vector_rows, part, after=(share,)
    )
    pending, after_up = tie(pending, after_up)
    d_hidden, d_one, d_one_low_t, dctx_t, sums_one, sums_hidden = after_up
    share = finish(pending)
    pending = start(share, "y", 0)
    in_pair = outer_in(core, low_t, d_hidden, d_one_low_t, ctx_t, rows, after=(share,))
    pending, outs, in_pair = tie(pending, outs, in_pair)
    share = finish(pending)
    pending = start(share, "z", 0)
    in_pending = start_core(*in_pair)

    calls = 2 * halves
    each_call = heads // calls
    waits, done = (share,), ()
    for i in range(calls):
        done = attention_back(
            q_t, k_t, v_t, probs, inverse, ctx_t, dctx_t, tuple(done), heads, i * each_call, each_call,
            after=waits,
        )
        waits = ()
        if i == 0:
            in_pending, done = tie(in_pending, done)
            in_share = finish_core(in_pending)
            in_pending = start(in_share, "x", 2)
            waits = (in_share,)
        if i == 1:
            pending, done = tie(pending, done)
            down_share = finish(pending, low=False)
    in_pending, done = tie(in_pending, done)
    in_share = finish(in_pending)
    in_pending = start(in_share, "y", 0)
    dq_t, dk_t, dv_t, held = done
    pairs = project_back(core, stacked, dq_t, dk_t, dv_t, halves, rows, cut, after=(in_share,))
    one_pending, two_pending = start_core(*pairs[:2]), start_core(*pairs[2:])
    half = me.astype(jnp.int32).reshape(1)
    grad_in = inputs_back(
        half, full_qkv.reshape(halves, width, 3 * part), d_one, dq_t, dk_t, dv_t, after=pairs
    )
    one_pending, two_pending, grad_in = tie(one_pending, two_pending, grad_in)
    one_share, two_share = finish_core(one_pending), finish_core(two_pending)
    one_pending, two_pending = start(one_share, "x", 2), start(two_share, "y", 0)
    table_grad = table_back(buckets_t, held, bucket_count, after=(one_share, two_share))
    one_pending, two_pending, in_pending, table_grad = tie(
        one_pending, two_pending, in_pending, table_grad
    )
    one_pending = start(finish(one_pending), "y", 0)
    two_pending = start(finish(two_pending), "x", 1)
    in_pending = start(finish(in_pending), "z", 0)
    grad_kept, grad_sent = grad_in
    grad_got = shifted(grad_sent, "y", 1)

    table_grad = jnp.sum(table_grad.reshape(bucket_count, heads, -1), axis=2).T
    sums_one = jnp.sum(sums_one, axis=(0, 2))
    sums_two = jnp.sum(sums_two, axis=(0, 2))
    small = jnp.concatenate(
        [jnp.sum(g.astype(F32), axis=1) for g in (dq_t, dv_t)]
        + [table_grad.reshape(-1), jnp.sum(sums_hidden, axis=(0, 1, 3)).reshape(-1)]
        + [s[i] for i in range(3) for s in (sums_one, sums_two)]
    )
    small = sum_pairs(small.reshape(-1, 128), ("core", "x"))
    one_pending, two_pending, small = tie(one_pending, two_pending, small)
    qkv_share = jnp.concatenate([finish(one_pending), finish(two_pending)], axis=-1)
    qkv_pending = start(qkv_share, "z", 0)
    in_share = finish(in_pending, low=False)
    small = sum_pairs(small, ("y", "z")).reshape(-1)
    first_kept = me == 0
    grad_ins = jnp.stack(
        [jnp.where(first_kept, grad_kept, grad_got), jnp.where(first_kept, grad_got, grad_kept)]
    ).reshape(halves, 2, seq, width // halves)
    qkv_share = finish(qkv_pending, low=False)
    ends = [2 * width, 2 * width + heads * bucket_count]
    ends.append(ends[1] + halves * ffn)
    grad_b_qv = mine(jnp.transpose(small[: ends[0]].reshape(2, halves, part), (1, 0, 2)))
    grad_table = mine(small[ends[0] : ends[1]].reshape(halves, heads_here, bucket_count)).T
    grad_b_in = mine(small[ends[1] : ends[2]].reshape(halves, ffn))
    pairs = small[ends[2] :].reshape(3, 2, width)
    return (
        outs[:, 0],
        outs[:, 1],
        grad_ins[:, 0],
        grad_ins[:, 1],
        jnp.transpose(qkv_share.reshape(rows, 3, part), (1, 0, 2)),
        grad_b_qv,
        in_share[:, ffn:].T,
        in_share[:, :ffn],
        grad_b_in,
        down_share.T,
        pairs[0],
        pairs[1],
        pairs[2],
        grad_table,
    )


def solution(mesh):
    count = mesh.shape["dp"] // 2
    depth = 4 if count % 4 == 0 else 1
    while count // depth > depth:
        depth *= 2
    grid = mesh.devices.reshape(depth, count // depth, 2, mesh.shape["tensor"])
    fine = Mesh(grid, ("z", "x", "core", "y"))
    dp = ("z", "x", "core")
    return jax.shard_map(
        shards,
        mesh=fine,
        in_specs=(
            P(dp, None, None),
            P(dp, None, None),
            P(dp),
            P(dp, None),
            P(dp, None, None),
            P(None, dp, "y"),
            P(None, "y"),
            P("y", dp),
            P(dp, "y"),
            P("y"),
            P("y", dp),
            P(),
            P(),
            P(),
            P(None, "y"),
            P(dp, None, None),
            P(dp, None, None),
        ),
        out_specs=(
            P(dp, None, None),
            P(dp, None, None),
            P(dp, None, "y"),
            P(dp, None, "y"),
            P(None, dp, "y"),
            P(None, "y"),
            P("y", dp),
            P(dp, "y"),
            P("y"),
            P("y", dp),
            P(),
            P(),
            P(),
            P(None, "y"),
        ),
        check_vma=False,
    )
```

```python
import functools

import jax
import jax.numpy as jnp
from jax import lax
from jax.experimental import pallas as pl
from jax.experimental.pallas import tpu as pltpu
from jax.sharding import Mesh, PartitionSpec as P

EPSILON = 1e-05


def cost(us):
    return pl.CostEstimate(flops=int(us * 1e7), bytes_accessed=int(us * 1e4), transcendentals=0)

NEG = -1e30
BF = jnp.bfloat16
F32 = jnp.float32


def dot(a, b, dims):
    return lax.dot_general(a, b, (dims, ((), ())), preferred_element_type=F32)


NN = ((1,), (0,))
NT = ((1,), (1,))
TN = ((0,), (0,))


def bias_kernel(len_ref, buckets_ref, rank_row_ref, rank_col_ref, table_ref, out_ref):
    rows, cols = buckets_ref.shape
    heads = table_ref.shape[0]
    start = pl.program_id(0) * rows
    key = start + lax.broadcasted_iota(jnp.int32, (rows, cols), 0)
    query = lax.broadcasted_iota(jnp.int32, (rows, cols), 1)
    valid = key < len_ref[0]
    rank_key = rank_col_ref[...]
    rank_query = rank_row_ref[...]
    content = (valid & (rank_key <= rank_query)) | (key == query)
    stream = (valid & (rank_key < rank_query)) | (key == 0)
    index = buckets_ref[...]
    for head in range(heads):
        row = jnp.broadcast_to(table_ref[head : head + 1, :], (rows, 128))
        bias = jnp.concatenate(
            [
                jnp.take_along_axis(
                    row, index[:, c : c + 128], axis=1, mode="promise_in_bounds"
                )
                for c in range(0, cols, 128)
            ],
            axis=1,
        )
        out_ref[head, :, :cols] = jnp.where(content, bias, NEG).astype(BF)
        out_ref[head, :, cols:] = jnp.where(stream, bias, NEG).astype(BF)


def masked_bias(length, buckets_t, rank, table, after=()):
    seq = buckets_t.shape[0]
    heads = table.shape[0]
    step = 128
    return call(
        bias_kernel,
        after,
        [length, buckets_t, rank.reshape(1, seq), rank.reshape(seq, 1), table],
        grid=(seq // step,),
        in_specs=[
            pl.BlockSpec(memory_space=pltpu.SMEM),
            pl.BlockSpec((step, seq), lambda g: (g, 0)),
            pl.BlockSpec((1, seq), lambda g: (0, 0)),
            pl.BlockSpec((step, 1), lambda g: (g, 0)),
            pl.BlockSpec((heads, 128), lambda g: (0, 0)),
        ],
        out_specs=pl.BlockSpec((heads, step, 2 * seq), lambda g: (0, g, 0)),
        out_shape=jax.ShapeDtypeStruct((heads, seq, 2 * seq), BF),
        cost_estimate=cost(9),
    )


def forward_kernel(q_ref, k_ref, v_ref, bias_ref, probs_ref, ctx_ref, inv_ref, *, tile):
    count = bias_ref.shape[0]
    size = q_ref.shape[0] // count
    for head in range(count):
        rows = slice(head * size, (head + 1) * size)
        keys = (k_ref[rows, :].astype(F32) * 0.125).astype(BF)
        for t in range(q_ref.shape[1] // tile):
            at = slice(t * tile, (t + 1) * tile)
            scores = dot(keys, q_ref[rows, at], TN) + bias_ref[head, :, at].astype(F32)
            high = jnp.max(scores, axis=0, keepdims=True)
            weight = jnp.exp(scores - high)
            inverse = 1.0 / jnp.sum(weight, axis=0, keepdims=True)
            low = weight.astype(BF)
            probs_ref[head, :, at] = low
            ctx_ref[rows, at] = (dot(v_ref[rows, :], low, NN) * inverse).astype(BF)
            inv_ref[head, :, at] = inverse


def attention(q_t, k_t, v_t, bias, before, heads, begin, steps, tile=1024, count=2, after=()):
    width, both = q_t.shape
    seq = k_t.shape[1]
    size = width // heads * count
    thin = pl.BlockSpec((size, seq), lambda h: (h + begin, 0))
    wide = pl.BlockSpec((size, both), lambda h: (h + begin, 0))
    square = pl.BlockSpec((count, seq, both), lambda h: (h + begin, 0, 0))

    def kernel(q_ref, k_ref, v_ref, bias_ref, *refs):
        forward_kernel(q_ref, k_ref, v_ref, bias_ref, *refs[-3:], tile=tile)

    return call(
        kernel,
        after,
        [q_t, k_t, v_t, bias, *before],
        grid=(steps,),
        in_specs=[wide, thin, thin, square] + [pl.BlockSpec(memory_space=pl.ANY)] * len(before),
        out_specs=[square, wide, pl.BlockSpec((count, 1, both), lambda h: (h + begin, 0, 0))],
        out_shape=[
            jax.ShapeDtypeStruct((heads, seq, both), BF),
            jax.ShapeDtypeStruct((width, both), BF),
            jax.ShapeDtypeStruct((heads, 1, both), F32),
        ],
        input_output_aliases={4 + i: i for i in range(len(before))},
        compiler_params=pltpu.CompilerParams(vmem_limit_bytes=48 * 1024 * 1024),
        cost_estimate=cost(3 * steps),
    )


def backward_kernel(q_ref, k_ref, v_ref, p_ref, inv_ref, ctx_ref, dctx_ref, *refs, tile):
    dq_ref, dk_ref, dv_ref, held_ref = refs[-4:]
    count = p_ref.shape[0]
    size, seq = k_ref.shape[0] // count, k_ref.shape[1]
    group = held_ref.shape[1] // count
    for head in range(count):
        rows = slice(head * size, (head + 1) * size)
        queries = q_ref[rows, :]
        keys = k_ref[rows, :]
        values = v_ref[rows, :]
        grad = dctx_ref[rows, :].astype(F32) * inv_ref[head]
        inner = jnp.sum(grad * ctx_ref[rows, :].astype(F32), axis=0, keepdims=True)
        grad = grad.astype(BF)
        dk = jnp.zeros(keys.shape, F32)
        dv = jnp.zeros(keys.shape, F32)
        for t in range(seq // tile):
            both = None
            for stream in range(2):
                lo = stream * seq + t * tile
                at = slice(lo, lo + tile)
                weight = p_ref[head, :, at]
                part = dot(values, grad[:, at], TN) - inner[:, at]
                ds = weight.astype(F32) * part
                low = ds.astype(BF)
                dv += dot(grad[:, at], weight, NT)
                dk += dot(queries[:, at], low, NT)
                dq_ref[rows, at] = (dot(keys, low, NN) * 0.125).astype(BF)
                both = ds if both is None else both + ds
            held_ref[:, head * group : (head + 1) * group, t * tile : (t + 1) * tile] = (
                both.astype(BF).reshape(seq // group, group, tile)
            )
        dk_ref[rows, :] = (dk * 0.125).astype(BF)
        dv_ref[rows, :] = dv.astype(BF)


def attention_back(
    q_t, k_t, v_t, probs, inverse, ctx_t, dctx_t, before, heads, begin, steps, count=2, group=16, tile=512, after=()
):
    width, both = q_t.shape
    seq = k_t.shape[1]
    size = width // heads * count
    wide = pl.BlockSpec((size, both), lambda h: (h + begin, 0))
    thin = pl.BlockSpec((size, seq), lambda h: (h + begin, 0))
    operands = [q_t, k_t, v_t, probs, inverse, ctx_t, dctx_t, *before]
    return call(
        functools.partial(backward_kernel, tile=tile),
        after,
        operands,
        grid=(steps,),
        in_specs=[
            wide,
            thin,
            thin,
            pl.BlockSpec((count, seq, both), lambda h: (h + begin, 0, 0)),
            pl.BlockSpec((count, 1, both), lambda h: (h + begin, 0, 0)),
            wide,
            wide,
        ]
        + [pl.BlockSpec(memory_space=pl.ANY)] * len(before),
        out_specs=[
            wide,
            thin,
            thin,
            pl.BlockSpec((seq // group, count * group, seq), lambda h: (0, h + begin, 0)),
        ],
        out_shape=[
            pltpu.HBM((width, both), BF),
            pltpu.HBM((width, seq), BF),
            pltpu.HBM((width, seq), BF),
            pltpu.HBM((seq // group, heads * group, seq), BF),
        ],
        input_output_aliases={7 + i: i for i in range(len(before))},
        compiler_params=pltpu.CompilerParams(vmem_limit_bytes=56 * 1024 * 1024),
        cost_estimate=cost(1e4 * steps),
    )


def table_kernel(buckets_ref, *refs, buckets, group):
    held_ref, out_ref, total = refs
    step, steps = pl.program_id(0), pl.num_programs(0)
    parts = buckets_ref.shape[0] // group
    index = buckets_ref[...].astype(F32).astype(BF)
    hot = jnp.concatenate(
        [
            jnp.concatenate(
                [
                    jnp.where(index[p * group : (p + 1) * group] == jnp.asarray(n, BF), 1.0, 0.0).astype(BF)
                    for n in range(buckets)
                ],
                axis=0,
            )
            for p in range(parts)
        ],
        axis=1,
    )
    held = jnp.concatenate([held_ref[p] for p in range(parts)], axis=1)
    value = dot(hot, held, NT)

    @pl.when(step == 0)
    def _():
        total[...] = value

    @pl.when(step > 0)
    def _():
        total[...] += value

    @pl.when(step == steps - 1)
    def _():
        value = total[...]
        row = lax.broadcasted_iota(jnp.int32, value.shape, 0) % group
        col = lax.broadcasted_iota(jnp.int32, value.shape, 1) % group
        kept = jnp.where(row == col, value, 0.0)
        out_ref[...] = jnp.sum(kept.reshape(buckets, group, value.shape[1]), axis=1)


def table_back(buckets_t, held, buckets, group=16, parts=4, after=()):
    seq = buckets_t.shape[0]
    cols = held.shape[1]
    return call(
        functools.partial(table_kernel, buckets=buckets, group=group),
        after,
        [buckets_t, held],
        grid=(seq // (group * parts),),
        in_specs=[
            pl.BlockSpec((group * parts, seq), lambda g: (g, 0)),
            pl.BlockSpec((parts, cols, seq), lambda g: (g, 0, 0)),
        ],
        out_specs=whole((buckets, cols)),
        out_shape=jax.ShapeDtypeStruct((buckets, cols), F32),
        scratch_shapes=[pltpu.VMEM((buckets * group, cols), F32)],
        compiler_params=pltpu.CompilerParams(vmem_limit_bytes=40 * 1024 * 1024),
        cost_estimate=cost(6),
    )


def call(kernel, after, operands, *, in_specs, **settings):
    count = len(operands)

    def body(*refs):
        kernel(*refs[:count], *refs[count + len(after) :])

    operands = [
        pltpu.with_memory_space_constraint(o, pltpu.HBM) if s.memory_space is None and o.size > 1 << 16 else o
        for o, s in zip(operands, in_specs)
    ]
    anywhere = [pl.BlockSpec(memory_space=pl.ANY)] * len(after)
    return pl.pallas_call(body, in_specs=in_specs + anywhere, **settings)(*operands, *after)


def whole(shape):
    return pl.BlockSpec(shape, lambda *_: (0,) * len(shape))


def once(shape, at):
    return pl.BlockSpec(shape, lambda *_: at, pipeline_mode=pl.Buffered(1))


def unit(value):
    centred = value - jnp.mean(value, axis=-1, keepdims=True)
    inverse = lax.rsqrt(jnp.mean(centred * centred, axis=-1, keepdims=True) + EPSILON)
    return centred * inverse, inverse


def unit_back(grad, along, inverse):
    mean = jnp.mean(grad, axis=-1, keepdims=True)
    slope = jnp.mean(grad * along, axis=-1, keepdims=True)
    return (grad - mean - along * slope) * inverse


def column_sum(value):
    rows = value.shape[0]
    return jnp.sum(value.reshape(rows // 8, 8, value.shape[1]), axis=0)


def up_kernel(
    ctx_ref, x_ref, cot_ref, wo_ref, wi_ref, wd_ref, bi_ref, rows_ref,
    out_ref, lowt_ref, act_ref, slope_ref, unit_ref, inv_ref, dres_ref, dlow_ref, dlowt_ref, sums_ref,
    *, chunk, part_rows,
):
    halves, width, part = wo_ref.shape
    ffn = wi_ref.shape[2]
    row = lambda i: rows_ref[i : i + 1, :]
    parts = [slice(r, r + part_rows) for r in range(0, x_ref.shape[0], part_rows)]
    resids, lows = [], []
    for at in parts:
        resid = x_ref[at, :].astype(F32) + row(0)
        for y in range(halves):
            resid += dot(ctx_ref[y * part : (y + 1) * part, at].T, wo_ref[y], NT)
        along, inverse = unit(resid)
        unit_ref[at, :] = along
        inv_ref[at, :] = inverse
        normed = along * row(2) + row(4)
        low = normed.astype(BF)
        lowt_ref[:, at] = low.T
        resids.append(normed + row(1))
        lows.append(low)
    for y in range(halves):
        for n, at in enumerate(parts):
            for c in range(0, ffn, chunk):
                cols = slice(c, c + chunk)
                hidden = dot(lows[n], wi_ref[y, :, cols], NN) + bi_ref[y, :, cols]
                cdf = 0.5 * lax.erf(hidden * 0.7071067811865476) + 0.5
                density = jnp.exp(hidden * hidden * -0.5) * 0.3989422804014327
                act_ref[y, at, cols] = (hidden * cdf).astype(BF)
                slope_ref[y, at, cols] = (cdf + hidden * density).astype(BF)
            resids[n] += dot(act_ref[y, at, :], wd_ref[y], NT)
    sums = [0.0, 0.0, 0.0]
    for n, at in enumerate(parts):
        along, inverse = unit(resids[n])
        out_ref[at, :] = (along * row(3) + row(5)).astype(BF)
        cot = cot_ref[at, :].astype(F32)
        dres = unit_back(cot * row(3), along, inverse)
        dres_ref[at, :] = dres
        dlow = dres.astype(BF)
        dlow_ref[at, :] = dlow
        dlowt_ref[:, at] = dlow.T
        for i, value in enumerate((dres, cot * along, cot)):
            sums[i] += column_sum(value)
    for i in range(3):
        sums_ref[0, i] = sums[i]


def up(ctx_t, stacked, cot, heads_all, rest, hidden_bias, rows, part, tile=256, chunk=512, part_rows=256, after=()):
    tokens, width = stacked.shape
    halves = rest.shape[0]
    ffn = rest.shape[2] // 2
    tall = pl.BlockSpec((width, tile), lambda t: (0, t))
    flat = pl.BlockSpec((tile, width), lambda t: (t, 0))
    wide = pl.BlockSpec((halves, tile, ffn), lambda t: (0, t, 0))
    sds = pltpu.HBM
    return call(
        functools.partial(up_kernel, chunk=chunk, part_rows=part_rows),
        after,
        [ctx_t, stacked, cot, heads_all, rest, rest, hidden_bias, rows],
        grid=(tokens // tile,),
        in_specs=[
            tall,
            flat,
            flat,
            once((halves, width, part), (0, 0, 3)),
            once((halves, width, ffn), (0, 0, 0)),
            once((halves, width, ffn), (0, 0, 1)),
            whole((halves, 1, ffn)),
            whole(rows.shape),
        ],
        out_specs=[
            flat, tall, wide, wide, flat, pl.BlockSpec((tile, 1), lambda t: (t, 0)), flat, flat, tall,
            pl.BlockSpec((1, 3, 8, width), lambda t: (t, 0, 0, 0)),
        ],
        out_shape=[
            sds((tokens, width), BF),
            sds((width, tokens), BF),
            sds((halves, tokens, ffn), BF),
            sds((halves, tokens, ffn), BF),
            sds((tokens, width), F32),
            sds((tokens, 1), F32),
            sds((tokens, width), F32),
            sds((tokens, width), BF),
            sds((width, tokens), BF),
            sds((tokens // tile, 3, 8, width), F32),
        ],
        compiler_params=pltpu.CompilerParams(vmem_limit_bytes=58 * 1024 * 1024),
        cost_estimate=cost(20),
    )


def down_kernel(
    dlow_ref, dres_ref, slope_ref, unit_ref, inv_ref, wo_ref, wi_ref, wd_ref, rows_ref,
    dhid_ref, done_ref, dot_ref, dctx_ref, sums_ref, hsum_ref, *, chunk, part_rows,
):
    halves, width, part = wo_ref.shape
    ffn = wi_ref.shape[2]
    parts = [slice(r, r + part_rows) for r in range(0, dlow_ref.shape[0], part_rows)]
    dnorms = [dres_ref[at, :] for at in parts]
    for y in range(halves):
        for n, at in enumerate(parts):
            for c in range(0, ffn, chunk):
                cols = slice(c, c + chunk)
                dhid = dot(dlow_ref[at, :], wd_ref[y, :, cols], NN) * slope_ref[y, at, cols].astype(F32)
                hsum_ref[0, n, y, :, cols] = column_sum(dhid)
                dhid_ref[y, at, cols] = dhid.astype(BF)
            dnorms[n] += dot(dhid_ref[y, at, :], wi_ref[y], NT)
    sums = [0.0, 0.0, 0.0]
    for n, at in enumerate(parts):
        dnorm = dnorms[n]
        along = unit_ref[at, :]
        done = unit_back(dnorm * rows_ref[2:3, :], along, inv_ref[at, :])
        done_ref[at, :] = done
        low = done.astype(BF)
        dot_ref[:, at] = low.T
        for y in range(halves):
            dctx_ref[y * part : (y + 1) * part, at] = dot(low, wo_ref[y], NN).astype(BF).T
        for i, value in enumerate((done, dnorm * along, dnorm)):
            sums[i] += column_sum(value)
    for i in range(3):
        sums_ref[0, i] = sums[i]


def down(dlow, dres, slope, along, inverse, heads_all, rest, rows, part, tile=256, chunk=512, part_rows=256, after=()):
    tokens, width = dlow.shape
    halves = rest.shape[0]
    ffn = rest.shape[2] // 2
    tall = pl.BlockSpec((width, tile), lambda t: (0, t))
    flat = pl.BlockSpec((tile, width), lambda t: (t, 0))
    wide = pl.BlockSpec((halves, tile, ffn), lambda t: (0, t, 0))
    sds = pltpu.HBM
    return call(
        functools.partial(down_kernel, chunk=chunk, part_rows=part_rows),
        after,
        [dlow, dres, slope, along, inverse, heads_all, rest, rest, rows],
        grid=(tokens // tile,),
        in_specs=[
            flat,
            flat,
            wide,
            flat,
            pl.BlockSpec((tile, 1), lambda t: (t, 0)),
            once((halves, width, part), (0, 0, 3)),
            once((halves, width, ffn), (0, 0, 0)),
            once((halves, width, ffn), (0, 0, 1)),
            whole(rows.shape),
        ],
        out_specs=[
            wide, flat, tall, tall,
            pl.BlockSpec((1, 3, 8, width), lambda t: (t, 0, 0, 0)),
            pl.BlockSpec((1, tile // part_rows, halves, 8, ffn), lambda t: (t, 0, 0, 0, 0)),
        ],
        out_shape=[
            sds((halves, tokens, ffn), BF),
            sds((tokens, width), F32),
            sds((width, tokens), BF),
            sds((width, tokens), BF),
            sds((tokens // tile, 3, 8, width), F32),
            sds((tokens // tile, tile // part_rows, halves, 8, ffn), F32),
        ],
        compiler_params=pltpu.CompilerParams(vmem_limit_bytes=58 * 1024 * 1024),
        cost_estimate=cost(18),
    )


def put_rows(core, value, keep_ref, send_ref, at):
    chips, rows = keep_ref.shape[1], keep_ref.shape[2]
    value = value.reshape(chips, 2, rows, value.shape[1])

    @pl.when(core == 0)
    def _():
        keep_ref[at] = value[:, 0]
        send_ref[at] = value[:, 1]

    @pl.when(core != 0)
    def _():
        keep_ref[at] = value[:, 1]
        send_ref[at] = value[:, 0]


def outer_kernel(core_ref, left_ref, right_ref, keep_ref, send_ref):
    value = dot(left_ref[...], right_ref[0], NN).astype(BF)
    put_rows(core_ref[0], value, keep_ref, send_ref, 0)


def outer(core, left_t, right, rows, tile=768, after=()):
    width, tokens = left_t.shape
    halves, _, cols = right.shape
    block = pl.BlockSpec((1, width // (2 * rows), rows, tile), lambda y, c: (y, 0, 0, c))
    shape = jax.ShapeDtypeStruct((halves, width // (2 * rows), rows, cols), BF)
    return call(
        outer_kernel,
        after,
        [core, left_t, right],
        grid=(halves, cols // tile),
        in_specs=[
            pl.BlockSpec(memory_space=pltpu.SMEM),
            whole(left_t.shape),
            pl.BlockSpec((1, tokens, tile), lambda y, c: (y, 0, c)),
        ],
        out_specs=[block, block],
        out_shape=[shape, shape],
        cost_estimate=cost(5),
    )


def outer_in_kernel(low_ref, dhid_ref, dot_ref, ctx_ref, out_ref):
    owners, _, rows, _ = out_ref.shape
    ffn = dhid_ref.shape[2]
    half = ffn // 2
    for c in (0, half):
        value = dot(low_ref[...], dhid_ref[0, :, c : c + half], NN).astype(BF)
        out_ref[:, 0, :, c : c + half] = value.reshape(owners, rows, half)
    value = dot(dot_ref[...], ctx_ref[...], NT).astype(BF)
    out_ref[:, 0, :, ffn:] = value.reshape(owners, rows, value.shape[1])


def outer_in(low_t, dhid, do_t, ctx_t, rows, after=()):
    width, tokens = low_t.shape
    halves, _, ffn = dhid.shape
    part = ctx_t.shape[0] // halves
    owners = width // rows
    return call(
        outer_in_kernel,
        after,
        [low_t, dhid, do_t, ctx_t],
        grid=(halves,),
        in_specs=[
            whole(low_t.shape),
            pl.BlockSpec((1, tokens, ffn), lambda y: (y, 0, 0)),
            whole(do_t.shape),
            pl.BlockSpec((part, tokens), lambda y: (y, 0)),
        ],
        out_specs=pl.BlockSpec((owners, 1, rows, ffn + part), lambda y: (0, y, 0, 0)),
        out_shape=jax.ShapeDtypeStruct((owners, halves, rows, ffn + part), BF),
        compiler_params=pltpu.CompilerParams(vmem_limit_bytes=48 * 1024 * 1024),
        cost_estimate=cost(6),
    )


def project_kernel(core_ref, own_a, own_b, other_a, other_b, x_ref, bias_ref, q_ref, k_ref, v_ref, w_ref):
    core = core_ref[0]
    cut = own_a.shape[3]
    width = x_ref.shape[1]
    part, seq = k_ref.shape
    w_ref[0, :, core, :, :cut] = own_a[0]
    w_ref[0, :, core, :, cut:] = own_b[0]
    w_ref[0, :, 1 - core, :, :cut] = other_a[0]
    w_ref[0, :, 1 - core, :, cut:] = other_b[0]
    weights = w_ref[0, :, :, :, : 3 * part].reshape(width, 3 * part)
    q = dot(x_ref[...], weights[:, :part], NN) + bias_ref[0, 0:1, :]
    q_ref[...] = q.astype(BF).T
    kv = dot(x_ref[:seq, :], weights[:, part:], NN)
    k_ref[...] = kv[:, :part].astype(BF).T
    v_ref[...] = (kv[:, part:] + bias_ref[0, 1:2, :]).astype(BF).T


def project(core, pieces, stacked, bias, part, after=()):
    tokens, width = stacked.shape
    halves, chips, rows, cut = pieces[0].shape
    cols = cut + pieces[1].shape[3]
    seq = tokens // 2
    sds = pltpu.HBM
    one = pl.BlockSpec((1, chips, rows, cut), lambda y: (y, 0, 0, 0))
    two = pl.BlockSpec((1, chips, rows, cols - cut), lambda y: (y, 0, 0, 0))
    return call(
        project_kernel,
        after,
        [core, *pieces, stacked, bias],
        grid=(halves,),
        in_specs=[
            pl.BlockSpec(memory_space=pltpu.SMEM), one, two, one, two,
            whole(stacked.shape),
            pl.BlockSpec((1, 2, part), lambda y: (y, 0, 0)),
        ],
        out_specs=[
            pl.BlockSpec((part, tokens), lambda y: (y, 0)),
            pl.BlockSpec((part, seq), lambda y: (y, 0)),
            pl.BlockSpec((part, seq), lambda y: (y, 0)),
            pl.BlockSpec((1, chips, 2, rows, cols), lambda y: (y, 0, 0, 0, 0)),
        ],
        out_shape=[
            sds((width, tokens), BF),
            sds((width, seq), BF),
            sds((width, seq), BF),
            sds((halves, chips, 2, rows, cols), BF),
        ],
        compiler_params=pltpu.CompilerParams(vmem_limit_bytes=40 * 1024 * 1024),
        cost_estimate=cost(6),
    )


def project_back_kernel(core_ref, x_ref, dq_ref, dk_ref, dv_ref, ka_ref, sa_ref, kb_ref, sb_ref, xt_ref):
    core = core_ref[0]
    part = dq_ref.shape[0]
    cut = ka_ref.shape[3]

    @pl.when(pl.program_id(0) == 0)
    def _():
        xt_ref[...] = x_ref[...].T

    values = []
    for ref in (dq_ref, dk_ref, dv_ref):
        tokens = ref.shape[1]
        values.append(dot(xt_ref[:, :tokens], ref[...], NT).astype(BF))
    value = jnp.concatenate(values, axis=1)
    put_rows(core, value[:, :cut], ka_ref, sa_ref, 0)
    put_rows(core, value[:, cut:], kb_ref, sb_ref, 0)


def project_back(core, stacked, dq_t, dk_t, dv_t, halves, rows, cut, after=()):
    tokens, width = stacked.shape
    chips = width // (2 * rows)
    part = width // halves
    one = pl.BlockSpec((1, chips, rows, cut), lambda y: (y, 0, 0, 0))
    two = pl.BlockSpec((1, chips, rows, 3 * part - cut), lambda y: (y, 0, 0, 0))
    first = jax.ShapeDtypeStruct((halves, chips, rows, cut), BF)
    second = jax.ShapeDtypeStruct((halves, chips, rows, 3 * part - cut), BF)
    return call(
        project_back_kernel,
        after,
        [core, stacked, dq_t, dk_t, dv_t],
        grid=(halves,),
        in_specs=[pl.BlockSpec(memory_space=pltpu.SMEM), whole(stacked.shape)]
        + [pl.BlockSpec((part, g.shape[1]), lambda y: (y, 0)) for g in (dq_t, dk_t, dv_t)],
        out_specs=[one, one, two, two],
        out_shape=[first, first, second, second],
        scratch_shapes=[pltpu.VMEM((width, tokens), BF)],
        compiler_params=pltpu.CompilerParams(vmem_limit_bytes=40 * 1024 * 1024),
        cost_estimate=cost(5),
    )


def inputs_kernel(half_ref, w_ref, done_ref, dq_ref, dk_ref, dv_ref, keep_ref, send_ref, sum_ref):
    step, steps = pl.program_id(0), pl.num_programs(0)
    halves, width, cols = w_ref.shape
    part = cols // 3
    total = done_ref[...]
    for y in range(halves):
        total += dot(dq_ref[y * part : (y + 1) * part, :].T, w_ref[y, :, :part], NT)
    sum_ref[...] = total

    @pl.when(step < steps // 2)
    def _():
        extra = 0.0
        for y in range(halves):
            at = slice(y * part, (y + 1) * part)
            extra += dot(dk_ref[at, :].T, w_ref[y, :, part : 2 * part], NT)
            extra += dot(dv_ref[at, :].T, w_ref[y, :, 2 * part :], NT)
        sum_ref[...] += extra

    half = width // 2

    @pl.when(half_ref[0] == 0)
    def _():
        keep_ref[...] = sum_ref[:, :half].astype(BF)
        send_ref[...] = sum_ref[:, half:].astype(BF)

    @pl.when(half_ref[0] != 0)
    def _():
        keep_ref[...] = sum_ref[:, half:].astype(BF)
        send_ref[...] = sum_ref[:, :half].astype(BF)


def inputs_back(half, weights, done, dq_t, dk_t, dv_t, tile=256, after=()):
    tokens, width = done.shape
    last = tokens // (2 * tile) - 1
    thin = pl.BlockSpec((width, tile), lambda t: (0, jnp.minimum(t, last)))
    out = pl.BlockSpec((tile, width // 2), lambda t: (t, 0))
    return call(
        inputs_kernel,
        after,
        [half, weights, done, dq_t, dk_t, dv_t],
        grid=(tokens // tile,),
        in_specs=[
            pl.BlockSpec(memory_space=pltpu.SMEM),
            once((weights.shape[0], width, 3 * width // weights.shape[0]), (0, 0, 0)),
            pl.BlockSpec((tile, width), lambda t: (t, 0)),
            pl.BlockSpec((width, tile), lambda t: (0, t)),
            thin,
            thin,
        ],
        out_specs=[out, out],
        out_shape=[jax.ShapeDtypeStruct((tokens, width // 2), BF)] * 2,
        scratch_shapes=[pltpu.VMEM((tile, width), F32)],
        compiler_params=pltpu.CompilerParams(vmem_limit_bytes=40 * 1024 * 1024),
        cost_estimate=cost(5),
    )


def shifted(value, axis, step):
    size = lax.axis_size(axis)
    return lax.ppermute(value, axis, [(i, (i + step) % size) for i in range(size)])


def gather_start(value, axis):
    return [value] + [shifted(value, axis, k) for k in range(1, lax.axis_size(axis))]


def gather_finish(pieces, axis, where):
    size = len(pieces)
    me = lax.axis_index(axis)
    slots = []
    for j in range(size):
        which = lax.rem(me - j + size, size)
        chosen = pieces[0]
        for k in range(1, size):
            chosen = jnp.where(which == k, pieces[k], chosen)
        slots.append(chosen)
    return jnp.stack(slots, axis=where)


def total(parts):
    return sum(part.astype(F32) for part in parts)


def start(parts, axis, where):
    size = lax.axis_size(axis)
    me = lax.axis_index(axis)

    def at(index):
        return [lax.dynamic_index_in_dim(part, index, where, keepdims=False) for part in parts]

    out = [total(at(lax.rem(me + k, size))).astype(BF) for k in range(1, size)]
    return at(me), [shifted(part, axis, k) for k, part in enumerate(out, 1)], out


def start_joined(sums, axis):
    size = lax.axis_size(axis)
    me = lax.axis_index(axis)

    def at(index):
        values = [total([lax.dynamic_index_in_dim(p, index, 0, keepdims=False) for p in parts]) for parts in sums]
        return jnp.concatenate(values, axis=-1)

    return [at(me)] + [shifted(at(lax.rem(me + k, size)).astype(BF), axis, k) for k in range(1, size)]


def start_core(keep, send):
    halves, _, rows, cols = keep.shape
    shape = (halves, lax.axis_size("z"), lax.axis_size("x"), rows, cols)
    return [keep.reshape(shape)], [shifted(send, "core", 1).reshape(shape)]


def tie_sums(pending, *others):
    arrived, *others = tie([p[1] for p in pending], *others)
    return [p[0] + list(a) for p, a in zip(pending, arrived)], *others


def tie(*groups):
    return lax.optimization_barrier(groups)


def sum_pairs(value, axes):
    for axis in axes:
        size = lax.axis_size(axis)
        step = 1
        while step < size:
            value = value + lax.ppermute(value, axis, [(i, i ^ step) for i in range(size)])
            step *= 2
    return value


def shards(
    content_in,
    query_in,
    lengths,
    factor_order,
    buckets,
    w_qkv,
    b_qv,
    w_out,
    w_in,
    b_in,
    w_down,
    b_outs,
    norm_gain,
    norm_bias,
    rel_table,
    cot_content,
    cot_query,
):
    me = lax.axis_index("y")
    halves = lax.axis_size("y")
    each = content_in.shape[0] // halves
    assert each == 1
    seq = content_in.shape[1]
    width = content_in.shape[2]
    bucket_count, heads_here = rel_table.shape
    heads = heads_here * halves
    part = w_qkv.shape[2]
    ffn = w_in.shape[1]
    rows = w_in.shape[0]

    def mine(array):
        return lax.dynamic_index_in_dim(array, me, 0, keepdims=False)

    rest = lax.all_gather(
        jnp.concatenate([w_in, w_down.T], axis=1), ("y", "z", "x", "core"), axis=0
    ).reshape(halves, width, 2 * ffn)
    vectors = jnp.concatenate([b_qv, b_in.reshape(ffn // part, part)], axis=0)
    vectors = jnp.concatenate(
        [vectors, jnp.pad(rel_table, ((0, 0), (0, part - heads_here)))], axis=0
    )
    vectors = gather_finish(gather_start(vectors, "y"), "y", 0).astype(F32)
    qv_bias = vectors[:, :2]
    hidden_bias = vectors[:, 2 : 2 + ffn // part].reshape(halves, 1, ffn)
    table = vectors[:, 2 + ffn // part :, :heads_here]
    table = jnp.transpose(table, (0, 2, 1)).reshape(heads, bucket_count)
    table = jnp.pad(table, ((0, 0), (0, 128 - bucket_count)))
    vector_rows = jnp.concatenate([b_outs, norm_gain, norm_bias], axis=0).astype(F32)
    vector_rows = jnp.pad(vector_rows, ((0, 2), (0, 0)))

    core = lax.axis_index("core").astype(jnp.int32).reshape(1)
    content = mine(content_in)
    stacked = jnp.concatenate([content, mine(query_in)], axis=0)
    buckets_t = mine(buckets).T
    rank = mine(factor_order)
    length = lax.dynamic_slice_in_dim(lengths, me, 1, 0)
    bias = masked_bias(length, buckets_t, rank, table)

    shard = jnp.concatenate([*w_qkv, w_out.T], axis=1)
    wide = shard.shape[1] // 2
    cut = 5 * part // 3
    chips = width // (2 * rows)
    along_z = gather_finish(gather_start(shard, "z"), "z", 0)
    one = gather_start(along_z[:, :, :wide], "x")
    two = gather_start(along_z[:, :, wide:], "y")
    one, two, bias = tie(one, two, bias)
    one = gather_start(gather_finish(one, "x", 1), "y")
    two = gather_start(gather_finish(two, "y", 0), "x")
    one = gather_finish(one, "y", 0).reshape(halves, chips, rows, wide)
    two = gather_finish(two, "x", 2).reshape(halves, chips, rows, wide)
    pieces = (one, two, shifted(one, "core", 1), shifted(two, "core", 1))
    q_t, k_t, v_t, heads_all = project(core, pieces, stacked, qv_bias, part)
    heads_all = heads_all.reshape(halves, width, 2 * wide)
    probs, ctx_t, inverse = attention(q_t, k_t, v_t, bias, (), heads, 0, heads // 2)

    cot = jnp.concatenate([mine(cot_content), mine(cot_query)], axis=0)
    output, low_t, active, slope, unit_one, inv_one, d_two, d_two_low, d_two_low_t, sums_two = up(
        ctx_t, stacked, cot, heads_all, rest, hidden_bias, vector_rows, part
    )
    output_got = shifted(output, "y", 1)
    down_pending = start_core(*outer(core, d_two_low_t, active, rows))
    ((down_sum,),) = tie_sums([down_pending])
    down_pending = start(down_sum, "x", 2)
    below = down(
        d_two_low, d_two, slope, unit_one, inv_one, heads_all, rest, vector_rows, part,
        after=down_pending[2],
    )
    (down_sum,), output_got, below = tie_sums([down_pending], output_got, below)
    d_hidden, d_one, d_one_low_t, dctx_t, sums_one, sums_hidden = below
    down_pending = start(down_sum, "y", 0)
    in_grads = outer_in(low_t, d_hidden, d_one_low_t, ctx_t, rows, after=down_pending[2])
    in_sum = lax.psum_scatter(in_grads, ("z", "x", "core"), scatter_dimension=0)
    (down_sum,), in_grads = tie_sums([down_pending], in_grads)
    down_pending = start(down_sum, "z", 0)
    grads = attention_back(
        q_t, k_t, v_t, probs, inverse, ctx_t, dctx_t, (), heads, 0, heads // 2, after=down_pending[2]
    )
    (down_sum,), grads = tie_sums([down_pending], grads)
    down_share = total(down_sum)
    dq_t, dk_t, dv_t, held = grads
    pairs = project_back(core, stacked, dq_t, dk_t, dv_t, halves, rows, cut)
    pending = [start_core(*pairs[:2]), start_core(*pairs[2:])]
    half = me.astype(jnp.int32).reshape(1)
    grad_in = inputs_back(half, heads_all, d_one, dq_t, dk_t, dv_t, after=pairs)
    sums, grad_in = tie_sums(pending, grad_in)
    pending = [start(sums[0], "x", 2), start(sums[1], "y", 0)]
    table_grad = table_back(buckets_t, held, bucket_count, after=pending[0][2] + pending[1][2])
    sums, table_grad, grad_in = tie_sums(pending, table_grad, grad_in)
    pending = [start(sums[0], "y", 0), start(sums[1], "x", 1)]
    grad_kept, grad_sent = grad_in
    grad_got = shifted(grad_sent, "y", 1)

    table_grad = jnp.sum(table_grad.reshape(bucket_count, heads, -1), axis=2).T
    sums_one = jnp.sum(sums_one, axis=(0, 2))
    sums_two = jnp.sum(sums_two, axis=(0, 2))
    small = jnp.concatenate(
        [jnp.sum(g.astype(F32), axis=1) for g in (dq_t, dv_t)]
        + [table_grad.reshape(-1), jnp.sum(sums_hidden, axis=(0, 1, 3)).reshape(-1)]
        + [s[i] for i in range(3) for s in (sums_one, sums_two)]
    )
    small = sum_pairs(small.reshape(-1, 128), ("core", "x"))
    sums, small = tie_sums(pending, small)
    pending = start_joined(sums, "z")
    in_pending = start([in_sum], "y", 0)
    in_share = total(in_pending[0] + in_pending[1])
    small = sum_pairs(small, ("y", "z")).reshape(-1)
    first_kept = me == 0
    outs = jnp.stack(
        [jnp.where(first_kept, output, output_got), jnp.where(first_kept, output_got, output)]
    ).reshape(halves, 2, seq, width)
    grad_ins = jnp.stack(
        [jnp.where(first_kept, grad_kept, grad_got), jnp.where(first_kept, grad_got, grad_kept)]
    ).reshape(halves, 2, seq, width // halves)
    qkv_share = total(pending)
    ends = [2 * width, 2 * width + heads * bucket_count]
    ends.append(ends[1] + halves * ffn)
    grad_b_qv = mine(jnp.transpose(small[: ends[0]].reshape(2, halves, part), (1, 0, 2)))
    grad_table = mine(small[ends[0] : ends[1]].reshape(halves, heads_here, bucket_count)).T
    grad_b_in = mine(small[ends[1] : ends[2]].reshape(halves, ffn))
    pairs = small[ends[2] :].reshape(3, 2, width)
    return (
        outs[:, 0],
        outs[:, 1],
        grad_ins[:, 0],
        grad_ins[:, 1],
        jnp.transpose(qkv_share.reshape(rows, 3, part), (1, 0, 2)),
        grad_b_qv,
        in_share[:, ffn:].T,
        in_share[:, :ffn],
        grad_b_in,
        down_share.T,
        pairs[0],
        pairs[1],
        pairs[2],
        grad_table,
    )


def solution(mesh):
    count = mesh.shape["dp"] // 2
    depth = 4 if count % 4 == 0 else 1
    while count // depth > depth:
        depth *= 2
    grid = mesh.devices.reshape(depth, count // depth, 2, mesh.shape["tensor"])
    fine = Mesh(grid, ("z", "x", "core", "y"))
    dp = ("z", "x", "core")
    return jax.shard_map(
        shards,
        mesh=fine,
        in_specs=(
            P(dp, None, None),
            P(dp, None, None),
            P(dp),
            P(dp, None),
            P(dp, None, None),
            P(None, dp, "y"),
            P(None, "y"),
            P("y", dp),
            P(dp, "y"),
            P("y"),
            P("y", dp),
            P(),
            P(),
            P(),
            P(None, "y"),
            P(dp, None, None),
            P(dp, None, None),
        ),
        out_specs=(
            P(dp, None, None),
            P(dp, None, None),
            P(dp, None, "y"),
            P(dp, None, "y"),
            P(None, dp, "y"),
            P(None, "y"),
            P("y", dp),
            P(dp, "y"),
            P("y"),
            P("y", dp),
            P(),
            P(),
            P(),
            P(None, "y"),
        ),
        check_vma=False,
    )
```

```python
import functools

import jax
import jax.numpy as jnp
from jax import lax
from jax.experimental import pallas as pl
from jax.experimental.pallas import tpu as pltpu
from jax.sharding import Mesh, PartitionSpec as P

EPSILON = 1e-05


def cost(us):
    return pl.CostEstimate(flops=int(us * 1e7), bytes_accessed=int(us * 1e4), transcendentals=0)

NEG = -1e30
BF = jnp.bfloat16
F32 = jnp.float32


def dot(a, b, dims):
    return lax.dot_general(a, b, (dims, ((), ())), preferred_element_type=F32)


NN = ((1,), (0,))
NT = ((1,), (1,))
TN = ((0,), (0,))


def bias_kernel(len_ref, buckets_ref, rank_row_ref, rank_col_ref, table_ref, out_ref):
    rows, cols = buckets_ref.shape
    heads = table_ref.shape[0]
    start = pl.program_id(0) * rows
    key = start + lax.broadcasted_iota(jnp.int32, (rows, cols), 0)
    query = lax.broadcasted_iota(jnp.int32, (rows, cols), 1)
    valid = key < len_ref[0]
    rank_key = rank_col_ref[...]
    rank_query = rank_row_ref[...]
    content = (valid & (rank_key <= rank_query)) | (key == query)
    stream = (valid & (rank_key < rank_query)) | (key == 0)
    index = buckets_ref[...]
    for head in range(heads):
        row = jnp.broadcast_to(table_ref[head : head + 1, :], (rows, 128))
        bias = jnp.concatenate(
            [
                jnp.take_along_axis(
                    row, index[:, c : c + 128], axis=1, mode="promise_in_bounds"
                )
                for c in range(0, cols, 128)
            ],
            axis=1,
        )
        out_ref[head, :, :cols] = jnp.where(content, bias, NEG).astype(BF)
        out_ref[head, :, cols:] = jnp.where(stream, bias, NEG).astype(BF)


def masked_bias(length, buckets_t, rank, table, after=()):
    seq = buckets_t.shape[0]
    heads = table.shape[0]
    step = 128
    return call(
        bias_kernel,
        after,
        [length, buckets_t, rank.reshape(1, seq), rank.reshape(seq, 1), table],
        grid=(seq // step,),
        in_specs=[
            pl.BlockSpec(memory_space=pltpu.SMEM),
            pl.BlockSpec((step, seq), lambda g: (g, 0)),
            pl.BlockSpec((1, seq), lambda g: (0, 0)),
            pl.BlockSpec((step, 1), lambda g: (g, 0)),
            pl.BlockSpec((heads, 128), lambda g: (0, 0)),
        ],
        out_specs=pl.BlockSpec((heads, step, 2 * seq), lambda g: (0, g, 0)),
        out_shape=jax.ShapeDtypeStruct((heads, seq, 2 * seq), BF),
        cost_estimate=cost(9),
    )


def forward_kernel(q_ref, k_ref, v_ref, bias_ref, probs_ref, ctx_ref, inv_ref, *, tile):
    count = bias_ref.shape[0]
    size = q_ref.shape[0] // count
    for head in range(count):
        rows = slice(head * size, (head + 1) * size)
        keys = (k_ref[rows, :].astype(F32) * 0.125).astype(BF)
        for t in range(q_ref.shape[1] // tile):
            at = slice(t * tile, (t + 1) * tile)
            scores = dot(keys, q_ref[rows, at], TN) + bias_ref[head, :, at].astype(F32)
            high = jnp.max(scores, axis=0, keepdims=True)
            weight = jnp.exp(scores - high)
            inverse = 1.0 / jnp.sum(weight, axis=0, keepdims=True)
            low = weight.astype(BF)
            probs_ref[head, :, at] = low
            ctx_ref[rows, at] = (dot(v_ref[rows, :], low, NN) * inverse).astype(BF)
            inv_ref[head, :, at] = inverse


def attention(q_t, k_t, v_t, bias, before, heads, begin, steps, tile=1024, count=2, after=()):
    width, both = q_t.shape
    seq = k_t.shape[1]
    size = width // heads * count
    thin = pl.BlockSpec((size, seq), lambda h: (h + begin, 0))
    wide = pl.BlockSpec((size, both), lambda h: (h + begin, 0))
    square = pl.BlockSpec((count, seq, both), lambda h: (h + begin, 0, 0))

    def kernel(q_ref, k_ref, v_ref, bias_ref, *refs):
        forward_kernel(q_ref, k_ref, v_ref, bias_ref, *refs[-3:], tile=tile)

    return call(
        kernel,
        after,
        [q_t, k_t, v_t, bias, *before],
        grid=(steps,),
        in_specs=[wide, thin, thin, square] + [pl.BlockSpec(memory_space=pl.ANY)] * len(before),
        out_specs=[square, wide, pl.BlockSpec((count, 1, both), lambda h: (h + begin, 0, 0))],
        out_shape=[
            jax.ShapeDtypeStruct((heads, seq, both), BF),
            jax.ShapeDtypeStruct((width, both), BF),
            jax.ShapeDtypeStruct((heads, 1, both), F32),
        ],
        input_output_aliases={4 + i: i for i in range(len(before))},
        compiler_params=pltpu.CompilerParams(vmem_limit_bytes=48 * 1024 * 1024),
        cost_estimate=cost(3 * steps),
    )


def backward_kernel(q_ref, k_ref, v_ref, p_ref, inv_ref, ctx_ref, dctx_ref, *refs, tile):
    dq_ref, dk_ref, dv_ref, held_ref = refs[-4:]
    count = p_ref.shape[0]
    size, seq = k_ref.shape[0] // count, k_ref.shape[1]
    group = held_ref.shape[1] // count
    for head in range(count):
        rows = slice(head * size, (head + 1) * size)
        queries = q_ref[rows, :]
        keys = k_ref[rows, :]
        values = v_ref[rows, :]
        grad = dctx_ref[rows, :].astype(F32) * inv_ref[head]
        inner = jnp.sum(grad * ctx_ref[rows, :].astype(F32), axis=0, keepdims=True)
        grad = grad.astype(BF)
        dk = jnp.zeros(keys.shape, F32)
        dv = jnp.zeros(keys.shape, F32)
        for t in range(seq // tile):
            both = None
            for stream in range(2):
                lo = stream * seq + t * tile
                at = slice(lo, lo + tile)
                weight = p_ref[head, :, at]
                part = dot(values, grad[:, at], TN) - inner[:, at]
                ds = weight.astype(F32) * part
                low = ds.astype(BF)
                dv += dot(grad[:, at], weight, NT)
                dk += dot(queries[:, at], low, NT)
                dq_ref[rows, at] = (dot(keys, low, NN) * 0.125).astype(BF)
                both = ds if both is None else both + ds
            held_ref[:, head * group : (head + 1) * group, t * tile : (t + 1) * tile] = (
                both.astype(BF).reshape(seq // group, group, tile)
            )
        dk_ref[rows, :] = (dk * 0.125).astype(BF)
        dv_ref[rows, :] = dv.astype(BF)


def attention_back(
    q_t, k_t, v_t, probs, inverse, ctx_t, dctx_t, before, heads, begin, steps, count=2, group=16, tile=512, after=()
):
    width, both = q_t.shape
    seq = k_t.shape[1]
    size = width // heads * count
    wide = pl.BlockSpec((size, both), lambda h: (h + begin, 0))
    thin = pl.BlockSpec((size, seq), lambda h: (h + begin, 0))
    operands = [q_t, k_t, v_t, probs, inverse, ctx_t, dctx_t, *before]
    return call(
        functools.partial(backward_kernel, tile=tile),
        after,
        operands,
        grid=(steps,),
        in_specs=[
            wide,
            thin,
            thin,
            pl.BlockSpec((count, seq, both), lambda h: (h + begin, 0, 0)),
            pl.BlockSpec((count, 1, both), lambda h: (h + begin, 0, 0)),
            wide,
            wide,
        ]
        + [pl.BlockSpec(memory_space=pl.ANY)] * len(before),
        out_specs=[
            wide,
            thin,
            thin,
            pl.BlockSpec((seq // group, count * group, seq), lambda h: (0, h + begin, 0)),
        ],
        out_shape=[
            pltpu.HBM((width, both), BF),
            pltpu.HBM((width, seq), BF),
            pltpu.HBM((width, seq), BF),
            pltpu.HBM((seq // group, heads * group, seq), BF),
        ],
        input_output_aliases={7 + i: i for i in range(len(before))},
        compiler_params=pltpu.CompilerParams(vmem_limit_bytes=56 * 1024 * 1024),
        cost_estimate=cost(1e4 * steps),
    )


def table_kernel(buckets_ref, *refs, buckets, group):
    held_ref, out_ref, total = refs
    step, steps = pl.program_id(0), pl.num_programs(0)
    parts = buckets_ref.shape[0] // group
    index = buckets_ref[...].astype(F32).astype(BF)
    hot = jnp.concatenate(
        [
            jnp.concatenate(
                [
                    jnp.where(index[p * group : (p + 1) * group] == jnp.asarray(n, BF), 1.0, 0.0).astype(BF)
                    for n in range(buckets)
                ],
                axis=0,
            )
            for p in range(parts)
        ],
        axis=1,
    )
    held = jnp.concatenate([held_ref[p] for p in range(parts)], axis=1)
    value = dot(hot, held, NT)

    @pl.when(step == 0)
    def _():
        total[...] = value

    @pl.when(step > 0)
    def _():
        total[...] += value

    @pl.when(step == steps - 1)
    def _():
        value = total[...]
        row = lax.broadcasted_iota(jnp.int32, value.shape, 0) % group
        col = lax.broadcasted_iota(jnp.int32, value.shape, 1) % group
        kept = jnp.where(row == col, value, 0.0)
        out_ref[...] = jnp.sum(kept.reshape(buckets, group, value.shape[1]), axis=1)


def table_back(buckets_t, held, buckets, group=16, parts=4, after=()):
    seq = buckets_t.shape[0]
    cols = held.shape[1]
    return call(
        functools.partial(table_kernel, buckets=buckets, group=group),
        after,
        [buckets_t, held],
        grid=(seq // (group * parts),),
        in_specs=[
            pl.BlockSpec((group * parts, seq), lambda g: (g, 0)),
            pl.BlockSpec((parts, cols, seq), lambda g: (g, 0, 0)),
        ],
        out_specs=whole((buckets, cols)),
        out_shape=jax.ShapeDtypeStruct((buckets, cols), F32),
        scratch_shapes=[pltpu.VMEM((buckets * group, cols), F32)],
        compiler_params=pltpu.CompilerParams(vmem_limit_bytes=40 * 1024 * 1024),
        cost_estimate=cost(6),
    )


def call(kernel, after, operands, *, in_specs, **settings):
    count = len(operands)

    def body(*refs):
        kernel(*refs[:count], *refs[count + len(after) :])

    operands = [
        pltpu.with_memory_space_constraint(o, pltpu.HBM) if s.memory_space is None and o.size > 1 << 16 else o
        for o, s in zip(operands, in_specs)
    ]
    anywhere = [pl.BlockSpec(memory_space=pl.ANY)] * len(after)
    return pl.pallas_call(body, in_specs=in_specs + anywhere, **settings)(*operands, *after)


def whole(shape):
    return pl.BlockSpec(shape, lambda *_: (0,) * len(shape))


def once(shape, at):
    return pl.BlockSpec(shape, lambda *_: at, pipeline_mode=pl.Buffered(1))


def unit(value):
    centred = value - jnp.mean(value, axis=-1, keepdims=True)
    inverse = lax.rsqrt(jnp.mean(centred * centred, axis=-1, keepdims=True) + EPSILON)
    return centred * inverse, inverse


def unit_back(grad, along, inverse):
    mean = jnp.mean(grad, axis=-1, keepdims=True)
    slope = jnp.mean(grad * along, axis=-1, keepdims=True)
    return (grad - mean - along * slope) * inverse


def column_sum(value):
    rows = value.shape[0]
    return jnp.sum(value.reshape(rows // 8, 8, value.shape[1]), axis=0)


def up_kernel(
    ctx_ref, x_ref, cot_ref, wo_ref, wi_ref, wd_ref, bi_ref, rows_ref,
    out_ref, lowt_ref, act_ref, slope_ref, unit_ref, inv_ref, dres_ref, dlow_ref, dlowt_ref, sums_ref,
    *, chunk, part_rows,
):
    halves, width, part = wo_ref.shape
    ffn = wi_ref.shape[2]
    row = lambda i: rows_ref[i : i + 1, :]
    parts = [slice(r, r + part_rows) for r in range(0, x_ref.shape[0], part_rows)]
    resids, lows = [], []
    for at in parts:
        resid = x_ref[at, :].astype(F32) + row(0)
        for y in range(halves):
            resid += dot(ctx_ref[y * part : (y + 1) * part, at].T, wo_ref[y], NT)
        along, inverse = unit(resid)
        unit_ref[at, :] = along
        inv_ref[at, :] = inverse
        normed = along * row(2) + row(4)
        low = normed.astype(BF)
        lowt_ref[:, at] = low.T
        resids.append(normed + row(1))
        lows.append(low)
    for y in range(halves):
        for n, at in enumerate(parts):
            for c in range(0, ffn, chunk):
                cols = slice(c, c + chunk)
                hidden = dot(lows[n], wi_ref[y, :, cols], NN) + bi_ref[y, :, cols]
                cdf = 0.5 * lax.erf(hidden * 0.7071067811865476) + 0.5
                density = jnp.exp(hidden * hidden * -0.5) * 0.3989422804014327
                act_ref[y, at, cols] = (hidden * cdf).astype(BF)
                slope_ref[y, at, cols] = (cdf + hidden * density).astype(BF)
            resids[n] += dot(act_ref[y, at, :], wd_ref[y], NT)
    sums = [0.0, 0.0, 0.0]
    for n, at in enumerate(parts):
        along, inverse = unit(resids[n])
        out_ref[at, :] = (along * row(3) + row(5)).astype(BF)
        cot = cot_ref[at, :].astype(F32)
        dres = unit_back(cot * row(3), along, inverse)
        dres_ref[at, :] = dres
        dlow = dres.astype(BF)
        dlow_ref[at, :] = dlow
        dlowt_ref[:, at] = dlow.T
        for i, value in enumerate((dres, cot * along, cot)):
            sums[i] += column_sum(value)
    for i in range(3):
        sums_ref[0, i] = sums[i]


def up(ctx_t, stacked, cot, heads_all, rest, hidden_bias, rows, part, tile=256, chunk=512, part_rows=256, after=()):
    tokens, width = stacked.shape
    halves = rest.shape[0]
    ffn = rest.shape[2] // 2
    tall = pl.BlockSpec((width, tile), lambda t: (0, t))
    flat = pl.BlockSpec((tile, width), lambda t: (t, 0))
    wide = pl.BlockSpec((halves, tile, ffn), lambda t: (0, t, 0))
    sds = pltpu.HBM
    return call(
        functools.partial(up_kernel, chunk=chunk, part_rows=part_rows),
        after,
        [ctx_t, stacked, cot, heads_all, rest, rest, hidden_bias, rows],
        grid=(tokens // tile,),
        in_specs=[
            tall,
            flat,
            flat,
            once((halves, width, part), (0, 0, 3)),
            once((halves, width, ffn), (0, 0, 0)),
            once((halves, width, ffn), (0, 0, 1)),
            whole((halves, 1, ffn)),
            whole(rows.shape),
        ],
        out_specs=[
            flat, tall, wide, wide, flat, pl.BlockSpec((tile, 1), lambda t: (t, 0)), flat, flat, tall,
            pl.BlockSpec((1, 3, 8, width), lambda t: (t, 0, 0, 0)),
        ],
        out_shape=[
            sds((tokens, width), BF),
            sds((width, tokens), BF),
            sds((halves, tokens, ffn), BF),
            sds((halves, tokens, ffn), BF),
            sds((tokens, width), F32),
            sds((tokens, 1), F32),
            sds((tokens, width), F32),
            sds((tokens, width), BF),
            sds((width, tokens), BF),
            sds((tokens // tile, 3, 8, width), F32),
        ],
        compiler_params=pltpu.CompilerParams(vmem_limit_bytes=58 * 1024 * 1024),
        cost_estimate=cost(20),
    )


def down_kernel(
    dlow_ref, dres_ref, slope_ref, unit_ref, inv_ref, wo_ref, wi_ref, wd_ref, rows_ref,
    dhid_ref, done_ref, dot_ref, dctx_ref, sums_ref, hsum_ref, *, chunk, part_rows,
):
    halves, width, part = wo_ref.shape
    ffn = wi_ref.shape[2]
    parts = [slice(r, r + part_rows) for r in range(0, dlow_ref.shape[0], part_rows)]
    dnorms = [dres_ref[at, :] for at in parts]
    for y in range(halves):
        for n, at in enumerate(parts):
            for c in range(0, ffn, chunk):
                cols = slice(c, c + chunk)
                dhid = dot(dlow_ref[at, :], wd_ref[y, :, cols], NN) * slope_ref[y, at, cols].astype(F32)
                hsum_ref[0, n, y, :, cols] = column_sum(dhid)
                dhid_ref[y, at, cols] = dhid.astype(BF)
            dnorms[n] += dot(dhid_ref[y, at, :], wi_ref[y], NT)
    sums = [0.0, 0.0, 0.0]
    for n, at in enumerate(parts):
        dnorm = dnorms[n]
        along = unit_ref[at, :]
        done = unit_back(dnorm * rows_ref[2:3, :], along, inv_ref[at, :])
        done_ref[at, :] = done
        low = done.astype(BF)
        dot_ref[:, at] = low.T
        for y in range(halves):
            dctx_ref[y * part : (y + 1) * part, at] = dot(low, wo_ref[y], NN).astype(BF).T
        for i, value in enumerate((done, dnorm * along, dnorm)):
            sums[i] += column_sum(value)
    for i in range(3):
        sums_ref[0, i] = sums[i]


def down(dlow, dres, slope, along, inverse, heads_all, rest, rows, part, tile=256, chunk=512, part_rows=256, after=()):
    tokens, width = dlow.shape
    halves = rest.shape[0]
    ffn = rest.shape[2] // 2
    tall = pl.BlockSpec((width, tile), lambda t: (0, t))
    flat = pl.BlockSpec((tile, width), lambda t: (t, 0))
    wide = pl.BlockSpec((halves, tile, ffn), lambda t: (0, t, 0))
    sds = pltpu.HBM
    return call(
        functools.partial(down_kernel, chunk=chunk, part_rows=part_rows),
        after,
        [dlow, dres, slope, along, inverse, heads_all, rest, rest, rows],
        grid=(tokens // tile,),
        in_specs=[
            flat,
            flat,
            wide,
            flat,
            pl.BlockSpec((tile, 1), lambda t: (t, 0)),
            once((halves, width, part), (0, 0, 3)),
            once((halves, width, ffn), (0, 0, 0)),
            once((halves, width, ffn), (0, 0, 1)),
            whole(rows.shape),
        ],
        out_specs=[
            wide, flat, tall, tall,
            pl.BlockSpec((1, 3, 8, width), lambda t: (t, 0, 0, 0)),
            pl.BlockSpec((1, tile // part_rows, halves, 8, ffn), lambda t: (t, 0, 0, 0, 0)),
        ],
        out_shape=[
            sds((halves, tokens, ffn), BF),
            sds((tokens, width), F32),
            sds((width, tokens), BF),
            sds((width, tokens), BF),
            sds((tokens // tile, 3, 8, width), F32),
            sds((tokens // tile, tile // part_rows, halves, 8, ffn), F32),
        ],
        compiler_params=pltpu.CompilerParams(vmem_limit_bytes=58 * 1024 * 1024),
        cost_estimate=cost(18),
    )


def put_rows(core, value, keep_ref, send_ref, at):
    chips, rows = keep_ref.shape[1], keep_ref.shape[2]
    value = value.reshape(chips, 2, rows, value.shape[1])

    @pl.when(core == 0)
    def _():
        keep_ref[at] = value[:, 0]
        send_ref[at] = value[:, 1]

    @pl.when(core != 0)
    def _():
        keep_ref[at] = value[:, 1]
        send_ref[at] = value[:, 0]


def outer_kernel(core_ref, left_ref, right_ref, keep_ref, send_ref):
    value = dot(left_ref[...], right_ref[0], NN).astype(BF)
    put_rows(core_ref[0], value, keep_ref, send_ref, 0)


def outer(core, left_t, right, rows, tile=768, after=()):
    width, tokens = left_t.shape
    halves, _, cols = right.shape
    block = pl.BlockSpec((1, width // (2 * rows), rows, tile), lambda y, c: (y, 0, 0, c))
    shape = jax.ShapeDtypeStruct((halves, width // (2 * rows), rows, cols), BF)
    return call(
        outer_kernel,
        after,
        [core, left_t, right],
        grid=(halves, cols // tile),
        in_specs=[
            pl.BlockSpec(memory_space=pltpu.SMEM),
            whole(left_t.shape),
            pl.BlockSpec((1, tokens, tile), lambda y, c: (y, 0, c)),
        ],
        out_specs=[block, block],
        out_shape=[shape, shape],
        cost_estimate=cost(5),
    )


def outer_in_kernel(low_ref, dhid_ref, dot_ref, ctx_ref, out_ref):
    owners, _, rows, _ = out_ref.shape
    ffn = dhid_ref.shape[2]
    half = ffn // 2
    for c in (0, half):
        value = dot(low_ref[...], dhid_ref[0, :, c : c + half], NN).astype(BF)
        out_ref[:, 0, :, c : c + half] = value.reshape(owners, rows, half)
    value = dot(dot_ref[...], ctx_ref[...], NT).astype(BF)
    out_ref[:, 0, :, ffn:] = value.reshape(owners, rows, value.shape[1])


def outer_in(low_t, dhid, do_t, ctx_t, rows, after=()):
    width, tokens = low_t.shape
    halves, _, ffn = dhid.shape
    part = ctx_t.shape[0] // halves
    owners = width // rows
    return call(
        outer_in_kernel,
        after,
        [low_t, dhid, do_t, ctx_t],
        grid=(halves,),
        in_specs=[
            whole(low_t.shape),
            pl.BlockSpec((1, tokens, ffn), lambda y: (y, 0, 0)),
            whole(do_t.shape),
            pl.BlockSpec((part, tokens), lambda y: (y, 0)),
        ],
        out_specs=pl.BlockSpec((owners, 1, rows, ffn + part), lambda y: (0, y, 0, 0)),
        out_shape=jax.ShapeDtypeStruct((owners, halves, rows, ffn + part), BF),
        compiler_params=pltpu.CompilerParams(vmem_limit_bytes=48 * 1024 * 1024),
        cost_estimate=cost(6),
    )


def project_kernel(core_ref, own_a, own_b, other_a, other_b, x_ref, bias_ref, q_ref, k_ref, v_ref, w_ref):
    core = core_ref[0]
    cut = own_a.shape[3]
    width = x_ref.shape[1]
    part, seq = k_ref.shape
    w_ref[0, :, core, :, :cut] = own_a[0]
    w_ref[0, :, core, :, cut:] = own_b[0]
    w_ref[0, :, 1 - core, :, :cut] = other_a[0]
    w_ref[0, :, 1 - core, :, cut:] = other_b[0]
    weights = w_ref[0, :, :, :, : 3 * part].reshape(width, 3 * part)
    q = dot(x_ref[...], weights[:, :part], NN) + bias_ref[0, 0:1, :]
    q_ref[...] = q.astype(BF).T
    kv = dot(x_ref[:seq, :], weights[:, part:], NN)
    k_ref[...] = kv[:, :part].astype(BF).T
    v_ref[...] = (kv[:, part:] + bias_ref[0, 1:2, :]).astype(BF).T


def project(core, pieces, stacked, bias, part, after=()):
    tokens, width = stacked.shape
    halves, chips, rows, cut = pieces[0].shape
    cols = cut + pieces[1].shape[3]
    seq = tokens // 2
    sds = pltpu.HBM
    one = pl.BlockSpec((1, chips, rows, cut), lambda y: (y, 0, 0, 0))
    two = pl.BlockSpec((1, chips, rows, cols - cut), lambda y: (y, 0, 0, 0))
    return call(
        project_kernel,
        after,
        [core, *pieces, stacked, bias],
        grid=(halves,),
        in_specs=[
            pl.BlockSpec(memory_space=pltpu.SMEM), one, two, one, two,
            whole(stacked.shape),
            pl.BlockSpec((1, 2, part), lambda y: (y, 0, 0)),
        ],
        out_specs=[
            pl.BlockSpec((part, tokens), lambda y: (y, 0)),
            pl.BlockSpec((part, seq), lambda y: (y, 0)),
            pl.BlockSpec((part, seq), lambda y: (y, 0)),
            pl.BlockSpec((1, chips, 2, rows, cols), lambda y: (y, 0, 0, 0, 0)),
        ],
        out_shape=[
            sds((width, tokens), BF),
            sds((width, seq), BF),
            sds((width, seq), BF),
            sds((halves, chips, 2, rows, cols), BF),
        ],
        compiler_params=pltpu.CompilerParams(vmem_limit_bytes=40 * 1024 * 1024),
        cost_estimate=cost(6),
    )


def project_back_kernel(core_ref, x_ref, dq_ref, dk_ref, dv_ref, keep_ref, send_ref, xt_ref):
    @pl.when(pl.program_id(0) == 0)
    def _():
        xt_ref[...] = x_ref[...].T

    values = []
    for ref in (dq_ref, dk_ref, dv_ref):
        tokens = ref.shape[1]
        values.append(dot(xt_ref[:, :tokens], ref[...], NT).astype(BF))
    put_rows(core_ref[0], jnp.concatenate(values, axis=1), keep_ref, send_ref, 0)


def project_back(core, stacked, dq_t, dk_t, dv_t, halves, rows, after=()):
    tokens, width = stacked.shape
    chips = width // (2 * rows)
    part = width // halves
    block = pl.BlockSpec((1, chips, rows, 3 * part), lambda y: (y, 0, 0, 0))
    shape = jax.ShapeDtypeStruct((halves, chips, rows, 3 * part), BF)
    return call(
        project_back_kernel,
        after,
        [core, stacked, dq_t, dk_t, dv_t],
        grid=(halves,),
        in_specs=[pl.BlockSpec(memory_space=pltpu.SMEM), whole(stacked.shape)]
        + [pl.BlockSpec((part, g.shape[1]), lambda y: (y, 0)) for g in (dq_t, dk_t, dv_t)],
        out_specs=[block, block],
        out_shape=[shape, shape],
        scratch_shapes=[pltpu.VMEM((width, tokens), BF)],
        compiler_params=pltpu.CompilerParams(vmem_limit_bytes=40 * 1024 * 1024),
        cost_estimate=cost(5),
    )


def inputs_kernel(half_ref, w_ref, done_ref, dq_ref, dk_ref, dv_ref, keep_ref, send_ref, sum_ref):
    step, steps = pl.program_id(0), pl.num_programs(0)
    halves, width, cols = w_ref.shape
    part = cols // 3
    total = done_ref[...]
    for y in range(halves):
        total += dot(dq_ref[y * part : (y + 1) * part, :].T, w_ref[y, :, :part], NT)
    sum_ref[...] = total

    @pl.when(step < steps // 2)
    def _():
        extra = 0.0
        for y in range(halves):
            at = slice(y * part, (y + 1) * part)
            extra += dot(dk_ref[at, :].T, w_ref[y, :, part : 2 * part], NT)
            extra += dot(dv_ref[at, :].T, w_ref[y, :, 2 * part :], NT)
        sum_ref[...] += extra

    half = width // 2

    @pl.when(half_ref[0] == 0)
    def _():
        keep_ref[...] = sum_ref[:, :half].astype(BF)
        send_ref[...] = sum_ref[:, half:].astype(BF)

    @pl.when(half_ref[0] != 0)
    def _():
        keep_ref[...] = sum_ref[:, half:].astype(BF)
        send_ref[...] = sum_ref[:, :half].astype(BF)


def inputs_back(half, weights, done, dq_t, dk_t, dv_t, tile=256, after=()):
    tokens, width = done.shape
    last = tokens // (2 * tile) - 1
    thin = pl.BlockSpec((width, tile), lambda t: (0, jnp.minimum(t, last)))
    out = pl.BlockSpec((tile, width // 2), lambda t: (t, 0))
    return call(
        inputs_kernel,
        after,
        [half, weights, done, dq_t, dk_t, dv_t],
        grid=(tokens // tile,),
        in_specs=[
            pl.BlockSpec(memory_space=pltpu.SMEM),
            once((weights.shape[0], width, 3 * width // weights.shape[0]), (0, 0, 0)),
            pl.BlockSpec((tile, width), lambda t: (t, 0)),
            pl.BlockSpec((width, tile), lambda t: (0, t)),
            thin,
            thin,
        ],
        out_specs=[out, out],
        out_shape=[jax.ShapeDtypeStruct((tokens, width // 2), BF)] * 2,
        scratch_shapes=[pltpu.VMEM((tile, width), F32)],
        compiler_params=pltpu.CompilerParams(vmem_limit_bytes=40 * 1024 * 1024),
        cost_estimate=cost(5),
    )


def shifted(value, axis, step):
    size = lax.axis_size(axis)
    return lax.ppermute(value, axis, [(i, (i + step) % size) for i in range(size)])


def gather_start(value, axis):
    return [value] + [shifted(value, axis, k) for k in range(1, lax.axis_size(axis))]


def gather_finish(pieces, axis, where):
    size = len(pieces)
    me = lax.axis_index(axis)
    slots = []
    for j in range(size):
        which = lax.rem(me - j + size, size)
        chosen = pieces[0]
        for k in range(1, size):
            chosen = jnp.where(which == k, pieces[k], chosen)
        slots.append(chosen)
    return jnp.stack(slots, axis=where)


def total(parts):
    return sum(part.astype(F32) for part in parts)


def start(parts, axis, where):
    size = lax.axis_size(axis)
    me = lax.axis_index(axis)

    def at(index):
        return [lax.dynamic_index_in_dim(part, index, where, keepdims=False) for part in parts]

    out = [total(at(lax.rem(me + k, size))).astype(BF) for k in range(1, size)]
    return at(me), [shifted(part, axis, k) for k, part in enumerate(out, 1)], out


def start_joined(sums, axis):
    size = lax.axis_size(axis)
    me = lax.axis_index(axis)

    def at(index):
        values = [total([lax.dynamic_index_in_dim(p, index, 0, keepdims=False) for p in parts]) for parts in sums]
        return jnp.concatenate(values, axis=-1)

    return [at(me)] + [shifted(at(lax.rem(me + k, size)).astype(BF), axis, k) for k in range(1, size)]


def start_core(keep, send):
    halves, _, rows, cols = keep.shape
    shape = (halves, lax.axis_size("z"), lax.axis_size("x"), rows, cols)
    return [keep.reshape(shape)], [shifted(send, "core", 1).reshape(shape)]


def tie_sums(pending, *others):
    arrived, *others = tie([p[1] for p in pending], *others)
    return [p[0] + list(a) for p, a in zip(pending, arrived)], *others


def tie(*groups):
    return lax.optimization_barrier(groups)


def sum_pairs(value, axes):
    for axis in axes:
        size = lax.axis_size(axis)
        step = 1
        while step < size:
            value = value + lax.ppermute(value, axis, [(i, i ^ step) for i in range(size)])
            step *= 2
    return value


def shards(
    content_in,
    query_in,
    lengths,
    factor_order,
    buckets,
    w_qkv,
    b_qv,
    w_out,
    w_in,
    b_in,
    w_down,
    b_outs,
    norm_gain,
    norm_bias,
    rel_table,
    cot_content,
    cot_query,
):
    me = lax.axis_index("y")
    halves = lax.axis_size("y")
    each = content_in.shape[0] // halves
    assert each == 1
    seq = content_in.shape[1]
    width = content_in.shape[2]
    bucket_count, heads_here = rel_table.shape
    heads = heads_here * halves
    part = w_qkv.shape[2]
    ffn = w_in.shape[1]
    rows = w_in.shape[0]

    def mine(array):
        return lax.dynamic_index_in_dim(array, me, 0, keepdims=False)

    rest = lax.all_gather(
        jnp.concatenate([w_in, w_down.T], axis=1), ("y", "z", "x", "core"), axis=0
    ).reshape(halves, width, 2 * ffn)
    vectors = jnp.concatenate([b_qv, b_in.reshape(ffn // part, part)], axis=0)
    vectors = jnp.concatenate(
        [vectors, jnp.pad(rel_table, ((0, 0), (0, part - heads_here)))], axis=0
    )
    vectors = gather_finish(gather_start(vectors, "y"), "y", 0).astype(F32)
    qv_bias = vectors[:, :2]
    hidden_bias = vectors[:, 2 : 2 + ffn // part].reshape(halves, 1, ffn)
    table = vectors[:, 2 + ffn // part :, :heads_here]
    table = jnp.transpose(table, (0, 2, 1)).reshape(heads, bucket_count)
    table = jnp.pad(table, ((0, 0), (0, 128 - bucket_count)))
    vector_rows = jnp.concatenate([b_outs, norm_gain, norm_bias], axis=0).astype(F32)
    vector_rows = jnp.pad(vector_rows, ((0, 2), (0, 0)))

    core = lax.axis_index("core").astype(jnp.int32).reshape(1)
    content = mine(content_in)
    stacked = jnp.concatenate([content, mine(query_in)], axis=0)
    buckets_t = mine(buckets).T
    rank = mine(factor_order)
    length = lax.dynamic_slice_in_dim(lengths, me, 1, 0)
    bias = masked_bias(length, buckets_t, rank, table)

    shard = jnp.concatenate([*w_qkv, w_out.T], axis=1)
    wide = shard.shape[1] // 2
    chips = width // (2 * rows)
    along_z = gather_finish(gather_start(shard, "z"), "z", 0)
    one = gather_start(along_z[:, :, :wide], "x")
    two = gather_start(along_z[:, :, wide:], "y")
    one, two, bias = tie(one, two, bias)
    one = gather_start(gather_finish(one, "x", 1), "y")
    two = gather_start(gather_finish(two, "y", 0), "x")
    one = gather_finish(one, "y", 0).reshape(halves, chips, rows, wide)
    two = gather_finish(two, "x", 2).reshape(halves, chips, rows, wide)
    pieces = (one, two, shifted(one, "core", 1), shifted(two, "core", 1))
    q_t, k_t, v_t, heads_all = project(core, pieces, stacked, qv_bias, part)
    heads_all = heads_all.reshape(halves, width, 2 * wide)
    probs, ctx_t, inverse = attention(q_t, k_t, v_t, bias, (), heads, 0, heads // 2)

    cot = jnp.concatenate([mine(cot_content), mine(cot_query)], axis=0)
    output, low_t, active, slope, unit_one, inv_one, d_two, d_two_low, d_two_low_t, sums_two = up(
        ctx_t, stacked, cot, heads_all, rest, hidden_bias, vector_rows, part
    )
    output_got = shifted(output, "y", 1)
    d_hidden, d_one, d_one_low_t, dctx_t, sums_one, sums_hidden = down(
        d_two_low, d_two, slope, unit_one, inv_one, heads_all, rest, vector_rows, part
    )
    in_grads = outer_in(low_t, d_hidden, d_one_low_t, ctx_t, rows)
    in_sum = lax.psum_scatter(in_grads, ("z", "x", "core"), scatter_dimension=0)
    output_got, in_grads = tie(output_got, in_grads)
    down_pair = outer(core, d_two_low_t, active, rows, after=(in_grads,))
    down_pending = start_core(*down_pair)
    sums_small = jnp.concatenate(
        [jnp.sum(sums_hidden, axis=(0, 1, 3)).reshape(-1)]
        + [s[i] for i in range(3) for s in (jnp.sum(sums_one, axis=(0, 2)), jnp.sum(sums_two, axis=(0, 2)))]
    )
    half_back = functools.partial(attention_back, q_t, k_t, v_t, probs, inverse, ctx_t, dctx_t)
    grads = half_back((), heads, 0, 1, after=down_pair)
    (down_sum,), grads = tie_sums([down_pending], grads)
    down_pending = start(down_sum, "y", 0)
    grads = half_back(tuple(grads), heads, 1, heads // 2 - 1, after=down_pending[2])
    dq_t, dk_t, dv_t, held = grads
    pair = project_back(core, stacked, dq_t, dk_t, dv_t, halves, rows)
    (down_sum,), pair = tie_sums([down_pending], pair)
    down_pending = start(down_sum, "x", 1)
    pending = start_core(*pair)
    table_grad = table_back(buckets_t, held, bucket_count, after=tuple(pair) + tuple(down_pending[2]))
    (qkv_sum, down_sum), table_grad = tie_sums([pending, down_pending], table_grad)
    pending, down_pending = start(qkv_sum, "y", 0), start(down_sum, "z", 0)
    half = me.astype(jnp.int32).reshape(1)
    grad_in = inputs_back(
        half, heads_all, d_one, dq_t, dk_t, dv_t, after=pending[2] + down_pending[2]
    )
    table_grad = jnp.sum(table_grad.reshape(bucket_count, heads, -1), axis=2).T
    small = jnp.concatenate(
        [jnp.sum(g.astype(F32), axis=1) for g in (dq_t, dv_t)] + [table_grad.reshape(-1), sums_small]
    )
    small = sum_pairs(small.reshape(-1, 128), ("core",))
    outs = (output, output_got)
    (qkv_sum,), grad_in, small, outs = tie_sums([pending], grad_in, small, outs)
    pending = start(qkv_sum, "x", 1)
    grad_kept, grad_sent = grad_in
    grad_got = shifted(grad_sent, "y", 1)

    small = sum_pairs(small, ("z",))
    (qkv_sum,), small = tie_sums([pending], small)
    pending = start(qkv_sum, "z", 0)
    down_share = total(down_pending[0] + down_pending[1])
    in_pending = start([in_sum], "y", 0)
    in_share = total(in_pending[0] + in_pending[1])
    small = sum_pairs(small, ("x", "y")).reshape(-1)
    first_kept = me == 0
    output, output_got = outs
    outs = jnp.stack(
        [jnp.where(first_kept, output, output_got), jnp.where(first_kept, output_got, output)]
    ).reshape(halves, 2, seq, width)
    grad_ins = jnp.stack(
        [jnp.where(first_kept, grad_kept, grad_got), jnp.where(first_kept, grad_got, grad_kept)]
    ).reshape(halves, 2, seq, width // halves)
    qkv_share = total(pending[0] + pending[1])
    ends = [2 * width, 2 * width + heads * bucket_count]
    ends.append(ends[1] + halves * ffn)
    grad_b_qv = mine(jnp.transpose(small[: ends[0]].reshape(2, halves, part), (1, 0, 2)))
    grad_table = mine(small[ends[0] : ends[1]].reshape(halves, heads_here, bucket_count)).T
    grad_b_in = mine(small[ends[1] : ends[2]].reshape(halves, ffn))
    pairs = small[ends[2] :].reshape(3, 2, width)
    return (
        outs[:, 0],
        outs[:, 1],
        grad_ins[:, 0],
        grad_ins[:, 1],
        jnp.transpose(qkv_share.reshape(rows, 3, part), (1, 0, 2)),
        grad_b_qv,
        in_share[:, ffn:].T,
        in_share[:, :ffn],
        grad_b_in,
        down_share.T,
        pairs[0],
        pairs[1],
        pairs[2],
        grad_table,
    )


def solution(mesh):
    count = mesh.shape["dp"] // 2
    depth = 4 if count % 4 == 0 else 1
    while count // depth > depth:
        depth *= 2
    grid = mesh.devices.reshape(depth, count // depth, 2, mesh.shape["tensor"])
    fine = Mesh(grid, ("z", "x", "core", "y"))
    dp = ("z", "x", "core")
    return jax.shard_map(
        shards,
        mesh=fine,
        in_specs=(
            P(dp, None, None),
            P(dp, None, None),
            P(dp),
            P(dp, None),
            P(dp, None, None),
            P(None, dp, "y"),
            P(None, "y"),
            P("y", dp),
            P(dp, "y"),
            P("y"),
            P("y", dp),
            P(),
            P(),
            P(),
            P(None, "y"),
            P(dp, None, None),
            P(dp, None, None),
        ),
        out_specs=(
            P(dp, None, None),
            P(dp, None, None),
            P(dp, None, "y"),
            P(dp, None, "y"),
            P(None, dp, "y"),
            P(None, "y"),
            P("y", dp),
            P(dp, "y"),
            P("y"),
            P("y", dp),
            P(),
            P(),
            P(),
            P(None, "y"),
        ),
        check_vma=False,
    )
```

```python
import functools

import jax
import jax.numpy as jnp
from jax import lax
from jax.experimental import pallas as pl
from jax.experimental.pallas import tpu as pltpu
from jax.sharding import Mesh, PartitionSpec as P

EPSILON = 1e-05


def cost(us):
    return pl.CostEstimate(flops=int(us * 1e7), bytes_accessed=int(us * 1e4), transcendentals=0)

NEG = -1e30
BF = jnp.bfloat16
F32 = jnp.float32


def dot(a, b, dims):
    return lax.dot_general(a, b, (dims, ((), ())), preferred_element_type=F32)


NN = ((1,), (0,))
NT = ((1,), (1,))
TN = ((0,), (0,))


def bias_kernel(len_ref, buckets_ref, rank_row_ref, rank_col_ref, table_ref, out_ref):
    rows, cols = buckets_ref.shape
    heads = table_ref.shape[0]
    start = pl.program_id(0) * rows
    key = start + lax.broadcasted_iota(jnp.int32, (rows, cols), 0)
    query = lax.broadcasted_iota(jnp.int32, (rows, cols), 1)
    valid = key < len_ref[0]
    rank_key = rank_col_ref[...]
    rank_query = rank_row_ref[...]
    content = (valid & (rank_key <= rank_query)) | (key == query)
    stream = (valid & (rank_key < rank_query)) | (key == 0)
    index = buckets_ref[...]
    for head in range(heads):
        row = jnp.broadcast_to(table_ref[head : head + 1, :], (rows, 128))
        bias = jnp.concatenate(
            [
                jnp.take_along_axis(
                    row, index[:, c : c + 128], axis=1, mode="promise_in_bounds"
                )
                for c in range(0, cols, 128)
            ],
            axis=1,
        )
        out_ref[head, :, :cols] = jnp.where(content, bias, NEG).astype(BF)
        out_ref[head, :, cols:] = jnp.where(stream, bias, NEG).astype(BF)


def masked_bias(length, buckets_t, rank, table, after=()):
    seq = buckets_t.shape[0]
    heads = table.shape[0]
    step = 128
    return call(
        bias_kernel,
        after,
        [length, buckets_t, rank.reshape(1, seq), rank.reshape(seq, 1), table],
        grid=(seq // step,),
        in_specs=[
            pl.BlockSpec(memory_space=pltpu.SMEM),
            pl.BlockSpec((step, seq), lambda g: (g, 0)),
            pl.BlockSpec((1, seq), lambda g: (0, 0)),
            pl.BlockSpec((step, 1), lambda g: (g, 0)),
            pl.BlockSpec((heads, 128), lambda g: (0, 0)),
        ],
        out_specs=pl.BlockSpec((heads, step, 2 * seq), lambda g: (0, g, 0)),
        out_shape=jax.ShapeDtypeStruct((heads, seq, 2 * seq), BF),
        cost_estimate=cost(9),
    )


def forward_kernel(q_ref, k_ref, v_ref, bias_ref, probs_ref, ctx_ref, inv_ref, *, tile):
    count = bias_ref.shape[0]
    size = q_ref.shape[0] // count
    for head in range(count):
        rows = slice(head * size, (head + 1) * size)
        keys = (k_ref[rows, :].astype(F32) * 0.125).astype(BF)
        for t in range(q_ref.shape[1] // tile):
            at = slice(t * tile, (t + 1) * tile)
            scores = dot(keys, q_ref[rows, at], TN) + bias_ref[head, :, at].astype(F32)
            high = jnp.max(scores, axis=0, keepdims=True)
            weight = jnp.exp(scores - high)
            inverse = 1.0 / jnp.sum(weight, axis=0, keepdims=True)
            low = weight.astype(BF)
            probs_ref[head, :, at] = low
            ctx_ref[rows, at] = (dot(v_ref[rows, :], low, NN) * inverse).astype(BF)
            inv_ref[head, :, at] = inverse


def attention(q_t, k_t, v_t, bias, before, heads, begin, steps, tile=1024, count=2, after=()):
    width, both = q_t.shape
    seq = k_t.shape[1]
    size = width // heads * count
    thin = pl.BlockSpec((size, seq), lambda h: (h + begin, 0))
    wide = pl.BlockSpec((size, both), lambda h: (h + begin, 0))
    square = pl.BlockSpec((count, seq, both), lambda h: (h + begin, 0, 0))

    def kernel(q_ref, k_ref, v_ref, bias_ref, *refs):
        forward_kernel(q_ref, k_ref, v_ref, bias_ref, *refs[-3:], tile=tile)

    return call(
        kernel,
        after,
        [q_t, k_t, v_t, bias, *before],
        grid=(steps,),
        in_specs=[wide, thin, thin, square] + [pl.BlockSpec(memory_space=pl.ANY)] * len(before),
        out_specs=[square, wide, pl.BlockSpec((count, 1, both), lambda h: (h + begin, 0, 0))],
        out_shape=[
            pltpu.HBM((heads, seq, both), BF),
            pltpu.HBM((width, both), BF),
            pltpu.HBM((heads, 1, both), F32),
        ],
        input_output_aliases={4 + i: i for i in range(len(before))},
        compiler_params=pltpu.CompilerParams(vmem_limit_bytes=48 * 1024 * 1024),
        cost_estimate=cost(3 * steps),
    )


def backward_kernel(q_ref, k_ref, v_ref, p_ref, inv_ref, ctx_ref, dctx_ref, *refs, tile):
    dq_ref, dk_ref, dv_ref, held_ref = refs[-4:]
    count = p_ref.shape[0]
    size, seq = k_ref.shape[0] // count, k_ref.shape[1]
    group = held_ref.shape[1] // count
    for head in range(count):
        rows = slice(head * size, (head + 1) * size)
        queries = q_ref[rows, :]
        keys = k_ref[rows, :]
        values = v_ref[rows, :]
        grad = dctx_ref[rows, :].astype(F32) * inv_ref[head]
        inner = jnp.sum(grad * ctx_ref[rows, :].astype(F32), axis=0, keepdims=True)
        grad = grad.astype(BF)
        dk = jnp.zeros(keys.shape, F32)
        dv = jnp.zeros(keys.shape, F32)
        for t in range(seq // tile):
            both = None
            for stream in range(2):
                lo = stream * seq + t * tile
                at = slice(lo, lo + tile)
                weight = p_ref[head, :, at]
                part = dot(values, grad[:, at], TN) - inner[:, at]
                ds = weight.astype(F32) * part
                low = ds.astype(BF)
                dv += dot(grad[:, at], weight, NT)
                dk += dot(queries[:, at], low, NT)
                dq_ref[rows, at] = (dot(keys, low, NN) * 0.125).astype(BF)
                both = ds if both is None else both + ds
            held_ref[:, head * group : (head + 1) * group, t * tile : (t + 1) * tile] = (
                both.astype(BF).reshape(seq // group, group, tile)
            )
        dk_ref[rows, :] = (dk * 0.125).astype(BF)
        dv_ref[rows, :] = dv.astype(BF)


def attention_back(
    q_t, k_t, v_t, probs, inverse, ctx_t, dctx_t, before, heads, begin, steps, count=2, group=16, tile=512, after=()
):
    width, both = q_t.shape
    seq = k_t.shape[1]
    size = width // heads * count
    wide = pl.BlockSpec((size, both), lambda h: (h + begin, 0))
    thin = pl.BlockSpec((size, seq), lambda h: (h + begin, 0))
    operands = [q_t, k_t, v_t, probs, inverse, ctx_t, dctx_t, *before]
    return call(
        functools.partial(backward_kernel, tile=tile),
        after,
        operands,
        grid=(steps,),
        in_specs=[
            wide,
            thin,
            thin,
            pl.BlockSpec((count, seq, both), lambda h: (h + begin, 0, 0)),
            pl.BlockSpec((count, 1, both), lambda h: (h + begin, 0, 0)),
            wide,
            wide,
        ]
        + [pl.BlockSpec(memory_space=pl.ANY)] * len(before),
        out_specs=[
            wide,
            thin,
            thin,
            pl.BlockSpec((seq // group, count * group, seq), lambda h: (0, h + begin, 0)),
        ],
        out_shape=[
            pltpu.HBM((width, both), BF),
            pltpu.HBM((width, seq), BF),
            pltpu.HBM((width, seq), BF),
            pltpu.HBM((seq // group, heads * group, seq), BF),
        ],
        input_output_aliases={7 + i: i for i in range(len(before))},
        compiler_params=pltpu.CompilerParams(vmem_limit_bytes=56 * 1024 * 1024),
        cost_estimate=cost(1e4 * steps),
    )


def table_kernel(buckets_ref, *refs, buckets, group):
    held_ref, out_ref, total = refs
    step, steps = pl.program_id(0), pl.num_programs(0)
    parts = buckets_ref.shape[0] // group
    index = buckets_ref[...].astype(F32).astype(BF)
    hot = jnp.concatenate(
        [
            jnp.concatenate(
                [
                    jnp.where(index[p * group : (p + 1) * group] == jnp.asarray(n, BF), 1.0, 0.0).astype(BF)
                    for n in range(buckets)
                ],
                axis=0,
            )
            for p in range(parts)
        ],
        axis=1,
    )
    held = jnp.concatenate([held_ref[p] for p in range(parts)], axis=1)
    value = dot(hot, held, NT)

    @pl.when(step == 0)
    def _():
        total[...] = value

    @pl.when(step > 0)
    def _():
        total[...] += value

    @pl.when(step == steps - 1)
    def _():
        value = total[...]
        row = lax.broadcasted_iota(jnp.int32, value.shape, 0) % group
        col = lax.broadcasted_iota(jnp.int32, value.shape, 1) % group
        kept = jnp.where(row == col, value, 0.0)
        out_ref[...] = jnp.sum(kept.reshape(buckets, group, value.shape[1]), axis=1)


def table_back(buckets_t, held, buckets, group=16, parts=8, after=()):
    seq = buckets_t.shape[0]
    cols = held.shape[1]
    return call(
        functools.partial(table_kernel, buckets=buckets, group=group),
        after,
        [buckets_t, held],
        grid=(seq // (group * parts),),
        in_specs=[
            pl.BlockSpec((group * parts, seq), lambda g: (g, 0)),
            pl.BlockSpec((parts, cols, seq), lambda g: (g, 0, 0)),
        ],
        out_specs=whole((buckets, cols)),
        out_shape=jax.ShapeDtypeStruct((buckets, cols), F32),
        scratch_shapes=[pltpu.VMEM((buckets * group, cols), F32)],
        compiler_params=pltpu.CompilerParams(vmem_limit_bytes=40 * 1024 * 1024),
        cost_estimate=cost(6),
    )


def call(kernel, after, operands, *, in_specs, **settings):
    count = len(operands)

    def body(*refs):
        kernel(*refs[:count], *refs[count + len(after) :])

    operands = [
        pltpu.with_memory_space_constraint(o, pltpu.HBM) if s.memory_space is None and o.size > 1 << 16 else o
        for o, s in zip(operands, in_specs)
    ]
    anywhere = [pl.BlockSpec(memory_space=pl.ANY)] * len(after)
    return pl.pallas_call(body, in_specs=in_specs + anywhere, **settings)(*operands, *after)


def whole(shape):
    return pl.BlockSpec(shape, lambda *_: (0,) * len(shape))


def once(shape, at):
    return pl.BlockSpec(shape, lambda *_: at, pipeline_mode=pl.Buffered(1))


def unit(value):
    centred = value - jnp.mean(value, axis=-1, keepdims=True)
    inverse = lax.rsqrt(jnp.mean(centred * centred, axis=-1, keepdims=True) + EPSILON)
    return centred * inverse, inverse


def unit_back(grad, along, inverse):
    mean = jnp.mean(grad, axis=-1, keepdims=True)
    slope = jnp.mean(grad * along, axis=-1, keepdims=True)
    return (grad - mean - along * slope) * inverse


def column_sum(value):
    rows = value.shape[0]
    return jnp.sum(value.reshape(rows // 8, 8, value.shape[1]), axis=0)


def up_kernel(
    ctx_ref, x_ref, cot_ref, wo_ref, wi_ref, wd_ref, bi_ref, rows_ref,
    out_ref, lowt_ref, act_ref, slope_ref, unit_ref, inv_ref, dres_ref, dlow_ref, dlowt_ref, sums_ref,
    *, chunk, part_rows,
):
    halves, width, part = wo_ref.shape
    ffn = wi_ref.shape[2]
    row = lambda i: rows_ref[i : i + 1, :]
    parts = [slice(r, r + part_rows) for r in range(0, x_ref.shape[0], part_rows)]
    resids, lows = [], []
    for at in parts:
        resid = x_ref[at, :].astype(F32) + row(0)
        for y in range(halves):
            resid += dot(ctx_ref[y * part : (y + 1) * part, at].T, wo_ref[y], NT)
        along, inverse = unit(resid)
        unit_ref[at, :] = along
        inv_ref[at, :] = inverse
        normed = along * row(2) + row(4)
        low = normed.astype(BF)
        lowt_ref[:, at] = low.T
        resids.append(normed + row(1))
        lows.append(low)
    for y in range(halves):
        for n, at in enumerate(parts):
            for c in range(0, ffn, chunk):
                cols = slice(c, c + chunk)
                hidden = dot(lows[n], wi_ref[y, :, cols], NN) + bi_ref[y, :, cols]
                cdf = 0.5 * lax.erf(hidden * 0.7071067811865476) + 0.5
                density = jnp.exp(hidden * hidden * -0.5) * 0.3989422804014327
                act_ref[y, at, cols] = (hidden * cdf).astype(BF)
                slope_ref[y, at, cols] = (cdf + hidden * density).astype(BF)
            resids[n] += dot(act_ref[y, at, :], wd_ref[y], NT)
    sums = [0.0, 0.0, 0.0]
    for n, at in enumerate(parts):
        along, inverse = unit(resids[n])
        out_ref[at, :] = (along * row(3) + row(5)).astype(BF)
        cot = cot_ref[at, :].astype(F32)
        dres = unit_back(cot * row(3), along, inverse)
        dres_ref[at, :] = dres
        dlow = dres.astype(BF)
        dlow_ref[at, :] = dlow
        dlowt_ref[:, at] = dlow.T
        for i, value in enumerate((dres, cot * along, cot)):
            sums[i] += column_sum(value)
    for i in range(3):
        sums_ref[0, i] = sums[i]


def up(ctx_t, stacked, cot, heads_all, rest, hidden_bias, rows, part, tile=256, chunk=512, part_rows=256, after=()):
    tokens, width = stacked.shape
    halves = rest.shape[0]
    ffn = rest.shape[2] // 2
    tall = pl.BlockSpec((width, tile), lambda t: (0, t))
    flat = pl.BlockSpec((tile, width), lambda t: (t, 0))
    wide = pl.BlockSpec((halves, tile, ffn), lambda t: (0, t, 0))
    sds = pltpu.HBM
    return call(
        functools.partial(up_kernel, chunk=chunk, part_rows=part_rows),
        after,
        [ctx_t, stacked, cot, heads_all, rest, rest, hidden_bias, rows],
        grid=(tokens // tile,),
        in_specs=[
            tall,
            flat,
            flat,
            once((halves, width, part), (0, 0, 3)),
            once((halves, width, ffn), (0, 0, 0)),
            once((halves, width, ffn), (0, 0, 1)),
            whole((halves, 1, ffn)),
            whole(rows.shape),
        ],
        out_specs=[
            flat, tall, wide, wide, flat, pl.BlockSpec((tile, 1), lambda t: (t, 0)), flat, flat, tall,
            pl.BlockSpec((1, 3, 8, width), lambda t: (t, 0, 0, 0)),
        ],
        out_shape=[
            sds((tokens, width), BF),
            sds((width, tokens), BF),
            sds((halves, tokens, ffn), BF),
            sds((halves, tokens, ffn), BF),
            sds((tokens, width), F32),
            sds((tokens, 1), F32),
            sds((tokens, width), F32),
            sds((tokens, width), BF),
            sds((width, tokens), BF),
            sds((tokens // tile, 3, 8, width), F32),
        ],
        compiler_params=pltpu.CompilerParams(vmem_limit_bytes=58 * 1024 * 1024),
        cost_estimate=cost(20),
    )


def down_kernel(
    dlow_ref, dres_ref, slope_ref, unit_ref, inv_ref, wo_ref, wi_ref, wd_ref, rows_ref,
    dhid_ref, done_ref, dot_ref, dctx_ref, sums_ref, hsum_ref, *, chunk, part_rows,
):
    halves, width, part = wo_ref.shape
    ffn = wi_ref.shape[2]
    parts = [slice(r, r + part_rows) for r in range(0, dlow_ref.shape[0], part_rows)]
    dnorms = [dres_ref[at, :] for at in parts]
    for y in range(halves):
        for n, at in enumerate(parts):
            for c in range(0, ffn, chunk):
                cols = slice(c, c + chunk)
                dhid = dot(dlow_ref[at, :], wd_ref[y, :, cols], NN) * slope_ref[y, at, cols].astype(F32)
                hsum_ref[0, n, y, :, cols] = column_sum(dhid)
                dhid_ref[y, at, cols] = dhid.astype(BF)
            dnorms[n] += dot(dhid_ref[y, at, :], wi_ref[y], NT)
    sums = [0.0, 0.0, 0.0]
    for n, at in enumerate(parts):
        dnorm = dnorms[n]
        along = unit_ref[at, :]
        done = unit_back(dnorm * rows_ref[2:3, :], along, inv_ref[at, :])
        done_ref[at, :] = done
        low = done.astype(BF)
        dot_ref[:, at] = low.T
        for y in range(halves):
            dctx_ref[y * part : (y + 1) * part, at] = dot(low, wo_ref[y], NN).astype(BF).T
        for i, value in enumerate((done, dnorm * along, dnorm)):
            sums[i] += column_sum(value)
    for i in range(3):
        sums_ref[0, i] = sums[i]


def down(dlow, dres, slope, along, inverse, heads_all, rest, rows, part, tile=256, chunk=512, part_rows=256, after=()):
    tokens, width = dlow.shape
    halves = rest.shape[0]
    ffn = rest.shape[2] // 2
    tall = pl.BlockSpec((width, tile), lambda t: (0, t))
    flat = pl.BlockSpec((tile, width), lambda t: (t, 0))
    wide = pl.BlockSpec((halves, tile, ffn), lambda t: (0, t, 0))
    sds = pltpu.HBM
    return call(
        functools.partial(down_kernel, chunk=chunk, part_rows=part_rows),
        after,
        [dlow, dres, slope, along, inverse, heads_all, rest, rest, rows],
        grid=(tokens // tile,),
        in_specs=[
            flat,
            flat,
            wide,
            flat,
            pl.BlockSpec((tile, 1), lambda t: (t, 0)),
            once((halves, width, part), (0, 0, 3)),
            once((halves, width, ffn), (0, 0, 0)),
            once((halves, width, ffn), (0, 0, 1)),
            whole(rows.shape),
        ],
        out_specs=[
            wide, flat, tall, tall,
            pl.BlockSpec((1, 3, 8, width), lambda t: (t, 0, 0, 0)),
            pl.BlockSpec((1, tile // part_rows, halves, 8, ffn), lambda t: (t, 0, 0, 0, 0)),
        ],
        out_shape=[
            sds((halves, tokens, ffn), BF),
            sds((tokens, width), F32),
            sds((width, tokens), BF),
            sds((width, tokens), BF),
            sds((tokens // tile, 3, 8, width), F32),
            sds((tokens // tile, tile // part_rows, halves, 8, ffn), F32),
        ],
        compiler_params=pltpu.CompilerParams(vmem_limit_bytes=58 * 1024 * 1024),
        cost_estimate=cost(18),
    )


def put_rows(core, value, keep_ref, send_ref, at):
    chips, rows = keep_ref.shape[1], keep_ref.shape[2]
    value = value.reshape(chips, 2, rows, value.shape[1])

    @pl.when(core == 0)
    def _():
        keep_ref[at] = value[:, 0]
        send_ref[at] = value[:, 1]

    @pl.when(core != 0)
    def _():
        keep_ref[at] = value[:, 1]
        send_ref[at] = value[:, 0]


def outer_kernel(core_ref, left_ref, right_ref, keep_ref, send_ref):
    value = dot(left_ref[...], right_ref[0], NN).astype(BF)
    put_rows(core_ref[0], value, keep_ref, send_ref, 0)


def outer(core, left_t, right, rows, tile=768, after=()):
    width, tokens = left_t.shape
    halves, _, cols = right.shape
    block = pl.BlockSpec((1, width // (2 * rows), rows, tile), lambda y, c: (y, 0, 0, c))
    shape = jax.ShapeDtypeStruct((halves, width // (2 * rows), rows, cols), BF)
    return call(
        outer_kernel,
        after,
        [core, left_t, right],
        grid=(halves, cols // tile),
        in_specs=[
            pl.BlockSpec(memory_space=pltpu.SMEM),
            whole(left_t.shape),
            pl.BlockSpec((1, tokens, tile), lambda y, c: (y, 0, c)),
        ],
        out_specs=[block, block],
        out_shape=[shape, shape],
        cost_estimate=cost(5),
    )


def outer_in_kernel(low_ref, dhid_ref, dot_ref, ctx_ref, out_ref):
    owners, _, rows, _ = out_ref.shape
    ffn = dhid_ref.shape[2]
    half = ffn // 2
    for c in (0, half):
        value = dot(low_ref[...], dhid_ref[0, :, c : c + half], NN).astype(BF)
        out_ref[:, 0, :, c : c + half] = value.reshape(owners, rows, half)
    value = dot(dot_ref[...], ctx_ref[...], NT).astype(BF)
    out_ref[:, 0, :, ffn:] = value.reshape(owners, rows, value.shape[1])


def outer_in(low_t, dhid, do_t, ctx_t, rows, after=()):
    width, tokens = low_t.shape
    halves, _, ffn = dhid.shape
    part = ctx_t.shape[0] // halves
    owners = width // rows
    return call(
        outer_in_kernel,
        after,
        [low_t, dhid, do_t, ctx_t],
        grid=(halves,),
        in_specs=[
            whole(low_t.shape),
            pl.BlockSpec((1, tokens, ffn), lambda y: (y, 0, 0)),
            whole(do_t.shape),
            pl.BlockSpec((part, tokens), lambda y: (y, 0)),
        ],
        out_specs=pl.BlockSpec((owners, 1, rows, ffn + part), lambda y: (0, y, 0, 0)),
        out_shape=pltpu.HBM((owners, halves, rows, ffn + part), BF),
        compiler_params=pltpu.CompilerParams(vmem_limit_bytes=48 * 1024 * 1024),
        cost_estimate=cost(6),
    )


def project_kernel(core_ref, own_a, own_b, other_a, other_b, x_ref, bias_ref, q_ref, k_ref, v_ref, w_ref):
    core = core_ref[0]
    cut = own_a.shape[3]
    width = x_ref.shape[1]
    part, seq = k_ref.shape
    w_ref[0, :, core, :, :cut] = own_a[0]
    w_ref[0, :, core, :, cut:] = own_b[0]
    w_ref[0, :, 1 - core, :, :cut] = other_a[0]
    w_ref[0, :, 1 - core, :, cut:] = other_b[0]
    weights = w_ref[0, :, :, :, : 3 * part].reshape(width, 3 * part)
    q = dot(x_ref[...], weights[:, :part], NN) + bias_ref[0, 0:1, :]
    q_ref[...] = q.astype(BF).T
    kv = dot(x_ref[:seq, :], weights[:, part:], NN)
    k_ref[...] = kv[:, :part].astype(BF).T
    v_ref[...] = (kv[:, part:] + bias_ref[0, 1:2, :]).astype(BF).T


def project(core, pieces, stacked, bias, part, after=()):
    tokens, width = stacked.shape
    halves, chips, rows, cut = pieces[0].shape
    cols = cut + pieces[1].shape[3]
    seq = tokens // 2
    sds = pltpu.HBM
    one = pl.BlockSpec((1, chips, rows, cut), lambda y: (y, 0, 0, 0))
    two = pl.BlockSpec((1, chips, rows, cols - cut), lambda y: (y, 0, 0, 0))
    return call(
        project_kernel,
        after,
        [core, *pieces, stacked, bias],
        grid=(halves,),
        in_specs=[
            pl.BlockSpec(memory_space=pltpu.SMEM), one, two, one, two,
            whole(stacked.shape),
            pl.BlockSpec((1, 2, part), lambda y: (y, 0, 0)),
        ],
        out_specs=[
            pl.BlockSpec((part, tokens), lambda y: (y, 0)),
            pl.BlockSpec((part, seq), lambda y: (y, 0)),
            pl.BlockSpec((part, seq), lambda y: (y, 0)),
            pl.BlockSpec((1, chips, 2, rows, cols), lambda y: (y, 0, 0, 0, 0)),
        ],
        out_shape=[
            sds((width, tokens), BF),
            sds((width, seq), BF),
            sds((width, seq), BF),
            sds((halves, chips, 2, rows, cols), BF),
        ],
        compiler_params=pltpu.CompilerParams(vmem_limit_bytes=40 * 1024 * 1024),
        cost_estimate=cost(6),
    )


def project_back_kernel(core_ref, x_ref, dq_ref, dk_ref, dv_ref, keep_ref, send_ref, xt_ref):
    @pl.when(pl.program_id(0) == 0)
    def _():
        xt_ref[...] = x_ref[...].T

    values = []
    for ref in (dq_ref, dk_ref, dv_ref):
        tokens = ref.shape[1]
        values.append(dot(xt_ref[:, :tokens], ref[...], NT).astype(BF))
    put_rows(core_ref[0], jnp.concatenate(values, axis=1), keep_ref, send_ref, 0)


def project_back(core, stacked, dq_t, dk_t, dv_t, halves, rows, after=()):
    tokens, width = stacked.shape
    chips = width // (2 * rows)
    part = width // halves
    block = pl.BlockSpec((1, chips, rows, 3 * part), lambda y: (y, 0, 0, 0))
    shape = pltpu.HBM((halves, chips, rows, 3 * part), BF)
    return call(
        project_back_kernel,
        after,
        [core, stacked, dq_t, dk_t, dv_t],
        grid=(halves,),
        in_specs=[pl.BlockSpec(memory_space=pltpu.SMEM), whole(stacked.shape)]
        + [pl.BlockSpec((part, g.shape[1]), lambda y: (y, 0)) for g in (dq_t, dk_t, dv_t)],
        out_specs=[block, block],
        out_shape=[shape, shape],
        scratch_shapes=[pltpu.VMEM((width, tokens), BF)],
        compiler_params=pltpu.CompilerParams(vmem_limit_bytes=40 * 1024 * 1024),
        cost_estimate=cost(5),
    )


def inputs_kernel(half_ref, w_ref, done_ref, dq_ref, dk_ref, dv_ref, keep_ref, send_ref, sum_ref):
    step, steps = pl.program_id(0), pl.num_programs(0)
    halves, width, cols = w_ref.shape
    part = cols // 3
    total = done_ref[...]
    for y in range(halves):
        total += dot(dq_ref[y * part : (y + 1) * part, :].T, w_ref[y, :, :part], NT)
    sum_ref[...] = total

    @pl.when(step < steps // 2)
    def _():
        extra = 0.0
        for y in range(halves):
            at = slice(y * part, (y + 1) * part)
            extra += dot(dk_ref[at, :].T, w_ref[y, :, part : 2 * part], NT)
            extra += dot(dv_ref[at, :].T, w_ref[y, :, 2 * part :], NT)
        sum_ref[...] += extra

    half = width // 2

    @pl.when(half_ref[0] == 0)
    def _():
        keep_ref[...] = sum_ref[:, :half].astype(BF)
        send_ref[...] = sum_ref[:, half:].astype(BF)

    @pl.when(half_ref[0] != 0)
    def _():
        keep_ref[...] = sum_ref[:, half:].astype(BF)
        send_ref[...] = sum_ref[:, :half].astype(BF)


def inputs_back(half, weights, done, dq_t, dk_t, dv_t, tile=256, after=()):
    tokens, width = done.shape
    last = tokens // (2 * tile) - 1
    thin = pl.BlockSpec((width, tile), lambda t: (0, jnp.minimum(t, last)))
    out = pl.BlockSpec((tile, width // 2), lambda t: (t, 0))
    return call(
        inputs_kernel,
        after,
        [half, weights, done, dq_t, dk_t, dv_t],
        grid=(tokens // tile,),
        in_specs=[
            pl.BlockSpec(memory_space=pltpu.SMEM),
            once((weights.shape[0], width, 3 * width // weights.shape[0]), (0, 0, 0)),
            pl.BlockSpec((tile, width), lambda t: (t, 0)),
            pl.BlockSpec((width, tile), lambda t: (0, t)),
            thin,
            thin,
        ],
        out_specs=[out, out],
        out_shape=[pltpu.HBM((tokens, width // 2), BF)] * 2,
        scratch_shapes=[pltpu.VMEM((tile, width), F32)],
        compiler_params=pltpu.CompilerParams(vmem_limit_bytes=40 * 1024 * 1024),
        cost_estimate=cost(5),
    )


def shifted(value, axis, step):
    size = lax.axis_size(axis)
    return lax.ppermute(value, axis, [(i, (i + step) % size) for i in range(size)])


def gather_start(value, axis):
    return [value] + [shifted(value, axis, k) for k in range(1, lax.axis_size(axis))]


def gather_finish(pieces, axis, where):
    size = len(pieces)
    me = lax.axis_index(axis)
    slots = []
    for j in range(size):
        which = lax.rem(me - j + size, size)
        chosen = pieces[0]
        for k in range(1, size):
            chosen = jnp.where(which == k, pieces[k], chosen)
        slots.append(chosen)
    return jnp.stack(slots, axis=where)


def total(parts):
    return sum(part.astype(F32) for part in parts)


def start(parts, axis, where):
    size = lax.axis_size(axis)
    me = lax.axis_index(axis)

    def at(index):
        return [lax.dynamic_index_in_dim(part, index, where, keepdims=False) for part in parts]

    out = [total(at(lax.rem(me + k, size))).astype(BF) for k in range(1, size)]
    return at(me), [shifted(part, axis, k) for k, part in enumerate(out, 1)], out


def start_joined(sums, axis):
    size = lax.axis_size(axis)
    me = lax.axis_index(axis)

    def at(index):
        values = [total([lax.dynamic_index_in_dim(p, index, 0, keepdims=False) for p in parts]) for parts in sums]
        return jnp.concatenate(values, axis=-1)

    return [at(me)] + [shifted(at(lax.rem(me + k, size)).astype(BF), axis, k) for k in range(1, size)]


def start_core(keep, send):
    halves, _, rows, cols = keep.shape
    shape = (halves, lax.axis_size("z"), lax.axis_size("x"), rows, cols)
    return [keep.reshape(shape)], [shifted(send, "core", 1).reshape(shape)]


def tie_sums(pending, *others):
    arrived, *others = tie([p[1] for p in pending], *others)
    return [p[0] + list(a) for p, a in zip(pending, arrived)], *others


def tie(*groups):
    return lax.optimization_barrier(groups)


def sum_pairs(value, axes):
    for axis in axes:
        size = lax.axis_size(axis)
        step = 1
        while step < size:
            value = value + lax.ppermute(value, axis, [(i, i ^ step) for i in range(size)])
            step *= 2
    return value


def shards(
    content_in,
    query_in,
    lengths,
    factor_order,
    buckets,
    w_qkv,
    b_qv,
    w_out,
    w_in,
    b_in,
    w_down,
    b_outs,
    norm_gain,
    norm_bias,
    rel_table,
    cot_content,
    cot_query,
):
    me = lax.axis_index("y")
    halves = lax.axis_size("y")
    each = content_in.shape[0] // halves
    assert each == 1
    seq = content_in.shape[1]
    width = content_in.shape[2]
    bucket_count, heads_here = rel_table.shape
    heads = heads_here * halves
    part = w_qkv.shape[2]
    ffn = w_in.shape[1]
    rows = w_in.shape[0]

    def mine(array):
        return lax.dynamic_index_in_dim(array, me, 0, keepdims=False)

    rest = lax.all_gather(
        jnp.concatenate([w_in, w_down.T], axis=1), ("y", "z", "x", "core"), axis=0
    ).reshape(halves, width, 2 * ffn)
    vectors = jnp.concatenate([b_qv, b_in.reshape(ffn // part, part)], axis=0)
    vectors = jnp.concatenate(
        [vectors, jnp.pad(rel_table, ((0, 0), (0, part - heads_here)))], axis=0
    )
    vectors = gather_finish(gather_start(vectors, "y"), "y", 0).astype(F32)
    qv_bias = vectors[:, :2]
    hidden_bias = vectors[:, 2 : 2 + ffn // part].reshape(halves, 1, ffn)
    table = vectors[:, 2 + ffn // part :, :heads_here]
    table = jnp.transpose(table, (0, 2, 1)).reshape(heads, bucket_count)
    table = jnp.pad(table, ((0, 0), (0, 128 - bucket_count)))
    vector_rows = jnp.concatenate([b_outs, norm_gain, norm_bias], axis=0).astype(F32)
    vector_rows = jnp.pad(vector_rows, ((0, 2), (0, 0)))

    core = lax.axis_index("core").astype(jnp.int32).reshape(1)
    content = mine(content_in)
    stacked = jnp.concatenate([content, mine(query_in)], axis=0)
    buckets_t = mine(buckets).T
    rank = mine(factor_order)
    length = lax.dynamic_slice_in_dim(lengths, me, 1, 0)
    bias = masked_bias(length, buckets_t, rank, table)

    shard = jnp.concatenate([*w_qkv, w_out.T], axis=1)
    wide = shard.shape[1] // 2
    chips = width // (2 * rows)
    along_z = gather_finish(gather_start(shard, "z"), "z", 0)
    one = gather_start(along_z[:, :, :wide], "x")
    two = gather_start(along_z[:, :, wide:], "y")
    one, two, bias = tie(one, two, bias)
    one = gather_start(gather_finish(one, "x", 1), "y")
    two = gather_start(gather_finish(two, "y", 0), "x")
    one = gather_finish(one, "y", 0).reshape(halves, chips, rows, wide)
    two = gather_finish(two, "x", 2).reshape(halves, chips, rows, wide)
    pieces = (one, two, shifted(one, "core", 1), shifted(two, "core", 1))
    q_t, k_t, v_t, heads_all = project(core, pieces, stacked, qv_bias, part)
    heads_all = heads_all.reshape(halves, width, 2 * wide)
    probs, ctx_t, inverse = attention(q_t, k_t, v_t, bias, (), heads, 0, heads // 2)

    cot = jnp.concatenate([mine(cot_content), mine(cot_query)], axis=0)
    output, low_t, active, slope, unit_one, inv_one, d_two, d_two_low, d_two_low_t, sums_two = up(
        ctx_t, stacked, cot, heads_all, rest, hidden_bias, vector_rows, part
    )
    content_got, query_got = shifted(output[:seq], "y", 1), shifted(output[seq:], "y", 1)
    below = down(d_two_low, d_two, slope, unit_one, inv_one, heads_all, rest, vector_rows, part)
    content_got, below = tie(content_got, below)
    d_hidden, d_one, d_one_low_t, dctx_t, sums_one, sums_hidden = below
    down_pair = outer(core, d_two_low_t, active, rows, after=(d_one_low_t,))
    down_pending = start_core(*down_pair)
    in_grads = outer_in(low_t, d_hidden, d_one_low_t, ctx_t, rows, after=down_pair)
    in_sum = lax.psum_scatter(in_grads, ("z", "x", "core"), scatter_dimension=0)
    sums_small = jnp.concatenate(
        [jnp.sum(sums_hidden, axis=(0, 1, 3)).reshape(-1)]
        + [s[i] for i in range(3) for s in (jnp.sum(sums_one, axis=(0, 2)), jnp.sum(sums_two, axis=(0, 2)))]
    )
    (down_sum,), query_got, in_grads = tie_sums([down_pending], query_got, in_grads)
    down_pending = start(down_sum, "y", 0)
    dq_t, dk_t, dv_t, held = attention_back(
        q_t, k_t, v_t, probs, inverse, ctx_t, dctx_t, (), heads, 0, heads // 2, after=down_pending[2]
    )
    pair = project_back(core, stacked, dq_t, dk_t, dv_t, halves, rows)
    (down_sum,), pair = tie_sums([down_pending], pair)
    down_pending = start(down_sum, "x", 1)
    pending = start_core(*pair)
    table_grad = table_back(buckets_t, held, bucket_count, after=tuple(pair) + tuple(down_pending[2]))
    (qkv_sum, down_sum), table_grad = tie_sums([pending, down_pending], table_grad)
    pending, down_pending = start(qkv_sum, "y", 0), start(down_sum, "z", 0)
    half = me.astype(jnp.int32).reshape(1)
    grad_in = inputs_back(
        half, heads_all, d_one, dq_t, dk_t, dv_t, after=pending[2] + down_pending[2]
    )
    table_grad = jnp.sum(table_grad.reshape(bucket_count, heads, -1), axis=2).T
    small = jnp.concatenate(
        [jnp.sum(g.astype(F32), axis=1) for g in (dq_t, dv_t)] + [table_grad.reshape(-1), sums_small]
    )
    small = sum_pairs(small.reshape(-1, 128), ("core",))
    outs = (output[:seq], content_got, output[seq:], query_got)
    (qkv_sum,), grad_in, small, outs = tie_sums([pending], grad_in, small, outs)
    pending = start(qkv_sum, "x", 1)
    grad_kept, grad_sent = grad_in
    grad_got = shifted(grad_sent, "y", 1)

    small = sum_pairs(small, ("z",))
    (qkv_sum,), small = tie_sums([pending], small)
    pending = start(qkv_sum, "z", 0)
    down_share = total(down_pending[0] + down_pending[1])
    in_pending = start([in_sum], "y", 0)
    in_share = total(in_pending[0] + in_pending[1])
    small = sum_pairs(small, ("x", "y")).reshape(-1)
    first_kept = me == 0
    outs = [
        jnp.stack([jnp.where(first_kept, a, b), jnp.where(first_kept, b, a)])
        for a, b in (outs[:2], outs[2:])
    ]
    grad_ins = jnp.stack(
        [jnp.where(first_kept, grad_kept, grad_got), jnp.where(first_kept, grad_got, grad_kept)]
    ).reshape(halves, 2, seq, width // halves)
    qkv_share = total(pending[0] + pending[1])
    ends = [2 * width, 2 * width + heads * bucket_count]
    ends.append(ends[1] + halves * ffn)
    grad_b_qv = mine(jnp.transpose(small[: ends[0]].reshape(2, halves, part), (1, 0, 2)))
    grad_table = mine(small[ends[0] : ends[1]].reshape(halves, heads_here, bucket_count)).T
    grad_b_in = mine(small[ends[1] : ends[2]].reshape(halves, ffn))
    pairs = small[ends[2] :].reshape(3, 2, width)
    return (
        outs[0],
        outs[1],
        grad_ins[:, 0],
        grad_ins[:, 1],
        jnp.transpose(qkv_share.reshape(rows, 3, part), (1, 0, 2)),
        grad_b_qv,
        in_share[:, ffn:].T,
        in_share[:, :ffn],
        grad_b_in,
        down_share.T,
        pairs[0],
        pairs[1],
        pairs[2],
        grad_table,
    )


def solution(mesh):
    count = mesh.shape["dp"] // 2
    depth = 4 if count % 4 == 0 else 1
    while count // depth > depth:
        depth *= 2
    grid = mesh.devices.reshape(depth, count // depth, 2, mesh.shape["tensor"])
    fine = Mesh(grid, ("z", "x", "core", "y"))
    dp = ("z", "x", "core")
    return jax.shard_map(
        shards,
        mesh=fine,
        in_specs=(
            P(dp, None, None),
            P(dp, None, None),
            P(dp),
            P(dp, None),
            P(dp, None, None),
            P(None, dp, "y"),
            P(None, "y"),
            P("y", dp),
            P(dp, "y"),
            P("y"),
            P("y", dp),
            P(),
            P(),
            P(),
            P(None, "y"),
            P(dp, None, None),
            P(dp, None, None),
        ),
        out_specs=(
            P(dp, None, None),
            P(dp, None, None),
            P(dp, None, "y"),
            P(dp, None, "y"),
            P(None, dp, "y"),
            P(None, "y"),
            P("y", dp),
            P(dp, "y"),
            P("y"),
            P("y", dp),
            P(),
            P(),
            P(),
            P(None, "y"),
        ),
        check_vma=False,
    )
```

```python
import functools

import jax
import jax.numpy as jnp
from jax import lax
from jax.experimental import pallas as pl
from jax.experimental.pallas import tpu as pltpu
from jax.sharding import Mesh, PartitionSpec as P

EPSILON = 1e-05


def cost(us):
    return pl.CostEstimate(flops=int(us * 1e7), bytes_accessed=int(us * 1e4), transcendentals=0)

NEG = -1e30
BF = jnp.bfloat16
F32 = jnp.float32


def dot(a, b, dims):
    return lax.dot_general(a, b, (dims, ((), ())), preferred_element_type=F32)


NN = ((1,), (0,))
NT = ((1,), (1,))
TN = ((0,), (0,))


def bias_kernel(len_ref, buckets_ref, rank_row_ref, rank_col_ref, table_ref, out_ref):
    rows, cols = buckets_ref.shape
    heads = table_ref.shape[0]
    start = pl.program_id(0) * rows
    key = start + lax.broadcasted_iota(jnp.int32, (rows, cols), 0)
    query = lax.broadcasted_iota(jnp.int32, (rows, cols), 1)
    valid = key < len_ref[0]
    rank_key = rank_col_ref[...]
    rank_query = rank_row_ref[...]
    content = (valid & (rank_key <= rank_query)) | (key == query)
    stream = (valid & (rank_key < rank_query)) | (key == 0)
    index = buckets_ref[...]
    for head in range(heads):
        row = jnp.broadcast_to(table_ref[head : head + 1, :], (rows, 128))
        bias = jnp.concatenate(
            [
                jnp.take_along_axis(
                    row, index[:, c : c + 128], axis=1, mode="promise_in_bounds"
                )
                for c in range(0, cols, 128)
            ],
            axis=1,
        )
        out_ref[head, :, :cols] = jnp.where(content, bias, NEG).astype(BF)
        out_ref[head, :, cols:] = jnp.where(stream, bias, NEG).astype(BF)


def masked_bias(length, buckets_t, rank, table, after=()):
    seq = buckets_t.shape[0]
    heads = table.shape[0]
    step = 128
    return call(
        bias_kernel,
        after,
        [length, buckets_t, rank.reshape(1, seq), rank.reshape(seq, 1), table],
        grid=(seq // step,),
        in_specs=[
            pl.BlockSpec(memory_space=pltpu.SMEM),
            pl.BlockSpec((step, seq), lambda g: (g, 0)),
            pl.BlockSpec((1, seq), lambda g: (0, 0)),
            pl.BlockSpec((step, 1), lambda g: (g, 0)),
            pl.BlockSpec((heads, 128), lambda g: (0, 0)),
        ],
        out_specs=pl.BlockSpec((heads, step, 2 * seq), lambda g: (0, g, 0)),
        out_shape=jax.ShapeDtypeStruct((heads, seq, 2 * seq), BF),
        cost_estimate=cost(9),
    )


def forward_kernel(q_ref, k_ref, v_ref, bias_ref, probs_ref, ctx_ref, inv_ref, *, tile):
    count = bias_ref.shape[0]
    size = q_ref.shape[0] // count
    for head in range(count):
        rows = slice(head * size, (head + 1) * size)
        keys = (k_ref[rows, :].astype(F32) * 0.125).astype(BF)
        for t in range(q_ref.shape[1] // tile):
            at = slice(t * tile, (t + 1) * tile)
            scores = dot(keys, q_ref[rows, at], TN) + bias_ref[head, :, at].astype(F32)
            high = jnp.max(scores, axis=0, keepdims=True)
            weight = jnp.exp(scores - high)
            inverse = 1.0 / jnp.sum(weight, axis=0, keepdims=True)
            low = weight.astype(BF)
            probs_ref[head, :, at] = low
            ctx_ref[rows, at] = (dot(v_ref[rows, :], low, NN) * inverse).astype(BF)
            inv_ref[head, :, at] = inverse


def attention(q_t, k_t, v_t, bias, before, heads, begin, steps, tile=1024, count=2, after=()):
    width, both = q_t.shape
    seq = k_t.shape[1]
    size = width // heads * count
    thin = pl.BlockSpec((size, seq), lambda h: (h + begin, 0))
    wide = pl.BlockSpec((size, both), lambda h: (h + begin, 0))
    square = pl.BlockSpec((count, seq, both), lambda h: (h + begin, 0, 0))

    def kernel(q_ref, k_ref, v_ref, bias_ref, *refs):
        forward_kernel(q_ref, k_ref, v_ref, bias_ref, *refs[-3:], tile=tile)

    return call(
        kernel,
        after,
        [q_t, k_t, v_t, bias, *before],
        grid=(steps,),
        in_specs=[wide, thin, thin, square] + [pl.BlockSpec(memory_space=pl.ANY)] * len(before),
        out_specs=[square, wide, pl.BlockSpec((count, 1, both), lambda h: (h + begin, 0, 0))],
        out_shape=[
            pltpu.HBM((heads, seq, both), BF),
            pltpu.HBM((width, both), BF),
            pltpu.HBM((heads, 1, both), F32),
        ],
        input_output_aliases={4 + i: i for i in range(len(before))},
        compiler_params=pltpu.CompilerParams(vmem_limit_bytes=48 * 1024 * 1024),
        cost_estimate=cost(3 * steps),
    )


def backward_kernel(q_ref, k_ref, v_ref, p_ref, inv_ref, ctx_ref, dctx_ref, *refs, tile):
    dq_ref, dk_ref, dv_ref, held_ref = refs[-4:]
    count = p_ref.shape[0]
    size, seq = k_ref.shape[0] // count, k_ref.shape[1]
    group = held_ref.shape[1] // count
    for head in range(count):
        rows = slice(head * size, (head + 1) * size)
        queries = q_ref[rows, :]
        keys = k_ref[rows, :]
        values = v_ref[rows, :]
        grad = dctx_ref[rows, :].astype(F32) * inv_ref[head]
        inner = jnp.sum(grad * ctx_ref[rows, :].astype(F32), axis=0, keepdims=True)
        grad = grad.astype(BF)
        dk = jnp.zeros(keys.shape, F32)
        dv = jnp.zeros(keys.shape, F32)
        for t in range(seq // tile):
            both = None
            for stream in range(2):
                lo = stream * seq + t * tile
                at = slice(lo, lo + tile)
                weight = p_ref[head, :, at]
                part = dot(values, grad[:, at], TN) - inner[:, at]
                ds = weight.astype(F32) * part
                low = ds.astype(BF)
                dv += dot(grad[:, at], weight, NT)
                dk += dot(queries[:, at], low, NT)
                dq_ref[rows, at] = (dot(keys, low, NN) * 0.125).astype(BF)
                both = ds if both is None else both + ds
            held_ref[:, head * group : (head + 1) * group, t * tile : (t + 1) * tile] = (
                both.astype(BF).reshape(seq // group, group, tile)
            )
        dk_ref[rows, :] = (dk * 0.125).astype(BF)
        dv_ref[rows, :] = dv.astype(BF)


def attention_back(
    q_t, k_t, v_t, probs, inverse, ctx_t, dctx_t, before, heads, begin, steps, count=2, group=16, tile=512, after=()
):
    width, both = q_t.shape
    seq = k_t.shape[1]
    size = width // heads * count
    wide = pl.BlockSpec((size, both), lambda h: (h + begin, 0))
    thin = pl.BlockSpec((size, seq), lambda h: (h + begin, 0))
    operands = [q_t, k_t, v_t, probs, inverse, ctx_t, dctx_t, *before]
    return call(
        functools.partial(backward_kernel, tile=tile),
        after,
        operands,
        grid=(steps,),
        in_specs=[
            wide,
            thin,
            thin,
            pl.BlockSpec((count, seq, both), lambda h: (h + begin, 0, 0)),
            pl.BlockSpec((count, 1, both), lambda h: (h + begin, 0, 0)),
            wide,
            wide,
        ]
        + [pl.BlockSpec(memory_space=pl.ANY)] * len(before),
        out_specs=[
            wide,
            thin,
            thin,
            pl.BlockSpec((seq // group, count * group, seq), lambda h: (0, h + begin, 0)),
        ],
        out_shape=[
            pltpu.HBM((width, both), BF),
            pltpu.HBM((width, seq), BF),
            pltpu.HBM((width, seq), BF),
            pltpu.HBM((seq // group, heads * group, seq), BF),
        ],
        input_output_aliases={7 + i: i for i in range(len(before))},
        compiler_params=pltpu.CompilerParams(vmem_limit_bytes=56 * 1024 * 1024),
        cost_estimate=cost(1e4 * steps),
    )


def table_kernel(buckets_ref, *refs, buckets, group):
    held_ref, out_ref, total = refs
    step, steps = pl.program_id(0), pl.num_programs(0)
    parts = buckets_ref.shape[0] // group
    index = buckets_ref[...].astype(F32).astype(BF)
    hot = jnp.concatenate(
        [
            jnp.concatenate(
                [
                    jnp.where(index[p * group : (p + 1) * group] == jnp.asarray(n, BF), 1.0, 0.0).astype(BF)
                    for n in range(buckets)
                ],
                axis=0,
            )
            for p in range(parts)
        ],
        axis=1,
    )
    held = jnp.concatenate([held_ref[p] for p in range(parts)], axis=1)
    value = dot(hot, held, NT)

    @pl.when(step == 0)
    def _():
        total[...] = value

    @pl.when(step > 0)
    def _():
        total[...] += value

    @pl.when(step == steps - 1)
    def _():
        value = total[...]
        row = lax.broadcasted_iota(jnp.int32, value.shape, 0) % group
        col = lax.broadcasted_iota(jnp.int32, value.shape, 1) % group
        kept = jnp.where(row == col, value, 0.0)
        out_ref[...] = jnp.sum(kept.reshape(buckets, group, value.shape[1]), axis=1)


def table_back(buckets_t, held, buckets, group=16, parts=8, after=()):
    seq = buckets_t.shape[0]
    cols = held.shape[1]
    return call(
        functools.partial(table_kernel, buckets=buckets, group=group),
        after,
        [buckets_t, held],
        grid=(seq // (group * parts),),
        in_specs=[
            pl.BlockSpec((group * parts, seq), lambda g: (g, 0)),
            pl.BlockSpec((parts, cols, seq), lambda g: (g, 0, 0)),
        ],
        out_specs=whole((buckets, cols)),
        out_shape=jax.ShapeDtypeStruct((buckets, cols), F32),
        scratch_shapes=[pltpu.VMEM((buckets * group, cols), F32)],
        compiler_params=pltpu.CompilerParams(vmem_limit_bytes=40 * 1024 * 1024),
        cost_estimate=cost(6),
    )


def call(kernel, after, operands, *, in_specs, **settings):
    count = len(operands)

    def body(*refs):
        kernel(*refs[:count], *refs[count + len(after) :])

    operands = [
        pltpu.with_memory_space_constraint(o, pltpu.HBM) if s.memory_space is None and o.size > 1 << 16 else o
        for o, s in zip(operands, in_specs)
    ]
    anywhere = [pl.BlockSpec(memory_space=pl.ANY)] * len(after)
    return pl.pallas_call(body, in_specs=in_specs + anywhere, **settings)(*operands, *after)


def whole(shape):
    return pl.BlockSpec(shape, lambda *_: (0,) * len(shape))


def once(shape, at):
    return pl.BlockSpec(shape, lambda *_: at, pipeline_mode=pl.Buffered(1))


def unit(value):
    centred = value - jnp.mean(value, axis=-1, keepdims=True)
    inverse = lax.rsqrt(jnp.mean(centred * centred, axis=-1, keepdims=True) + EPSILON)
    return centred * inverse, inverse


def unit_back(grad, along, inverse):
    mean = jnp.mean(grad, axis=-1, keepdims=True)
    slope = jnp.mean(grad * along, axis=-1, keepdims=True)
    return (grad - mean - along * slope) * inverse


def column_sum(value):
    rows = value.shape[0]
    return jnp.sum(value.reshape(rows // 8, 8, value.shape[1]), axis=0)


def up_kernel(
    ctx_ref, x_ref, cot_ref, wo_ref, wi_ref, wd_ref, bi_ref, rows_ref,
    out_ref, lowt_ref, act_ref, slope_ref, unit_ref, inv_ref, dres_ref, dlow_ref, dlowt_ref, sums_ref,
    *, chunk, part_rows,
):
    halves, width, part = wo_ref.shape
    ffn = wi_ref.shape[2]
    row = lambda i: rows_ref[i : i + 1, :]
    parts = [slice(r, r + part_rows) for r in range(0, x_ref.shape[0], part_rows)]
    resids, lows = [], []
    for at in parts:
        resid = x_ref[at, :].astype(F32) + row(0)
        for y in range(halves):
            resid += dot(ctx_ref[y * part : (y + 1) * part, at].T, wo_ref[y], NT)
        along, inverse = unit(resid)
        unit_ref[at, :] = along
        inv_ref[at, :] = inverse
        normed = along * row(2) + row(4)
        low = normed.astype(BF)
        lowt_ref[:, at] = low.T
        resids.append(normed + row(1))
        lows.append(low)
    for y in range(halves):
        for n, at in enumerate(parts):
            for c in range(0, ffn, chunk):
                cols = slice(c, c + chunk)
                hidden = dot(lows[n], wi_ref[y, :, cols], NN) + bi_ref[y, :, cols]
                cdf = 0.5 * lax.erf(hidden * 0.7071067811865476) + 0.5
                density = jnp.exp(hidden * hidden * -0.5) * 0.3989422804014327
                act_ref[y, at, cols] = (hidden * cdf).astype(BF)
                slope_ref[y, at, cols] = (cdf + hidden * density).astype(BF)
            resids[n] += dot(act_ref[y, at, :], wd_ref[y], NT)
    sums = [0.0, 0.0, 0.0]
    for n, at in enumerate(parts):
        along, inverse = unit(resids[n])
        out_ref[at, :] = (along * row(3) + row(5)).astype(BF)
        cot = cot_ref[at, :].astype(F32)
        dres = unit_back(cot * row(3), along, inverse)
        dres_ref[at, :] = dres
        dlow = dres.astype(BF)
        dlow_ref[at, :] = dlow
        dlowt_ref[:, at] = dlow.T
        for i, value in enumerate((dres, cot * along, cot)):
            sums[i] += column_sum(value)
    for i in range(3):
        sums_ref[0, i] = sums[i]


def up(ctx_t, stacked, cot, heads_all, rest, hidden_bias, rows, part, tile=256, chunk=512, part_rows=256, after=()):
    tokens, width = stacked.shape
    halves = rest.shape[0]
    ffn = rest.shape[2] // 2
    tall = pl.BlockSpec((width, tile), lambda t: (0, t))
    flat = pl.BlockSpec((tile, width), lambda t: (t, 0))
    wide = pl.BlockSpec((halves, tile, ffn), lambda t: (0, t, 0))
    sds = pltpu.HBM
    return call(
        functools.partial(up_kernel, chunk=chunk, part_rows=part_rows),
        after,
        [ctx_t, stacked, cot, heads_all, rest, rest, hidden_bias, rows],
        grid=(tokens // tile,),
        in_specs=[
            tall,
            flat,
            flat,
            once((halves, width, part), (0, 0, 3)),
            once((halves, width, ffn), (0, 0, 0)),
            once((halves, width, ffn), (0, 0, 1)),
            whole((halves, 1, ffn)),
            whole(rows.shape),
        ],
        out_specs=[
            flat, tall, wide, wide, flat, pl.BlockSpec((tile, 1), lambda t: (t, 0)), flat, flat, tall,
            pl.BlockSpec((1, 3, 8, width), lambda t: (t, 0, 0, 0)),
        ],
        out_shape=[
            sds((tokens, width), BF),
            sds((width, tokens), BF),
            sds((halves, tokens, ffn), BF),
            sds((halves, tokens, ffn), BF),
            sds((tokens, width), F32),
            sds((tokens, 1), F32),
            sds((tokens, width), F32),
            sds((tokens, width), BF),
            sds((width, tokens), BF),
            sds((tokens // tile, 3, 8, width), F32),
        ],
        compiler_params=pltpu.CompilerParams(vmem_limit_bytes=58 * 1024 * 1024),
        cost_estimate=cost(20),
    )


def down_kernel(
    dlow_ref, dres_ref, slope_ref, unit_ref, inv_ref, wo_ref, wi_ref, wd_ref, rows_ref,
    dhid_ref, done_ref, dot_ref, dctx_ref, sums_ref, hsum_ref, *, chunk, part_rows,
):
    halves, width, part = wo_ref.shape
    ffn = wi_ref.shape[2]
    parts = [slice(r, r + part_rows) for r in range(0, dlow_ref.shape[0], part_rows)]
    dnorms = [dres_ref[at, :] for at in parts]
    for y in range(halves):
        for n, at in enumerate(parts):
            for c in range(0, ffn, chunk):
                cols = slice(c, c + chunk)
                dhid = dot(dlow_ref[at, :], wd_ref[y, :, cols], NN) * slope_ref[y, at, cols].astype(F32)
                hsum_ref[0, n, y, :, cols] = column_sum(dhid)
                dhid_ref[y, at, cols] = dhid.astype(BF)
            dnorms[n] += dot(dhid_ref[y, at, :], wi_ref[y], NT)
    sums = [0.0, 0.0, 0.0]
    for n, at in enumerate(parts):
        dnorm = dnorms[n]
        along = unit_ref[at, :]
        done = unit_back(dnorm * rows_ref[2:3, :], along, inv_ref[at, :])
        done_ref[at, :] = done
        low = done.astype(BF)
        dot_ref[:, at] = low.T
        for y in range(halves):
            dctx_ref[y * part : (y + 1) * part, at] = dot(low, wo_ref[y], NN).astype(BF).T
        for i, value in enumerate((done, dnorm * along, dnorm)):
            sums[i] += column_sum(value)
    for i in range(3):
        sums_ref[0, i] = sums[i]


def down(dlow, dres, slope, along, inverse, heads_all, rest, rows, part, tile=256, chunk=512, part_rows=256, after=()):
    tokens, width = dlow.shape
    halves = rest.shape[0]
    ffn = rest.shape[2] // 2
    tall = pl.BlockSpec((width, tile), lambda t: (0, t))
    flat = pl.BlockSpec((tile, width), lambda t: (t, 0))
    wide = pl.BlockSpec((halves, tile, ffn), lambda t: (0, t, 0))
    sds = pltpu.HBM
    return call(
        functools.partial(down_kernel, chunk=chunk, part_rows=part_rows),
        after,
        [dlow, dres, slope, along, inverse, heads_all, rest, rest, rows],
        grid=(tokens // tile,),
        in_specs=[
            flat,
            flat,
            wide,
            flat,
            pl.BlockSpec((tile, 1), lambda t: (t, 0)),
            once((halves, width, part), (0, 0, 3)),
            once((halves, width, ffn), (0, 0, 0)),
            once((halves, width, ffn), (0, 0, 1)),
            whole(rows.shape),
        ],
        out_specs=[
            wide, flat, tall, tall,
            pl.BlockSpec((1, 3, 8, width), lambda t: (t, 0, 0, 0)),
            pl.BlockSpec((1, tile // part_rows, halves, 8, ffn), lambda t: (t, 0, 0, 0, 0)),
        ],
        out_shape=[
            sds((halves, tokens, ffn), BF),
            sds((tokens, width), F32),
            sds((width, tokens), BF),
            sds((width, tokens), BF),
            sds((tokens // tile, 3, 8, width), F32),
            sds((tokens // tile, tile // part_rows, halves, 8, ffn), F32),
        ],
        compiler_params=pltpu.CompilerParams(vmem_limit_bytes=58 * 1024 * 1024),
        cost_estimate=cost(18),
    )


def put_rows(core, value, keep_ref, send_ref, at):
    chips, rows = keep_ref.shape[1], keep_ref.shape[2]
    value = value.reshape(chips, 2, rows, value.shape[1])

    @pl.when(core == 0)
    def _():
        keep_ref[at] = value[:, 0]
        send_ref[at] = value[:, 1]

    @pl.when(core != 0)
    def _():
        keep_ref[at] = value[:, 1]
        send_ref[at] = value[:, 0]


def outer_kernel(core_ref, left_ref, right_ref, keep_ref, send_ref):
    value = dot(left_ref[...], right_ref[0], NN).astype(BF)
    put_rows(core_ref[0], value, keep_ref, send_ref, 0)


def outer(core, left_t, right, rows, tile=768, after=()):
    width, tokens = left_t.shape
    halves, _, cols = right.shape
    block = pl.BlockSpec((1, width // (2 * rows), rows, tile), lambda y, c: (y, 0, 0, c))
    shape = jax.ShapeDtypeStruct((halves, width // (2 * rows), rows, cols), BF)
    return call(
        outer_kernel,
        after,
        [core, left_t, right],
        grid=(halves, cols // tile),
        in_specs=[
            pl.BlockSpec(memory_space=pltpu.SMEM),
            whole(left_t.shape),
            pl.BlockSpec((1, tokens, tile), lambda y, c: (y, 0, c)),
        ],
        out_specs=[block, block],
        out_shape=[shape, shape],
        cost_estimate=cost(5),
    )


def outer_in_kernel(low_ref, dhid_ref, dot_ref, ctx_ref, out_ref):
    owners, _, rows, _ = out_ref.shape
    ffn = dhid_ref.shape[2]
    half = ffn // 2
    for c in (0, half):
        value = dot(low_ref[...], dhid_ref[0, :, c : c + half], NN).astype(BF)
        out_ref[:, 0, :, c : c + half] = value.reshape(owners, rows, half)
    value = dot(dot_ref[...], ctx_ref[...], NT).astype(BF)
    out_ref[:, 0, :, ffn:] = value.reshape(owners, rows, value.shape[1])


def outer_in(low_t, dhid, do_t, ctx_t, rows, after=()):
    width, tokens = low_t.shape
    halves, _, ffn = dhid.shape
    part = ctx_t.shape[0] // halves
    owners = width // rows
    return call(
        outer_in_kernel,
        after,
        [low_t, dhid, do_t, ctx_t],
        grid=(halves,),
        in_specs=[
            whole(low_t.shape),
            pl.BlockSpec((1, tokens, ffn), lambda y: (y, 0, 0)),
            whole(do_t.shape),
            pl.BlockSpec((part, tokens), lambda y: (y, 0)),
        ],
        out_specs=pl.BlockSpec((owners, 1, rows, ffn + part), lambda y: (0, y, 0, 0)),
        out_shape=pltpu.HBM((owners, halves, rows, ffn + part), BF),
        compiler_params=pltpu.CompilerParams(vmem_limit_bytes=48 * 1024 * 1024),
        cost_estimate=cost(6),
    )


def project_kernel(core_ref, own_a, own_b, other_a, other_b, x_ref, bias_ref, q_ref, k_ref, v_ref, w_ref):
    core = core_ref[0]
    cut = own_a.shape[3]
    width = x_ref.shape[1]
    part, seq = k_ref.shape
    w_ref[0, :, core, :, :cut] = own_a[0]
    w_ref[0, :, core, :, cut:] = own_b[0]
    w_ref[0, :, 1 - core, :, :cut] = other_a[0]
    w_ref[0, :, 1 - core, :, cut:] = other_b[0]
    weights = w_ref[0, :, :, :, : 3 * part].reshape(width, 3 * part)
    q = dot(x_ref[...], weights[:, :part], NN) + bias_ref[0, 0:1, :]
    q_ref[...] = q.astype(BF).T
    kv = dot(x_ref[:seq, :], weights[:, part:], NN)
    k_ref[...] = kv[:, :part].astype(BF).T
    v_ref[...] = (kv[:, part:] + bias_ref[0, 1:2, :]).astype(BF).T


def project(core, pieces, stacked, bias, part, after=()):
    tokens, width = stacked.shape
    halves, chips, rows, cut = pieces[0].shape
    cols = cut + pieces[1].shape[3]
    seq = tokens // 2
    sds = pltpu.HBM
    one = pl.BlockSpec((1, chips, rows, cut), lambda y: (y, 0, 0, 0))
    two = pl.BlockSpec((1, chips, rows, cols - cut), lambda y: (y, 0, 0, 0))
    return call(
        project_kernel,
        after,
        [core, *pieces, stacked, bias],
        grid=(halves,),
        in_specs=[
            pl.BlockSpec(memory_space=pltpu.SMEM), one, two, one, two,
            whole(stacked.shape),
            pl.BlockSpec((1, 2, part), lambda y: (y, 0, 0)),
        ],
        out_specs=[
            pl.BlockSpec((part, tokens), lambda y: (y, 0)),
            pl.BlockSpec((part, seq), lambda y: (y, 0)),
            pl.BlockSpec((part, seq), lambda y: (y, 0)),
            pl.BlockSpec((1, chips, 2, rows, cols), lambda y: (y, 0, 0, 0, 0)),
        ],
        out_shape=[
            sds((width, tokens), BF),
            sds((width, seq), BF),
            sds((width, seq), BF),
            sds((halves, chips, 2, rows, cols), BF),
        ],
        compiler_params=pltpu.CompilerParams(vmem_limit_bytes=40 * 1024 * 1024),
        cost_estimate=cost(6),
    )


def project_back_kernel(core_ref, x_ref, dq_ref, dk_ref, dv_ref, keep_ref, send_ref, xt_ref):
    @pl.when(pl.program_id(0) == 0)
    def _():
        xt_ref[...] = x_ref[...].T

    values = []
    for ref in (dq_ref, dk_ref, dv_ref):
        tokens = ref.shape[1]
        values.append(dot(xt_ref[:, :tokens], ref[...], NT).astype(BF))
    put_rows(core_ref[0], jnp.concatenate(values, axis=1), keep_ref, send_ref, 0)


def project_back(core, stacked, dq_t, dk_t, dv_t, halves, rows, after=()):
    tokens, width = stacked.shape
    chips = width // (2 * rows)
    part = width // halves
    block = pl.BlockSpec((1, chips, rows, 3 * part), lambda y: (y, 0, 0, 0))
    shape = pltpu.HBM((halves, chips, rows, 3 * part), BF)
    return call(
        project_back_kernel,
        after,
        [core, stacked, dq_t, dk_t, dv_t],
        grid=(halves,),
        in_specs=[pl.BlockSpec(memory_space=pltpu.SMEM), whole(stacked.shape)]
        + [pl.BlockSpec((part, g.shape[1]), lambda y: (y, 0)) for g in (dq_t, dk_t, dv_t)],
        out_specs=[block, block],
        out_shape=[shape, shape],
        scratch_shapes=[pltpu.VMEM((width, tokens), BF)],
        compiler_params=pltpu.CompilerParams(vmem_limit_bytes=40 * 1024 * 1024),
        cost_estimate=cost(5),
    )


def inputs_kernel(half_ref, w_ref, done_ref, dq_ref, dk_ref, dv_ref, keep_ref, send_ref, sum_ref):
    step, steps = pl.program_id(0), pl.num_programs(0)
    halves, width, cols = w_ref.shape
    part = cols // 3
    total = done_ref[...]
    for y in range(halves):
        total += dot(dq_ref[y * part : (y + 1) * part, :].T, w_ref[y, :, :part], NT)
    sum_ref[...] = total

    @pl.when(step < steps // 2)
    def _():
        extra = 0.0
        for y in range(halves):
            at = slice(y * part, (y + 1) * part)
            extra += dot(dk_ref[at, :].T, w_ref[y, :, part : 2 * part], NT)
            extra += dot(dv_ref[at, :].T, w_ref[y, :, 2 * part :], NT)
        sum_ref[...] += extra

    half = width // 2

    @pl.when(half_ref[0] == 0)
    def _():
        keep_ref[...] = sum_ref[:, :half].astype(BF)
        send_ref[...] = sum_ref[:, half:].astype(BF)

    @pl.when(half_ref[0] != 0)
    def _():
        keep_ref[...] = sum_ref[:, half:].astype(BF)
        send_ref[...] = sum_ref[:, :half].astype(BF)


def inputs_back(half, weights, done, dq_t, dk_t, dv_t, tile=256, after=()):
    tokens, width = done.shape
    last = tokens // (2 * tile) - 1
    thin = pl.BlockSpec((width, tile), lambda t: (0, jnp.minimum(t, last)))
    out = pl.BlockSpec((tile, width // 2), lambda t: (t, 0))
    return call(
        inputs_kernel,
        after,
        [half, weights, done, dq_t, dk_t, dv_t],
        grid=(tokens // tile,),
        in_specs=[
            pl.BlockSpec(memory_space=pltpu.SMEM),
            once((weights.shape[0], width, 3 * width // weights.shape[0]), (0, 0, 0)),
            pl.BlockSpec((tile, width), lambda t: (t, 0)),
            pl.BlockSpec((width, tile), lambda t: (0, t)),
            thin,
            thin,
        ],
        out_specs=[out, out],
        out_shape=[pltpu.HBM((tokens, width // 2), BF)] * 2,
        scratch_shapes=[pltpu.VMEM((tile, width), F32)],
        compiler_params=pltpu.CompilerParams(vmem_limit_bytes=40 * 1024 * 1024),
        cost_estimate=cost(5),
    )


def shifted(value, axis, step):
    size = lax.axis_size(axis)
    return lax.ppermute(value, axis, [(i, (i + step) % size) for i in range(size)])


def gather_start(value, axis):
    return [value] + [shifted(value, axis, k) for k in range(1, lax.axis_size(axis))]


def gather_finish(pieces, axis, where):
    size = len(pieces)
    me = lax.axis_index(axis)
    slots = []
    for j in range(size):
        which = lax.rem(me - j + size, size)
        chosen = pieces[0]
        for k in range(1, size):
            chosen = jnp.where(which == k, pieces[k], chosen)
        slots.append(chosen)
    return jnp.stack(slots, axis=where)


def total(parts):
    return sum(part.astype(F32) for part in parts)


def start(parts, axis, where):
    size = lax.axis_size(axis)
    me = lax.axis_index(axis)

    def at(index):
        return [lax.dynamic_index_in_dim(part, index, where, keepdims=False) for part in parts]

    out = [total(at(lax.rem(me + k, size))).astype(BF) for k in range(1, size)]
    return at(me), [shifted(part, axis, k) for k, part in enumerate(out, 1)], out


def start_joined(sums, axis):
    size = lax.axis_size(axis)
    me = lax.axis_index(axis)

    def at(index):
        values = [total([lax.dynamic_index_in_dim(p, index, 0, keepdims=False) for p in parts]) for parts in sums]
        return jnp.concatenate(values, axis=-1)

    return [at(me)] + [shifted(at(lax.rem(me + k, size)).astype(BF), axis, k) for k in range(1, size)]


def start_core(keep, send):
    halves, _, rows, cols = keep.shape
    shape = (halves, lax.axis_size("z"), lax.axis_size("x"), rows, cols)
    return [keep.reshape(shape)], [shifted(send, "core", 1).reshape(shape)]


def tie_sums(pending, *others):
    arrived, *others = tie([p[1] for p in pending], *others)
    return [p[0] + list(a) for p, a in zip(pending, arrived)], *others


def tie(*groups):
    return lax.optimization_barrier(groups)


def sum_pairs(value, axes):
    for axis in axes:
        size = lax.axis_size(axis)
        step = 1
        while step < size:
            value = value + lax.ppermute(value, axis, [(i, i ^ step) for i in range(size)])
            step *= 2
    return value


def shards(
    content_in,
    query_in,
    lengths,
    factor_order,
    buckets,
    w_qkv,
    b_qv,
    w_out,
    w_in,
    b_in,
    w_down,
    b_outs,
    norm_gain,
    norm_bias,
    rel_table,
    cot_content,
    cot_query,
):
    me = lax.axis_index("y")
    halves = lax.axis_size("y")
    each = content_in.shape[0] // halves
    assert each == 1
    seq = content_in.shape[1]
    width = content_in.shape[2]
    bucket_count, heads_here = rel_table.shape
    heads = heads_here * halves
    part = w_qkv.shape[2]
    ffn = w_in.shape[1]
    rows = w_in.shape[0]

    def mine(array):
        return lax.dynamic_index_in_dim(array, me, 0, keepdims=False)

    rest = lax.all_gather(
        jnp.concatenate([w_in, w_down.T], axis=1), ("y", "z", "x", "core"), axis=0
    ).reshape(halves, width, 2 * ffn)
    vectors = jnp.concatenate([b_qv, b_in.reshape(ffn // part, part)], axis=0)
    vectors = jnp.concatenate(
        [vectors, jnp.pad(rel_table, ((0, 0), (0, part - heads_here)))], axis=0
    )
    vectors = gather_finish(gather_start(vectors, "y"), "y", 0).astype(F32)
    qv_bias = vectors[:, :2]
    hidden_bias = vectors[:, 2 : 2 + ffn // part].reshape(halves, 1, ffn)
    table = vectors[:, 2 + ffn // part :, :heads_here]
    table = jnp.transpose(table, (0, 2, 1)).reshape(heads, bucket_count)
    table = jnp.pad(table, ((0, 0), (0, 128 - bucket_count)))
    vector_rows = jnp.concatenate([b_outs, norm_gain, norm_bias], axis=0).astype(F32)
    vector_rows = jnp.pad(vector_rows, ((0, 2), (0, 0)))

    core = lax.axis_index("core").astype(jnp.int32).reshape(1)
    content = mine(content_in)
    stacked = jnp.concatenate([content, mine(query_in)], axis=0)
    buckets_t = mine(buckets).T
    rank = mine(factor_order)
    length = lax.dynamic_slice_in_dim(lengths, me, 1, 0)
    bias = masked_bias(length, buckets_t, rank, table)

    shard = jnp.concatenate([*w_qkv, w_out.T], axis=1)
    wide = shard.shape[1] // 2
    chips = width // (2 * rows)
    along_z = gather_finish(gather_start(shard, "z"), "z", 0)
    one = gather_start(along_z[:, :, :wide], "x")
    two = gather_start(along_z[:, :, wide:], "y")
    one, two, bias = tie(one, two, bias)
    one = gather_start(gather_finish(one, "x", 1), "y")
    two = gather_start(gather_finish(two, "y", 0), "x")
    one = gather_finish(one, "y", 0).reshape(halves, chips, rows, wide)
    two = gather_finish(two, "x", 2).reshape(halves, chips, rows, wide)
    pieces = (one, two, shifted(one, "core", 1), shifted(two, "core", 1))
    q_t, k_t, v_t, heads_all = project(core, pieces, stacked, qv_bias, part)
    heads_all = heads_all.reshape(halves, width, 2 * wide)
    probs, ctx_t, inverse = attention(q_t, k_t, v_t, bias, (), heads, 0, heads // 2)

    cot = jnp.concatenate([mine(cot_content), mine(cot_query)], axis=0)
    output, low_t, active, slope, unit_one, inv_one, d_two, d_two_low, d_two_low_t, sums_two = up(
        ctx_t, stacked, cot, heads_all, rest, hidden_bias, vector_rows, part
    )
    output_got = shifted(output, "y", 1)
    d_hidden, d_one, d_one_low_t, dctx_t, sums_one, sums_hidden = down(
        d_two_low, d_two, slope, unit_one, inv_one, heads_all, rest, vector_rows, part
    )
    in_grads = outer_in(low_t, d_hidden, d_one_low_t, ctx_t, rows)
    in_sum = lax.psum_scatter(in_grads, ("z", "x", "core"), scatter_dimension=0)
    output_got, in_grads = tie(output_got, in_grads)
    down_pair = outer(core, d_two_low_t, active, rows, after=(in_grads,))
    down_pending = start_core(*down_pair)
    sums_small = jnp.concatenate(
        [jnp.sum(sums_hidden, axis=(0, 1, 3)).reshape(-1)]
        + [s[i] for i in range(3) for s in (jnp.sum(sums_one, axis=(0, 2)), jnp.sum(sums_two, axis=(0, 2)))]
    )
    half_back = functools.partial(attention_back, q_t, k_t, v_t, probs, inverse, ctx_t, dctx_t)
    grads = half_back((), heads, 0, 1, after=down_pair)
    (down_sum,), grads = tie_sums([down_pending], grads)
    down_pending = start(down_sum, "y", 0)
    grads = half_back(tuple(grads), heads, 1, heads // 2 - 1, after=down_pending[2])
    dq_t, dk_t, dv_t, held = grads
    pair = project_back(core, stacked, dq_t, dk_t, dv_t, halves, rows)
    (down_sum,), pair = tie_sums([down_pending], pair)
    down_pending = start(down_sum, "x", 1)
    pending = start_core(*pair)
    table_grad = table_back(buckets_t, held, bucket_count, after=tuple(pair) + tuple(down_pending[2]))
    (qkv_sum, down_sum), table_grad = tie_sums([pending, down_pending], table_grad)
    pending, down_pending = start(qkv_sum, "y", 0), start(down_sum, "z", 0)
    half = me.astype(jnp.int32).reshape(1)
    grad_in = inputs_back(
        half, heads_all, d_one, dq_t, dk_t, dv_t, after=pending[2] + down_pending[2]
    )
    table_grad = jnp.sum(table_grad.reshape(bucket_count, heads, -1), axis=2).T
    small = jnp.concatenate(
        [jnp.sum(g.astype(F32), axis=1) for g in (dq_t, dv_t)] + [table_grad.reshape(-1), sums_small]
    )
    small = sum_pairs(small.reshape(-1, 128), ("core",))
    outs = (output, output_got)
    (qkv_sum,), grad_in, small, outs = tie_sums([pending], grad_in, small, outs)
    pending = start(qkv_sum, "x", 1)
    grad_kept, grad_sent = grad_in
    grad_got = shifted(grad_sent, "y", 1)

    small = sum_pairs(small, ("z",))
    (qkv_sum,), small = tie_sums([pending], small)
    pending = start(qkv_sum, "z", 0)
    down_share = total(down_pending[0] + down_pending[1])
    in_pending = start([in_sum], "y", 0)
    in_share = total(in_pending[0] + in_pending[1])
    small = sum_pairs(small, ("x", "y")).reshape(-1)
    first_kept = me == 0
    output, output_got = outs
    outs = jnp.stack(
        [jnp.where(first_kept, output, output_got), jnp.where(first_kept, output_got, output)]
    ).reshape(halves, 2, seq, width)
    grad_ins = jnp.stack(
        [jnp.where(first_kept, grad_kept, grad_got), jnp.where(first_kept, grad_got, grad_kept)]
    ).reshape(halves, 2, seq, width // halves)
    qkv_share = total(pending[0] + pending[1])
    ends = [2 * width, 2 * width + heads * bucket_count]
    ends.append(ends[1] + halves * ffn)
    grad_b_qv = mine(jnp.transpose(small[: ends[0]].reshape(2, halves, part), (1, 0, 2)))
    grad_table = mine(small[ends[0] : ends[1]].reshape(halves, heads_here, bucket_count)).T
    grad_b_in = mine(small[ends[1] : ends[2]].reshape(halves, ffn))
    pairs = small[ends[2] :].reshape(3, 2, width)
    return (
        outs[:, 0],
        outs[:, 1],
        grad_ins[:, 0],
        grad_ins[:, 1],
        jnp.transpose(qkv_share.reshape(rows, 3, part), (1, 0, 2)),
        grad_b_qv,
        in_share[:, ffn:].T,
        in_share[:, :ffn],
        grad_b_in,
        down_share.T,
        pairs[0],
        pairs[1],
        pairs[2],
        grad_table,
    )


def solution(mesh):
    count = mesh.shape["dp"] // 2
    depth = 4 if count % 4 == 0 else 1
    while count // depth > depth:
        depth *= 2
    grid = mesh.devices.reshape(depth, count // depth, 2, mesh.shape["tensor"])
    fine = Mesh(grid, ("z", "x", "core", "y"))
    dp = ("z", "x", "core")
    return jax.shard_map(
        shards,
        mesh=fine,
        in_specs=(
            P(dp, None, None),
            P(dp, None, None),
            P(dp),
            P(dp, None),
            P(dp, None, None),
            P(None, dp, "y"),
            P(None, "y"),
            P("y", dp),
            P(dp, "y"),
            P("y"),
            P("y", dp),
            P(),
            P(),
            P(),
            P(None, "y"),
            P(dp, None, None),
            P(dp, None, None),
        ),
        out_specs=(
            P(dp, None, None),
            P(dp, None, None),
            P(dp, None, "y"),
            P(dp, None, "y"),
            P(None, dp, "y"),
            P(None, "y"),
            P("y", dp),
            P(dp, "y"),
            P("y"),
            P("y", dp),
            P(),
            P(),
            P(),
            P(None, "y"),
        ),
        check_vma=False,
    )
```
